32 devices in a mesh: dp: 8 (over y, x, core), fsdp: 4 (over z).
Axes of the slice: x: 2, y: 2, z: 4, core: 2. Of those that a mesh axis runs over, the one named last changes fastest.
Arguments:
- tokens: bfloat16 [24576, 1024], P(('dp', 'fsdp')), may hold values from -6 to 6
- lengths: int32 [32, 4], P(('dp', 'fsdp')), may hold values from 0 to 768, as said below
- cotangent: bfloat16 [24576, 1024], P(('dp', 'fsdp')), may hold values from -6 to 6
- norm_gain: float32 [1024], P('fsdp'), may hold values from 0.5 to 1.5
- input_weight: float32 [1024, 4096], P('fsdp'), may hold values from -0.1875 to 0.1875
- select_weight: float32 [96, 2048], P(None, 'fsdp'), may hold values from -0.125 to 0.125
- step_weight: float32 [64, 2048], P(None, 'fsdp'), may hold values from -0.75 to 0.75
- channel_params: float32 [23, 2048], P(None, 'fsdp'), may hold values from -10 to 4, as said below
- output_weight: float32 [2048, 1024], P('fsdp'), may hold values from -0.25 to 0.25
- moment_gain: float32 [1024], P('fsdp'), may hold values from -0.00390625 to 0.00390625
- moment_input: float32 [1024, 4096], P('fsdp'), may hold values from -0.00390625 to 0.00390625
- moment_select: float32 [96, 2048], P(None, 'fsdp'), may hold values from -0.00390625 to 0.00390625
- moment_step: float32 [64, 2048], P(None, 'fsdp'), may hold values from -0.00390625 to 0.00390625
- moment_channel: float32 [23, 2048], P(None, 'fsdp'), may hold values from -0.00390625 to 0.00390625
- moment_output: float32 [2048, 1024], P('fsdp'), may hold values from -0.00390625 to 0.00390625
- square_gain: float32 [1024], P('fsdp'), may hold values from 1e-08 to 1e-06
- square_input: float32 [1024, 4096], P('fsdp'), may hold values from 1e-08 to 1e-06
- square_select: float32 [96, 2048], P(None, 'fsdp'), may hold values from 1e-08 to 1e-06
- square_step: float32 [64, 2048], P(None, 'fsdp'), may hold values from 1e-08 to 1e-06
- square_channel: float32 [23, 2048], P(None, 'fsdp'), may hold values from 1e-08 to 1e-06
- square_output: float32 [2048, 1024], P('fsdp'), may hold values from 1e-08 to 1e-06
Outputs:
- layer_output: bfloat16 [24576, 1024], P(('dp', 'fsdp'))
- input_grad: bfloat16 [24576, 1024], P(('dp', 'fsdp'))
- grad_norm: float32 [], replicated
- update_gain: float32 [1024], P('fsdp')
- update_input: float32 [1024, 4096], P('fsdp')
- update_select: float32 [96, 2048], P(None, 'fsdp')
- update_step: float32 [64, 2048], P(None, 'fsdp')
- update_channel: float32 [23, 2048], P(None, 'fsdp')
- update_output: float32 [2048, 1024], P('fsdp')
- total_gain: float32 [1024], P('fsdp')
- total_input: float32 [1024, 4096], P('fsdp')
- total_select: float32 [96, 2048], P(None, 'fsdp')
- total_step: float32 [64, 2048], P(None, 'fsdp')
- total_channel: float32 [23, 2048], P(None, 'fsdp')
- total_output: float32 [2048, 1024], P('fsdp')
The draws below stay inside these ranges and needn't reach their ends.
Inputs may be any that keep to these rules, and one draw needn't show every extreme that they name: Row k lists the cluster lengths of device k's 768 token slots in order; each row sums to between 384 and 768; in every draw some device holds one cluster of exactly 768 tokens, the rest of its row 0; a length may be 0. `channel_params`: rows 0 to 15 are logarithms of positive decay rates, the step-size bias row is the inverse softplus of a positive step size, the skip row is positive.
All inputs are finite; a program needn't handle non-finite values.
Results may differ from the reference program's by a relative error of at most 0.0065.
The reference program's roundings to bfloat16 on the way (of `normed`, `mixed` and `gated`) count: a program that leaves them out, or rounds other values in their place, can miss the bound.
Values may be sent and summed in bfloat16 or wider, within the bound.
A program may use at most 320 MiB of HBM per device.

```python
import math
import jax
import jax.numpy as jnp
from jax import lax

D = 1024
DI = 2048
N = 16
R = 64
CONV = 4
TOK_DEV = 768
SPAN = 64
CLUS = 4
TOKENS = 24576


def draw_lengths(key, part):
    lanes = TOKENS // TOK_DEV
    key_total, key_full, key_rest, key_cuts = jax.random.split(key, 4)
    totals = jax.random.randint(key_total, (lanes,), TOK_DEV // 2, TOK_DEV + 1).astype(jnp.int32)
    full_lane = jax.random.randint(key_full, (), 0, lanes)
    rest = (jax.random.randint(key_rest, (lanes,), 0, 65536) % (totals // 8 + 1)).astype(jnp.int32)
    raw_cuts = jax.random.randint(key_cuts, (lanes, CLUS - 2), 0, TOK_DEV + 1)
    cuts = jnp.sort(raw_cuts * rest[:, None] // TOK_DEV, axis=1).astype(jnp.int32)
    zeros = jnp.zeros((lanes, 1), jnp.int32)
    edges = jnp.concatenate([zeros, cuts, rest[:, None]], axis=1)
    pieces = (edges[:, 1:] - edges[:, :-1]).astype(jnp.int32)
    rows = jnp.concatenate([(totals - rest)[:, None], pieces], axis=1).astype(jnp.int32)
    whole_row = jnp.where(jnp.arange(CLUS) == 0, TOK_DEV, 0).astype(jnp.int32)
    is_full = (jnp.arange(lanes) == full_lane)[:, None]
    return jnp.where(is_full, whole_row[None, :], rows).astype(jnp.int32)


def draw_channel_params(key, part):
    key_rate, key_kernel, key_shift, key_step, key_skip = jax.random.split(key, 5)
    levels = jnp.arange(1, N + 1, dtype=jnp.float32)[:, None]
    a_log = jnp.log(levels * jax.random.uniform(key_rate, (N, DI), jnp.float32, 0.5, 1.5))
    kernel = 0.5 * jnp.clip(jax.random.normal(key_kernel, (CONV, DI), jnp.float32), -4.0, 4.0)
    low_step, high_step, low_skip, high_skip, shift_mean = (0.0001, 0.01, 0.1, 0.3, 1.0)
    shift = shift_mean + 0.3 * jnp.clip(jax.random.normal(key_shift, (1, DI), jnp.float32), -4.0, 4.0)
    step_size = jnp.exp(jax.random.uniform(key_step, (1, DI), jnp.float32, jnp.log(low_step), jnp.log(high_step)))
    step_bias = step_size + jnp.log(-jnp.expm1(-step_size))
    skip = jax.random.uniform(key_skip, (1, DI), jnp.float32, low_skip, high_skip)
    return jnp.concatenate([a_log, kernel, shift, step_bias, skip], axis=0).astype(jnp.float32)


def block_scale(key, shape, cuts, least, high):
    def one(dim, blocks):
        heights = jax.random.uniform(jax.random.fold_in(jax.random.fold_in(key, 6), dim), (blocks,), jnp.float32, least / len(cuts), high / len(cuts))
        return jnp.repeat(jnp.exp(heights), shape[dim] // blocks).reshape((-1,) + (1,) * (len(shape) - dim - 1))

    level = one(*cuts[0])
    for cut in cuts[1:]:
        level = level * one(*cut)
    return level


def gaussian(rng, dims, spread, most, cuts=(), kind=jnp.bfloat16):
    drawn = jax.random.normal(rng, dims, jnp.float32) * spread
    if len(cuts) > 0:
        drawn = block_scale(rng, dims, cuts, -0.22, 0.18) * drawn
    return jnp.clip(drawn, min=-most, max=most).astype(kind)


def setup_inputs(seed: int = 0) -> dict:
    seeds = jax.random.split(jax.random.key(seed), 22)
    tokens = gaussian(seeds[0], (TOKENS, D), 1.0, 6.0, ((0, 32),))
    lengths = draw_lengths(jax.random.fold_in(seeds[21], 71), 0)
    cotangent = gaussian(seeds[2], (TOKENS, D), 1.0, 6.0, ((0, 32),))
    norm_gain = jnp.clip(1.0 + 0.1 * jax.random.normal(seeds[3], (D,), jnp.float32), 0.5, 1.5)
    input_weight = gaussian(seeds[4], (D, 2 * DI), D ** -0.5, 0.1875, ((0, 4),), jnp.float32)
    select_weight = gaussian(seeds[5], (R + 2 * N, DI), DI ** -0.5, 0.125, ((1, 4),), jnp.float32)
    step_weight = gaussian(seeds[6], (R, DI), R ** -0.5, 0.75, ((1, 4),), jnp.float32)
    channel_params = draw_channel_params(jax.random.fold_in(seeds[21], 71), 0)
    output_weight = gaussian(seeds[8], (DI, D), (DI // 4) ** -0.5, 0.25, ((0, 4),), jnp.float32)
    moment_gain = gaussian(seeds[9], (D,), 0.0003, 0.00390625, ((0, 4),), jnp.float32)
    moment_input = gaussian(seeds[10], (D, 2 * DI), 0.0003, 0.00390625, ((0, 4),), jnp.float32)
    moment_select = gaussian(seeds[11], (R + 2 * N, DI), 0.0003, 0.00390625, ((1, 4),), jnp.float32)
    moment_step = gaussian(seeds[12], (R, DI), 0.0003, 0.00390625, ((1, 4),), jnp.float32)
    moment_channel = gaussian(seeds[13], (N + CONV + 3, DI), 0.0003, 0.00390625, ((1, 4),), jnp.float32)
    moment_output = gaussian(seeds[14], (DI, D), 0.0003, 0.00390625, ((0, 4),), jnp.float32)
    square_gain = jnp.clip(jnp.exp(math.log(9.999999974752427e-07) - 4.6051702 * jax.random.uniform(seeds[15], (D,), jnp.float32) ** block_scale(seeds[15], (D,), ((0, 4),), -0.2, 0.2)), 9.99999993922529e-09, 9.999999974752427e-07)
    square_input = jnp.clip(jnp.exp(math.log(9.999999974752427e-07) - 4.6051702 * jax.random.uniform(seeds[16], (D, 2 * DI), jnp.float32) ** block_scale(seeds[16], (D, 2 * DI), ((0, 4),), -0.2, 0.2)), 9.99999993922529e-09, 9.999999974752427e-07)
    square_select = jnp.clip(jnp.exp(math.log(9.999999974752427e-07) - 4.6051702 * jax.random.uniform(seeds[17], (R + 2 * N, DI), jnp.float32) ** block_scale(seeds[17], (R + 2 * N, DI), ((1, 4),), -0.2, 0.2)), 9.99999993922529e-09, 9.999999974752427e-07)
    square_step = jnp.clip(jnp.exp(math.log(9.999999974752427e-07) - 4.6051702 * jax.random.uniform(seeds[18], (R, DI), jnp.float32) ** block_scale(seeds[18], (R, DI), ((1, 4),), -0.2, 0.2)), 9.99999993922529e-09, 9.999999974752427e-07)
    square_channel = jnp.clip(jnp.exp(math.log(9.999999974752427e-07) - 4.6051702 * jax.random.uniform(seeds[19], (N + CONV + 3, DI), jnp.float32) ** block_scale(seeds[19], (N + CONV + 3, DI), ((1, 4),), -0.2, 0.2)), 9.99999993922529e-09, 9.999999974752427e-07)
    square_output = jnp.clip(jnp.exp(math.log(9.999999974752427e-07) - 4.6051702 * jax.random.uniform(seeds[20], (DI, D), jnp.float32) ** block_scale(seeds[20], (DI, D), ((0, 4),), -0.2, 0.2)), 9.99999993922529e-09, 9.999999974752427e-07)
    return {"tokens": tokens, "lengths": lengths, "cotangent": cotangent, "norm_gain": norm_gain, "input_weight": input_weight, "select_weight": select_weight, "step_weight": step_weight, "channel_params": channel_params, "output_weight": output_weight, "moment_gain": moment_gain, "moment_input": moment_input, "moment_select": moment_select, "moment_step": moment_step, "moment_channel": moment_channel, "moment_output": moment_output, "square_gain": square_gain, "square_input": square_input, "square_select": square_select, "square_step": square_step, "square_channel": square_channel, "square_output": square_output}


@jax.custom_vjp
def low(v):
    return lax.optimization_barrier(v.astype(jnp.bfloat16)).astype(jnp.float32)

@jax.custom_vjp
def low_back(v):
    return v

def low_keep(v):
    return (low(v), None)

def low_pass(kept, grad):
    return (grad,)

def back_keep(v):
    return (v, None)

def back_low(kept, grad):
    return (low(grad),)
low.defvjp(low_keep, low_pass)
low_back.defvjp(back_keep, back_low)
highest = lax.Precision.HIGHEST
norm_eps = 1e-05
beta_one = 0.9
beta_two = 0.95
adam_eps = 1e-08
decay_rate = 0.1
adam_step = 10.0
clip_norm = 1.0

def block_layout(lengths_row, count):
    ends = jnp.cumsum(lengths_row, dtype=jnp.int32)
    starts = ends - lengths_row
    places = jnp.arange(count, dtype=jnp.int32)
    live_mask = (places < ends[-1]).astype(jnp.float32)
    begun = jnp.where(starts[None, :] <= places[:, None], starts[None, :], jnp.zeros_like(starts)[None, :])
    offset = places - lax.optimization_barrier(jnp.max(begun, axis=1))
    return (live_mask, offset.astype(jnp.int32))

def rms_scale(values, scales):
    return values * lax.rsqrt(lax.optimization_barrier(jnp.mean(values * values, axis=1, keepdims=True)) + norm_eps) * scales[None, :]

def causal_conv(values, kernel, shift, offset):
    total = shift[None, :] + kernel[CONV - 1][None, :] * values
    for distance in range(1, CONV):
        moved = jnp.pad(values, ((distance, 0), (0, 0)))[:-distance]
        keep = (offset >= distance).astype(jnp.float32)[:, None]
        total = total + kernel[CONV - 1 - distance][None, :] * moved * keep
    return total

def scan_token(rates):

    def advance(carried, token_row):
        step_size, values, bsel, csel, restart = token_row
        carried = jnp.exp(step_size[None, :] * rates) * (1.0 - restart) * carried + bsel[:, None] * (step_size * values)[None, :]
        return (carried, lax.optimization_barrier(jnp.sum(csel[:, None] * carried, axis=0)))
    return advance

def selective_scan(rates, step_size, values, bsel, csel, restart):
    length = step_size.shape[0]
    blocks = length // SPAN

    def shaped(array):
        return array.reshape((blocks, SPAN) + array.shape[1:])

    @jax.checkpoint
    def one_block(carried, slices):
        return lax.scan(scan_token(rates), carried, slices)
    start = jnp.zeros(rates.shape, jnp.float32)
    _, scanned = lax.scan(one_block, start, (shaped(step_size), shaped(values), shaped(bsel), shaped(csel), shaped(restart)))
    return scanned.reshape(length, rates.shape[1])

def mixer_core(values, bsel, csel, step_pre, gate_half, channel, restart):
    step_size = jax.nn.softplus(step_pre + channel[N + CONV + 1][None, :])
    rates = -jnp.exp(channel[:N])
    scanned = selective_scan(rates, step_size, values, bsel, csel, restart)
    scanned = scanned + channel[N + CONV + 2][None, :] * values
    return scanned * jax.nn.silu(gate_half)

def layer_block(inputs, gain, full_input, full_select, full_step, full_output, channel, live_mask, offset):
    restart = (offset == 0).astype(jnp.float32)
    normed = low(rms_scale(inputs, gain))
    projected = low_back(jnp.dot(normed, full_input, precision=highest))
    conv_input = projected[:, :DI]
    gate_half = projected[:, DI:]
    mixed = low(jax.nn.silu(causal_conv(conv_input, channel[N:N + CONV], channel[N + CONV], offset)))
    selection = low_back(jnp.dot(mixed, full_select.T, precision=highest))
    step_low = low(selection[:, :R])
    step_pre = low_back(jnp.dot(step_low, full_step, precision=highest))
    gated = low(mixer_core(mixed, selection[:, R:R + N], selection[:, R + N:], step_pre, gate_half, channel, restart))
    branch = low_back(jnp.dot(gated, full_output, precision=highest))
    return inputs + live_mask[:, None] * branch

def channel_decay(rows_total):
    places = jnp.arange(rows_total, dtype=jnp.int32)[:, None]
    return ((places >= N) & (places < N + CONV)).astype(jnp.float32)

def adam_direction(weight, grad, first, second, factor, decay):
    clipped = grad * factor
    first = beta_one * first + (1.0 - beta_one) * clipped
    second = beta_two * second + (1.0 - beta_two) * clipped * clipped
    first_hat = first / (1.0 - beta_one ** adam_step)
    second_hat = second / (1.0 - beta_two ** adam_step)
    return first_hat / (jnp.sqrt(second_hat) + adam_eps) + decay_rate * decay * weight

def reference(tokens, lengths, cotangent, norm_gain, input_weight, select_weight, step_weight, channel_params, output_weight, moment_gain, moment_input, moment_select, moment_step, moment_channel, moment_output, square_gain, square_input, square_select, square_step, square_channel, square_output):
    blocks = tokens.shape[0] // TOK_DEV
    live_mask, offset = jax.vmap(lambda lane: block_layout(lane, TOK_DEV))(lengths)
    inputs = tokens.astype(jnp.float32).reshape(blocks, TOK_DEV, D)
    params = (norm_gain, input_weight, select_weight, step_weight, channel_params, output_weight)

    def forward(values, weights):
        gain, full_input, full_select, full_step, channel, full_output = weights
        low_input = low(full_input)
        low_select = low(full_select)
        low_step = low(full_step)
        low_output = low(full_output)

        def one_lane(slices):
            lane_inputs, lane_live, lane_offset = slices
            return layer_block(lane_inputs, gain, low_input, low_select, low_step, low_output, channel, lane_live, lane_offset)
        return lax.map(jax.checkpoint(one_lane), (values, live_mask, offset))
    result, pullback = jax.vjp(forward, inputs, params)
    grad_inputs, grads = pullback(cotangent.astype(jnp.float32).reshape(blocks, TOK_DEV, D))
    layer_output = result.reshape(TOKENS, D).astype(jnp.bfloat16)
    input_grad = grad_inputs.reshape(TOKENS, D).astype(jnp.bfloat16)
    grad_norm = jnp.sqrt(sum([jnp.sum(grad * grad) for grad in grads]))
    factor = jnp.minimum(1.0, clip_norm / (grad_norm + 1e-06))
    decays = (0.0, 1.0, 1.0, 1.0, channel_decay(N + CONV + 3), 1.0)
    firsts = (moment_gain, moment_input, moment_select, moment_step, moment_channel, moment_output)
    seconds = (square_gain, square_input, square_select, square_step, square_channel, square_output)
    updates = [adam_direction(params[which], grads[which], firsts[which], seconds[which], factor, decays[which]) for which in range(6)]
    return (layer_output, input_grad, grad_norm, updates[0], updates[1], updates[2], updates[3], updates[4], updates[5], grads[0], grads[1], grads[2], grads[3], grads[4], grads[5])
```

```python
import functools
import math

import jax
import jax.numpy as jnp
from jax import lax
from jax.experimental import pallas as pl
from jax.experimental.pallas import tpu as pltpu
from jax.sharding import PartitionSpec as P

DI = 2048
N = 16
R = 64
CONV = 4
LANES = 128
COLS = DI // LANES
HALVES = COLS // 8
BLOCK = 64
GROUP = 8

norm_eps = 1e-05
beta_one = 0.9
beta_two = 0.95
adam_eps = 1e-08
decay_rate = 0.1
adam_step = 10.0
clip_norm = 1.0
RESET = 1e30


def block_layout(lengths_row, count):
    places = jnp.arange(count, dtype=jnp.int32)
    begun = jnp.zeros((count,), jnp.int32)
    end = jnp.zeros((), jnp.int32)
    for cluster in range(lengths_row.shape[0]):
        begun = jnp.where(end <= places, jnp.maximum(begun, end), begun)
        end = end + lengths_row[cluster]
    live_mask = (places < end).astype(jnp.float32)
    return live_mask, places - begun

def rms_scale(values, scales):
    return (
        values
        * lax.rsqrt(jnp.mean(values * values, axis=1, keepdims=True) + norm_eps)
        * scales[None, :]
    )


def causal_conv(values, kernel, shift, offset):
    total = shift[None, :] + kernel[CONV - 1][None, :] * values
    for distance in range(1, CONV):
        moved = jnp.pad(values, ((distance, 0), (0, 0)))[:-distance]
        keep = (offset >= distance).astype(jnp.float32)[:, None]
        total = total + kernel[CONV - 1 - distance][None, :] * moved * keep
    return total


def spread(ref, value, first):
    for col in range(COLS):
        ref[pl.ds(first + 8 * col, 8), :] = value[:, LANES * col : LANES * (col + 1)]


def token_rows(ref, first, half, token):
    return ref[pl.ds(first + 64 * half + token, 8, stride=8), :]


def splat(ref, row):
    return ref[pl.ds(row, 8, stride=0), :]


def prepare(rows, sel, dt_ref, mixed_ref, dts, us, bb):
    first = rows * 16
    step = dt_ref[pl.ds(rows, 8), :]
    chosen = sel[pl.ds(rows, 8), :]
    fresh = chosen[:, 2 * N : 2 * N + 1] > 0.5
    spread(dts, jnp.where(fresh, RESET, step), first)
    spread(us, step * mixed_ref[pl.ds(rows, 8), :], first)
    for k in range(2 * N):
        bb[pl.ds(rows * 2 * N + 8 * k, 8), :] = jnp.broadcast_to(chosen[:, k : k + 1], (8, LANES))


def forward_kernel(dt_ref, mixed_ref, sel, rates, y_ref, hs_ref, state, dts, us, bb, ys):
    @pl.when(pl.program_id(0) == 0)
    def _():
        state[...] = jnp.zeros_like(state)

    def stage(g, _):
        prepare(pl.multiple_of(g * 8, 8), sel, dt_ref, mixed_ref, dts, us, bb)
        return 0

    lax.fori_loop(0, BLOCK // 8, stage, 0)
    for low in range(0, N, GROUP):
        names = [(n, half) for n in range(low, low + GROUP) for half in range(HALVES)]

        def steps(g, carried):
            rows = pl.multiple_of(g * 8, 8)
            first = rows * 16
            kept = dict(zip(names, carried))
            for token in range(8):
                dt = [token_rows(dts, first, half, token) for half in range(HALVES)]
                u = [token_rows(us, first, half, token) for half in range(HALVES)]
                total = [None] * HALVES
                for n in range(low, low + GROUP):
                    b = splat(bb, rows * 2 * N + 8 * n + token)
                    c = splat(bb, rows * 2 * N + 8 * (N + n) + token)
                    for half in range(HALVES):
                        h = jnp.exp2(dt[half] * rates[2 * n + half]) * kept[n, half] + b * u[half]
                        kept[n, half] = h
                        hs_ref[rows + token, 2 * n + half] = h
                        part = c * h
                        total[half] = part if total[half] is None else total[half] + part
                for half in range(HALVES):
                    at = pl.ds(first + 64 * half + token, 8, stride=8)
                    ys[at, :] = total[half] if low == 0 else ys[at, :] + total[half]
            return tuple(kept[name] for name in names)

        start = tuple(state[2 * n + half] for n, half in names)
        for name, value in zip(names, lax.fori_loop(0, BLOCK // 8, steps, start)):
            state[2 * name[0] + name[1]] = value

    def finish(g, _):
        rows = pl.multiple_of(g * 8, 8)
        for col in range(COLS):
            y_ref[pl.ds(rows, 8), LANES * col : LANES * (col + 1)] = ys[pl.ds(rows * 16 + 8 * col, 8), :]
        return 0

    lax.fori_loop(0, BLOCK // 8, finish, 0)


def backward_kernel(
    dt_ref, mixed_ref, gs_ref, sel, rates, hs_ref, last_ref,
    sum_in, sum_decay, parts, grad_rates,
    carry, dts, us, gss, bb, s1, s2, prods,
):
    @pl.when(pl.program_id(0) == 0)
    def _():
        carry[...] = jnp.zeros_like(carry)
        grad_rates[...] = jnp.zeros_like(grad_rates)

    def stage(g, _):
        rows = pl.multiple_of(g * 8, 8)
        prepare(rows, sel, dt_ref, mixed_ref, dts, us, bb)
        spread(gss, gs_ref[pl.ds(rows, 8), :], rows * 16)
        return 0

    lax.fori_loop(0, BLOCK // 8, stage, 0)
    for low in range(0, N, GROUP):
        names = [(n, half) for n in range(low, low + GROUP) for half in range(HALVES)]

        def steps(step, carried):
            g = BLOCK // 8 - 1 - step
            rows = pl.multiple_of(g * 8, 8)
            first = rows * 16
            kept = dict(zip(names, carried[: len(names)]))
            total = dict(zip(names, carried[len(names) :]))
            for token in reversed(range(8)):
                dt = [token_rows(dts, first, half, token) for half in range(HALVES)]
                u = [token_rows(us, first, half, token) for half in range(HALVES)]
                gs = [token_rows(gss, first, half, token) for half in range(HALVES)]
                in_sum = [None] * HALVES
                decay_sum = [None] * HALVES
                for n in range(low, low + GROUP):
                    b = splat(bb, rows * 2 * N + 8 * n + token)
                    c = splat(bb, rows * 2 * N + 8 * (N + n) + token)
                    for_b = for_c = None
                    for half in range(HALVES):
                        at = 2 * n + half
                        if token > 0:
                            before = hs_ref[rows + token - 1, at]
                        else:
                            before = jnp.where(g == 0, last_ref[0, at], hs_ref[jnp.maximum(rows - 1, 0), at])
                        rate = rates[at]
                        adjoint = c * gs[half] + kept[n, half]
                        part_c = gs[half] * hs_ref[rows + token, at]
                        part_b = adjoint * u[half]
                        for_c = part_c if for_c is None else for_c + part_c
                        for_b = part_b if for_b is None else for_b + part_b
                        part = b * adjoint
                        in_sum[half] = part if in_sum[half] is None else in_sum[half] + part
                        later = jnp.exp2(dt[half] * rate) * adjoint
                        kept[n, half] = later
                        slope = later * before
                        part = rate * slope
                        decay_sum[half] = part if decay_sum[half] is None else decay_sum[half] + part
                        total[n, half] = total[n, half] + dt[half] * slope
                    prods[pl.ds(8 * (n - low), 8), :] = for_b
                    prods[pl.ds(8 * (GROUP + n - low), 8), :] = for_c
                for half in range(HALVES):
                    at = pl.ds(first + 64 * half + token, 8, stride=8)
                    s1[at, :] = in_sum[half] if low == 0 else s1[at, :] + in_sum[half]
                    s2[at, :] = decay_sum[half] if low == 0 else s2[at, :] + decay_sum[half]
                for kind in range(2):
                    rows_of = [prods[pl.ds(8 * GROUP * kind + s, GROUP, stride=8), :] for s in range(8)]
                    while len(rows_of) > 1:
                        rows_of = [a + b for a, b in zip(rows_of[::2], rows_of[1::2])]
                    parts[rows + token, pl.ds(N * kind + low, GROUP), :] = rows_of[0]
            return tuple(kept[name] for name in names) + tuple(total[name] for name in names)

        start = tuple(carry[2 * n + half] for n, half in names)
        start = start + tuple(grad_rates[2 * n + half] for n, half in names)
        ended = lax.fori_loop(0, BLOCK // 8, steps, start)
        for name, value, sums in zip(names, ended[: len(names)], ended[len(names) :]):
            carry[2 * name[0] + name[1]] = value
            grad_rates[2 * name[0] + name[1]] = sums

    def finish(g, _):
        rows = pl.multiple_of(g * 8, 8)
        for col in range(COLS):
            lanes = slice(LANES * col, LANES * (col + 1))
            sum_in[pl.ds(rows, 8), lanes] = s1[pl.ds(rows * 16 + 8 * col, 8), :]
            sum_decay[pl.ds(rows, 8), lanes] = s2[pl.ds(rows * 16 + 8 * col, 8), :]
        return 0

    lax.fori_loop(0, BLOCK // 8, finish, 0)


def scan_forward(dt, mixed, sel, rates):
    count = dt.shape[0]
    rows = pl.BlockSpec((BLOCK, DI), lambda i: (i, 0))
    return pl.pallas_call(
        forward_kernel,
        grid=(count // BLOCK,),
        in_specs=[
            rows,
            rows,
            pl.BlockSpec((BLOCK, LANES), lambda i: (i, 0)),
            pl.BlockSpec((2 * N, 8, LANES), lambda i: (0, 0, 0)),
        ],
        out_specs=[rows, pl.BlockSpec((BLOCK, 2 * N, 8, LANES), lambda i: (i, 0, 0, 0))],
        out_shape=[
            jax.ShapeDtypeStruct((count, DI), jnp.float32),
            jax.ShapeDtypeStruct((count, 2 * N, 8, LANES), jnp.float32),
        ],
        scratch_shapes=[
            pltpu.VMEM((2 * N, 8, LANES), jnp.float32),
            pltpu.VMEM((BLOCK * COLS, LANES), jnp.float32),
            pltpu.VMEM((BLOCK * COLS, LANES), jnp.float32),
            pltpu.VMEM((BLOCK * 2 * N, LANES), jnp.float32),
            pltpu.VMEM((BLOCK * COLS, LANES), jnp.float32),
        ],
        compiler_params=pltpu.CompilerParams(vmem_limit_bytes=48 << 20),
        cost_estimate=pl.CostEstimate(
            flops=6 * count * N * DI, bytes_accessed=4 * count * N * DI, transcendentals=count * N * DI
        ),
        name="scan_forward",
    )(dt, mixed, sel, rates)


def scan_backward(dt, mixed, gs, sel, rates, states):
    count = dt.shape[0]
    blocks = count // BLOCK
    rows = pl.BlockSpec((BLOCK, DI), lambda i: (blocks - 1 - i, 0))
    return pl.pallas_call(
        backward_kernel,
        grid=(blocks,),
        in_specs=[
            rows,
            rows,
            rows,
            pl.BlockSpec((BLOCK, LANES), lambda i: (blocks - 1 - i, 0)),
            pl.BlockSpec((2 * N, 8, LANES), lambda i: (0, 0, 0)),
            pl.BlockSpec((BLOCK, 2 * N, 8, LANES), lambda i: (blocks - 1 - i, 0, 0, 0)),
            pl.BlockSpec(
                (1, 2 * N, 8, LANES),
                lambda i: (jnp.maximum((blocks - 1 - i) * BLOCK - 1, 0), 0, 0, 0),
            ),
        ],
        out_specs=[
            rows,
            rows,
            pl.BlockSpec((BLOCK, 2 * N, LANES), lambda i: (blocks - 1 - i, 0, 0)),
            pl.BlockSpec((2 * N, 8, LANES), lambda i: (0, 0, 0)),
        ],
        out_shape=[
            jax.ShapeDtypeStruct((count, DI), jnp.float32),
            jax.ShapeDtypeStruct((count, DI), jnp.float32),
            jax.ShapeDtypeStruct((count, 2 * N, LANES), jnp.float32),
            jax.ShapeDtypeStruct((2 * N, 8, LANES), jnp.float32),
        ],
        scratch_shapes=[pltpu.VMEM((2 * N, 8, LANES), jnp.float32)]
        + [pltpu.VMEM((BLOCK * COLS, LANES), jnp.float32)] * 3
        + [pltpu.VMEM((BLOCK * 2 * N, LANES), jnp.float32)]
        + [pltpu.VMEM((BLOCK * COLS, LANES), jnp.float32)] * 2
        + [pltpu.VMEM((16 * GROUP, LANES), jnp.float32)],
        compiler_params=pltpu.CompilerParams(vmem_limit_bytes=48 << 20),
        cost_estimate=pl.CostEstimate(
            flops=15 * count * N * DI, bytes_accessed=4 * count * N * DI, transcendentals=count * N * DI
        ),
        name="scan_backward",
    )(dt, mixed, gs, sel, rates, states, states)


def contract(left, right, left_dim, right_dim):
    return lax.dot_general(
        left, right, (((left_dim,), (right_dim,)), ((), ())), preferred_element_type=jnp.float32
    )


def channel_decay(rows_total):
    places = jnp.arange(rows_total, dtype=jnp.int32)[:, None]
    return ((places >= N) & (places < N + CONV)).astype(jnp.float32)


def adam_direction(weight, grad, first, second, factor, decay):
    clipped = grad * factor
    first = beta_one * first + (1.0 - beta_one) * clipped
    second = beta_two * second + (1.0 - beta_two) * clipped * clipped
    first_hat = first / (1.0 - beta_one**adam_step)
    second_hat = second / (1.0 - beta_two**adam_step)
    return first_hat / (jnp.sqrt(second_hat) + adam_eps) + decay_rate * decay * weight


def local(
    tokens,
    lengths,
    cotangent,
    norm_gain,
    input_weight,
    select_weight,
    step_weight,
    channel_params,
    output_weight,
    moment_gain,
    moment_input,
    moment_select,
    moment_step,
    moment_channel,
    moment_output,
    square_gain,
    square_input,
    square_select,
    square_step,
    square_channel,
    square_output,
):
    row_count = tokens.shape[0]
    live_mask, offset = block_layout(lengths[0], row_count)
    restart = (offset == 0).astype(jnp.float32)
    full_input, full_select, full_step, full_output = (
        lax.all_gather(input_weight.astype(jnp.bfloat16), "fsdp", axis=0, tiled=True),
        lax.all_gather(select_weight.astype(jnp.bfloat16), "fsdp", axis=1, tiled=True),
        lax.all_gather(step_weight.astype(jnp.bfloat16), "fsdp", axis=1, tiled=True),
        lax.all_gather(output_weight.astype(jnp.bfloat16), "fsdp", axis=0, tiled=True),
    )
    gain, channel = (
        lax.all_gather(norm_gain, "fsdp", axis=0, tiled=True),
        lax.all_gather(channel_params, "fsdp", axis=1, tiled=True),
    )
    inputs = tokens.astype(jnp.float32)
    normed_value, norm_pull = jax.vjp(rms_scale, inputs, gain)
    normed = normed_value.astype(jnp.bfloat16)
    projected = jnp.dot(normed, full_input, preferred_element_type=jnp.float32)
    conv_input = projected[:, :DI]
    gate_half = projected[:, DI:]

    def conv_piece(values, kernel, shift):
        return jax.nn.silu(causal_conv(values, kernel, shift, offset))

    conv_value, conv_pull = jax.vjp(
        conv_piece, conv_input, channel[N : N + CONV], channel[N + CONV]
    )
    mixed = conv_value.astype(jnp.bfloat16)
    mixed_values = mixed.astype(jnp.float32)
    selection = contract(mixed, full_select, 1, 1)
    step_low = selection[:, :R].astype(jnp.bfloat16)
    step_pre = jnp.dot(step_low, full_step, preferred_element_type=jnp.float32)
    step_in = step_pre + channel[N + CONV + 1][None, :]
    step_size = jax.nn.softplus(step_in)
    rates = -jnp.exp(channel[:N])
    rates_low = (rates * math.log2(math.e)).reshape(2 * N, 8, LANES)
    chosen = jnp.concatenate(
        [selection[:, R:], restart[:, None], jnp.zeros((row_count, LANES - 2 * N - 1), jnp.float32)], axis=1
    )
    skip = channel[N + CONV + 2][None, :]
    state_out, states = scan_forward(step_size, mixed_values, chosen, rates_low)
    scanned = state_out + skip * mixed_values
    gate_value, gate_pull = jax.vjp(jax.nn.silu, gate_half)
    gated = (scanned * gate_value).astype(jnp.bfloat16)
    branch = jnp.dot(gated, full_output, preferred_element_type=jnp.float32)
    layer_output = (inputs + live_mask[:, None] * branch).astype(jnp.bfloat16)
    upstream = cotangent.astype(jnp.float32)
    grad_branch = (upstream * live_mask[:, None]).astype(jnp.bfloat16)
    grad_output = contract(gated, grad_branch, 0, 0)
    grad_gated = contract(grad_branch, full_output, 1, 1)
    grad_scanned = grad_gated * gate_value
    (grad_gate,) = gate_pull(grad_gated * scanned)
    sum_in, sum_decay, parts, sums = scan_backward(
        step_size, mixed_values, grad_scanned, chosen, rates_low, states
    )
    grad_both = jnp.sum(parts, axis=2)
    grad_mixed = step_size * sum_in + skip * grad_scanned
    grad_pre = (mixed_values * sum_in + math.log(2.0) * sum_decay) * jax.nn.sigmoid(step_in)
    grad_pre_low = grad_pre.astype(jnp.bfloat16)
    grad_step = contract(step_low, grad_pre_low, 0, 0)
    grad_step_low = contract(grad_pre_low, full_step, 1, 1)
    grad_selection = jnp.concatenate([grad_step_low, grad_both], axis=1).astype(jnp.bfloat16)
    grad_select = contract(grad_selection, mixed, 0, 0)
    grad_mixed = grad_mixed + jnp.dot(
        grad_selection, full_select, preferred_element_type=jnp.float32
    )
    grad_conv_input, grad_kernel, grad_shift = conv_pull(grad_mixed)
    grad_projected = jnp.concatenate([grad_conv_input, grad_gate], axis=1).astype(jnp.bfloat16)
    grad_input = contract(normed, grad_projected, 0, 0)
    grad_normed = contract(grad_projected, full_input, 1, 1)
    grad_inputs, grad_gain = norm_pull(grad_normed)
    input_grad = (upstream + grad_inputs).astype(jnp.bfloat16)
    grad_channel = jnp.concatenate(
        [
            rates * sums.reshape(N, DI),
            grad_kernel,
            grad_shift[None, :],
            jnp.sum(grad_pre, axis=0, keepdims=True),
            jnp.sum(grad_scanned * mixed_values, axis=0, keepdims=True),
        ],
        axis=0,
    )
    owned_gain, owned_input, owned_select, owned_step, owned_channel, owned_output = (
        lax.psum_scatter(grad_gain, "fsdp", scatter_dimension=0, tiled=True),
        lax.psum_scatter(grad_input, "fsdp", scatter_dimension=0, tiled=True),
        lax.psum_scatter(grad_select, "fsdp", scatter_dimension=1, tiled=True),
        lax.psum_scatter(grad_step, "fsdp", scatter_dimension=1, tiled=True),
        lax.psum_scatter(grad_channel, "fsdp", scatter_dimension=1, tiled=True),
        lax.psum_scatter(grad_output, "fsdp", scatter_dimension=0, tiled=True),
    )
    sum_gain, sum_input, sum_select, sum_step, sum_channel, sum_output = lax.psum(
        (owned_gain, owned_input, owned_select, owned_step, owned_channel, owned_output), "dp"
    )
    grads = (sum_gain, sum_input, sum_select, sum_step, sum_channel, sum_output)
    local_square = sum([jnp.sum(grad * grad) for grad in grads])
    total_square = lax.psum(local_square, "fsdp")
    grad_norm = jnp.sqrt(total_square)
    factor = jnp.minimum(1.0, clip_norm / (grad_norm + 1e-06))
    params = (norm_gain, input_weight, select_weight, step_weight, channel_params, output_weight)
    firsts = (moment_gain, moment_input, moment_select, moment_step, moment_channel, moment_output)
    seconds = (square_gain, square_input, square_select, square_step, square_channel, square_output)
    decays = (0.0, 1.0, 1.0, 1.0, channel_decay(channel_params.shape[0]), 1.0)
    updates = [
        adam_direction(
            params[which], grads[which], firsts[which], seconds[which], factor, decays[which]
        )
        for which in range(6)
    ]
    return (
        layer_output,
        input_grad,
        grad_norm,
        updates[0],
        updates[1],
        updates[2],
        updates[3],
        updates[4],
        updates[5],
        grads[0],
        grads[1],
        grads[2],
        grads[3],
        grads[4],
        grads[5],
    )


def solution(mesh):
    in_specs = (
        P(("dp", "fsdp"), None),
        P(("dp", "fsdp"), None),
        P(("dp", "fsdp"), None),
        P("fsdp"),
        P("fsdp", None),
        P(None, "fsdp"),
        P(None, "fsdp"),
        P(None, "fsdp"),
        P("fsdp", None),
        P("fsdp"),
        P("fsdp", None),
        P(None, "fsdp"),
        P(None, "fsdp"),
        P(None, "fsdp"),
        P("fsdp", None),
        P("fsdp"),
        P("fsdp", None),
        P(None, "fsdp"),
        P(None, "fsdp"),
        P(None, "fsdp"),
        P("fsdp", None),
    )
    out_specs = (
        P(("dp", "fsdp"), None),
        P(("dp", "fsdp"), None),
        P(),
        P("fsdp"),
        P("fsdp", None),
        P(None, "fsdp"),
        P(None, "fsdp"),
        P(None, "fsdp"),
        P("fsdp", None),
        P("fsdp"),
        P("fsdp", None),
        P(None, "fsdp"),
        P(None, "fsdp"),
        P(None, "fsdp"),
        P("fsdp", None),
    )
    return jax.shard_map(local, mesh=mesh, in_specs=in_specs, out_specs=out_specs, check_vma=False)
```

```python
import functools
import math

import jax
import jax.numpy as jnp
from jax import lax
from jax.experimental import pallas as pl
from jax.experimental.pallas import tpu as pltpu
from jax.sharding import PartitionSpec as P

DI = 2048
N = 16
R = 64
CONV = 4
LANES = 128
COLS = DI // LANES
HALVES = COLS // 8
BLOCK = 64
GROUP = 8

norm_eps = 1e-05
beta_one = 0.9
beta_two = 0.95
adam_eps = 1e-08
decay_rate = 0.1
adam_step = 10.0
clip_norm = 1.0
RESET = 1e30


def block_layout(lengths_row, count):
    places = jnp.arange(count, dtype=jnp.int32)
    begun = jnp.zeros((count,), jnp.int32)
    end = jnp.zeros((), jnp.int32)
    for cluster in range(lengths_row.shape[0]):
        begun = jnp.where(end <= places, jnp.maximum(begun, end), begun)
        end = end + lengths_row[cluster]
    live_mask = (places < end).astype(jnp.float32)
    return live_mask, places - begun

def rms_scale(values, scales):
    return (
        values
        * lax.rsqrt(jnp.mean(values * values, axis=1, keepdims=True) + norm_eps)
        * scales[None, :]
    )


def causal_conv(values, kernel, shift, offset):
    total = shift[None, :] + kernel[CONV - 1][None, :] * values
    for distance in range(1, CONV):
        moved = jnp.pad(values, ((distance, 0), (0, 0)))[:-distance]
        keep = (offset >= distance).astype(jnp.float32)[:, None]
        total = total + kernel[CONV - 1 - distance][None, :] * moved * keep
    return total


def spread(ref, value, first):
    for col in range(COLS):
        ref[pl.ds(first + 8 * col, 8), :] = value[:, LANES * col : LANES * (col + 1)]


def token_rows(ref, first, half, token):
    return ref[pl.ds(first + 64 * half + token, 8, stride=8), :]


def splat(ref, row):
    return ref[pl.ds(row, 8, stride=0), :]


def prepare(rows, sel, dt_ref, mixed_ref, dts, us, bb):
    first = rows * 16
    step = dt_ref[pl.ds(rows, 8), :]
    chosen = sel[pl.ds(rows, 8), :]
    fresh = chosen[:, 2 * N : 2 * N + 1] > 0.5
    spread(dts, jnp.where(fresh, RESET, step), first)
    spread(us, step * mixed_ref[pl.ds(rows, 8), :], first)
    for k in range(2 * N):
        bb[pl.ds(rows * 2 * N + 8 * k, 8), :] = jnp.broadcast_to(chosen[:, k : k + 1], (8, LANES))


def forward_kernel(dt_ref, mixed_ref, sel, rates, y_ref, hs_ref, state, dts, us, bb, ys):
    @pl.when(pl.program_id(0) == 0)
    def _():
        state[...] = jnp.zeros_like(state)

    def stage(g, _):
        prepare(pl.multiple_of(g * 8, 8), sel, dt_ref, mixed_ref, dts, us, bb)
        return 0

    lax.fori_loop(0, BLOCK // 8, stage, 0)
    for low in range(0, N, GROUP):
        names = [(n, half) for n in range(low, low + GROUP) for half in range(HALVES)]

        def steps(g, carried):
            rows = pl.multiple_of(g * 8, 8)
            first = rows * 16
            kept = dict(zip(names, carried))
            for token in range(8):
                dt = [token_rows(dts, first, half, token) for half in range(HALVES)]
                u = [token_rows(us, first, half, token) for half in range(HALVES)]
                total = [None] * HALVES
                for n in range(low, low + GROUP):
                    b = splat(bb, rows * 2 * N + 8 * n + token)
                    c = splat(bb, rows * 2 * N + 8 * (N + n) + token)
                    for half in range(HALVES):
                        h = jnp.exp2(dt[half] * rates[2 * n + half]) * kept[n, half] + b * u[half]
                        kept[n, half] = h
                        hs_ref[rows + token, 2 * n + half] = h
                        part = c * h
                        total[half] = part if total[half] is None else total[half] + part
                for half in range(HALVES):
                    at = pl.ds(first + 64 * half + token, 8, stride=8)
                    ys[at, :] = total[half] if low == 0 else ys[at, :] + total[half]
            return tuple(kept[name] for name in names)

        start = tuple(state[2 * n + half] for n, half in names)
        for name, value in zip(names, lax.fori_loop(0, BLOCK // 8, steps, start)):
            state[2 * name[0] + name[1]] = value

    def finish(g, _):
        rows = pl.multiple_of(g * 8, 8)
        for col in range(COLS):
            y_ref[pl.ds(rows, 8), LANES * col : LANES * (col + 1)] = ys[pl.ds(rows * 16 + 8 * col, 8), :]
        return 0

    lax.fori_loop(0, BLOCK // 8, finish, 0)


def backward_kernel(
    dt_ref, mixed_ref, gs_ref, sel, rates, hs_ref, last_ref,
    sum_in, sum_decay, parts, grad_rates,
    carry, dts, us, gss, bb, s1, s2, prods,
):
    @pl.when(pl.program_id(0) == 0)
    def _():
        carry[...] = jnp.zeros_like(carry)
        grad_rates[...] = jnp.zeros_like(grad_rates)

    def stage(g, _):
        rows = pl.multiple_of(g * 8, 8)
        prepare(rows, sel, dt_ref, mixed_ref, dts, us, bb)
        spread(gss, gs_ref[pl.ds(rows, 8), :], rows * 16)
        return 0

    lax.fori_loop(0, BLOCK // 8, stage, 0)
    for low in range(0, N, GROUP):
        names = [(n, half) for n in range(low, low + GROUP) for half in range(HALVES)]

        def steps(step, carried):
            g = BLOCK // 8 - 1 - step
            rows = pl.multiple_of(g * 8, 8)
            first = rows * 16
            kept = dict(zip(names, carried[: len(names)]))
            total = dict(zip(names, carried[len(names) :]))
            for token in reversed(range(8)):
                dt = [token_rows(dts, first, half, token) for half in range(HALVES)]
                u = [token_rows(us, first, half, token) for half in range(HALVES)]
                gs = [token_rows(gss, first, half, token) for half in range(HALVES)]
                in_sum = [None] * HALVES
                decay_sum = [None] * HALVES
                for n in range(low, low + GROUP):
                    b = splat(bb, rows * 2 * N + 8 * n + token)
                    c = splat(bb, rows * 2 * N + 8 * (N + n) + token)
                    for_b = for_c = None
                    for half in range(HALVES):
                        at = 2 * n + half
                        if token > 0:
                            before = hs_ref[rows + token - 1, at]
                        else:
                            before = jnp.where(g == 0, last_ref[0, at], hs_ref[jnp.maximum(rows - 1, 0), at])
                        rate = rates[at]
                        adjoint = c * gs[half] + kept[n, half]
                        part_c = gs[half] * hs_ref[rows + token, at]
                        part_b = adjoint * u[half]
                        for_c = part_c if for_c is None else for_c + part_c
                        for_b = part_b if for_b is None else for_b + part_b
                        part = b * adjoint
                        in_sum[half] = part if in_sum[half] is None else in_sum[half] + part
                        later = jnp.exp2(dt[half] * rate) * adjoint
                        kept[n, half] = later
                        slope = later * before
                        part = rate * slope
                        decay_sum[half] = part if decay_sum[half] is None else decay_sum[half] + part
                        total[n, half] = total[n, half] + dt[half] * slope
                    prods[pl.ds(8 * (n - low), 8), :] = for_b
                    prods[pl.ds(8 * (GROUP + n - low), 8), :] = for_c
                for half in range(HALVES):
                    at = pl.ds(first + 64 * half + token, 8, stride=8)
                    s1[at, :] = in_sum[half] if low == 0 else s1[at, :] + in_sum[half]
                    s2[at, :] = decay_sum[half] if low == 0 else s2[at, :] + decay_sum[half]
                for kind in range(2):
                    rows_of = [prods[pl.ds(8 * GROUP * kind + s, GROUP, stride=8), :] for s in range(8)]
                    while len(rows_of) > 1:
                        rows_of = [a + b for a, b in zip(rows_of[::2], rows_of[1::2])]
                    parts[rows + token, pl.ds(N * kind + low, GROUP), :] = rows_of[0]
            return tuple(kept[name] for name in names) + tuple(total[name] for name in names)

        start = tuple(carry[2 * n + half] for n, half in names)
        start = start + tuple(grad_rates[2 * n + half] for n, half in names)
        ended = lax.fori_loop(0, BLOCK // 8, steps, start)
        for name, value, sums in zip(names, ended[: len(names)], ended[len(names) :]):
            carry[2 * name[0] + name[1]] = value
            grad_rates[2 * name[0] + name[1]] = sums

    def finish(g, _):
        rows = pl.multiple_of(g * 8, 8)
        for col in range(COLS):
            lanes = slice(LANES * col, LANES * (col + 1))
            sum_in[pl.ds(rows, 8), lanes] = s1[pl.ds(rows * 16 + 8 * col, 8), :]
            sum_decay[pl.ds(rows, 8), lanes] = s2[pl.ds(rows * 16 + 8 * col, 8), :]
        return 0

    lax.fori_loop(0, BLOCK // 8, finish, 0)


def scan_forward(dt, mixed, sel, rates):
    count = dt.shape[0]
    rows = pl.BlockSpec((BLOCK, DI), lambda i: (i, 0))
    return pl.pallas_call(
        forward_kernel,
        grid=(count // BLOCK,),
        in_specs=[
            rows,
            rows,
            pl.BlockSpec((BLOCK, LANES), lambda i: (i, 0)),
            pl.BlockSpec((2 * N, 8, LANES), lambda i: (0, 0, 0)),
        ],
        out_specs=[rows, pl.BlockSpec((BLOCK, 2 * N, 8, LANES), lambda i: (i, 0, 0, 0))],
        out_shape=[
            jax.ShapeDtypeStruct((count, DI), jnp.float32),
            jax.ShapeDtypeStruct((count, 2 * N, 8, LANES), jnp.float32),
        ],
        scratch_shapes=[
            pltpu.VMEM((2 * N, 8, LANES), jnp.float32),
            pltpu.VMEM((BLOCK * COLS, LANES), jnp.float32),
            pltpu.VMEM((BLOCK * COLS, LANES), jnp.float32),
            pltpu.VMEM((BLOCK * 2 * N, LANES), jnp.float32),
            pltpu.VMEM((BLOCK * COLS, LANES), jnp.float32),
        ],
        compiler_params=pltpu.CompilerParams(vmem_limit_bytes=48 << 20),
        cost_estimate=pl.CostEstimate(
            flops=6 * count * N * DI, bytes_accessed=4 * count * N * DI, transcendentals=count * N * DI
        ),
        name="scan_forward",
    )(dt, mixed, sel, rates)


def scan_backward(dt, mixed, gs, sel, rates, states):
    count = dt.shape[0]
    blocks = count // BLOCK
    rows = pl.BlockSpec((BLOCK, DI), lambda i: (blocks - 1 - i, 0))
    return pl.pallas_call(
        backward_kernel,
        grid=(blocks,),
        in_specs=[
            rows,
            rows,
            rows,
            pl.BlockSpec((BLOCK, LANES), lambda i: (blocks - 1 - i, 0)),
            pl.BlockSpec((2 * N, 8, LANES), lambda i: (0, 0, 0)),
            pl.BlockSpec((BLOCK, 2 * N, 8, LANES), lambda i: (blocks - 1 - i, 0, 0, 0)),
            pl.BlockSpec(
                (1, 2 * N, 8, LANES),
                lambda i: (jnp.maximum((blocks - 1 - i) * BLOCK - 1, 0), 0, 0, 0),
            ),
        ],
        out_specs=[
            rows,
            rows,
            pl.BlockSpec((BLOCK, 2 * N, LANES), lambda i: (blocks - 1 - i, 0, 0)),
            pl.BlockSpec((2 * N, 8, LANES), lambda i: (0, 0, 0)),
        ],
        out_shape=[
            jax.ShapeDtypeStruct((count, DI), jnp.float32),
            jax.ShapeDtypeStruct((count, DI), jnp.float32),
            jax.ShapeDtypeStruct((count, 2 * N, LANES), jnp.float32),
            jax.ShapeDtypeStruct((2 * N, 8, LANES), jnp.float32),
        ],
        scratch_shapes=[pltpu.VMEM((2 * N, 8, LANES), jnp.float32)]
        + [pltpu.VMEM((BLOCK * COLS, LANES), jnp.float32)] * 3
        + [pltpu.VMEM((BLOCK * 2 * N, LANES), jnp.float32)]
        + [pltpu.VMEM((BLOCK * COLS, LANES), jnp.float32)] * 2
        + [pltpu.VMEM((16 * GROUP, LANES), jnp.float32)],
        compiler_params=pltpu.CompilerParams(vmem_limit_bytes=48 << 20),
        cost_estimate=pl.CostEstimate(
            flops=15 * count * N * DI, bytes_accessed=4 * count * N * DI, transcendentals=count * N * DI
        ),
        name="scan_backward",
    )(dt, mixed, gs, sel, rates, states, states)


def mesh_copy(src, dst, sems, at, device):
    return pltpu.make_async_remote_copy(
        src_ref=src,
        dst_ref=dst,
        send_sem=sems.at[0, at],
        recv_sem=sems.at[1, at],
        device_id=device,
        device_id_type=pl.DeviceIdType.MESH,
    )


def placed(plan):
    group = lax.axis_index("dp")
    return lax.axis_index("fsdp"), group // 2, lax.rem(group, 2)


def peers_of(plan):
    shards, places = plan
    mine, place, side = placed(plan)
    along = [(place * 2 + side, lax.rem(mine + k, shards)) for k in range(1, shards)]
    plane = [((place ^ j) * 2 + side, mine) for j in range(1, places)]
    return along, plane, (place * 2 + 1 - side, mine)


def greet(plan):
    along, plane, pair = peers_of(plan)
    barrier = pltpu.get_barrier_semaphore()
    everyone = along + plane + [pair]
    for device in everyone:
        pl.semaphore_signal(barrier, inc=1, device_id=device, device_id_type=pl.DeviceIdType.MESH)
    pl.semaphore_wait(barrier, len(everyone))


def gather_kernel(plan, count, *refs):
    own, full = refs[:count], refs[count : 2 * count]
    near, far, wide, cross = refs[2 * count :]
    shards, places = plan
    mine, place, side = placed(plan)
    along, plane, pair = peers_of(plan)
    greet(plan)
    local, first, second, third = [], [], [], []
    for s in range(count):
        keep = pltpu.make_async_copy(own[s], full[s].at[mine, place, side], near.at[s])
        keep.start()
        local.append(keep)
        sends = [
            mesh_copy(own[s], full[s].at[mine, place, side], far, s * (shards - 1) + k, device)
            for k, device in enumerate(along)
        ]
        for copy in sends:
            copy.start()
        first.append(sends)
    for s in range(count):
        local[s].wait()
        for copy in first[s]:
            copy.wait_recv()
        sends = [
            mesh_copy(
                full[s].at[:, place, side], full[s].at[:, place, side], wide, s * (places - 1) + k, device
            )
            for k, device in enumerate(plane)
        ]
        for copy in sends:
            copy.start()
        second.append(sends)
    for s in range(count):
        for copy in second[s]:
            copy.wait_recv()
        copy = mesh_copy(full[s].at[:, :, side], full[s].at[:, :, side], cross, s, pair)
        copy.start()
        third.append(copy)
    for s in range(count):
        for copy in first[s] + second[s]:
            copy.wait_send()
        third[s].wait()


def gather_pieces(plan, pieces, name, collective_id):
    shards, places = plan
    count = len(pieces)
    return pl.pallas_call(
        functools.partial(gather_kernel, plan, count),
        in_specs=[pl.BlockSpec(memory_space=pl.ANY)] * count,
        out_specs=[pl.BlockSpec(memory_space=pl.ANY)] * count,
        out_shape=[jax.ShapeDtypeStruct((shards, places, 2) + piece.shape, piece.dtype) for piece in pieces],
        scratch_shapes=[
            pltpu.SemaphoreType.DMA((count,)),
            pltpu.SemaphoreType.DMA((2, count * (shards - 1))),
            pltpu.SemaphoreType.DMA((2, count * (places - 1))),
            pltpu.SemaphoreType.DMA((2, count)),
        ],
        compiler_params=pltpu.CompilerParams(collective_id=collective_id, has_side_effects=True),
        cost_estimate=pl.CostEstimate(flops=0, bytes_accessed=32 << 20, transcendentals=0),
        name=name,
    )(*pieces)


def wide_sum(values):
    total = values[0].astype(jnp.float32)
    for value in values[1:]:
        total = total + value.astype(jnp.float32)
    return total.astype(jnp.bfloat16)


def reduce_kernel(plan, count, *refs):
    parts, full = refs[:count], refs[count : 2 * count]
    held = refs[2 * count : 3 * count]
    from_pair = refs[3 * count : 4 * count]
    from_plane = refs[4 * count : 5 * count]
    from_along = refs[5 * count : 6 * count]
    near, cross, wide, far, back, over = refs[6 * count :]
    shards, places = plan
    mine, place, side = placed(plan)
    along, plane, pair = peers_of(plan)
    greet(plan)
    local, first, second, third, fourth, fifth = [], [], [], [], [], []
    for s in range(count):
        keep = pltpu.make_async_copy(parts[s].at[:, :, side], held[s], near.at[s])
        keep.start()
        local.append(keep)
        copy = mesh_copy(parts[s].at[:, :, 1 - side], from_pair[s], cross, s, pair)
        copy.start()
        first.append(copy)
    for s in range(count):
        local[s].wait()
        first[s].wait_recv()

        @pl.loop(0, shards * places)
        def _(i, s=s):
            a, b = i // places, lax.rem(i, places)
            held[s][a, b] = wide_sum([held[s][a, b], from_pair[s][a, b]])

        sends = [
            mesh_copy(held[s].at[:, place ^ (k + 1)], from_plane[s].at[k], wide, s * (places - 1) + k, device)
            for k, device in enumerate(plane)
        ]
        for copy in sends:
            copy.start()
        second.append(sends)
    for s in range(count):
        for copy in second[s]:
            copy.wait_recv()

        @pl.loop(0, shards)
        def _(i, s=s):
            held[s][i, place] = wide_sum([held[s][i, place]] + [from_plane[s][k, i] for k in range(places - 1)])

        sends = [
            mesh_copy(
                held[s].at[lax.rem(mine + k + 1, shards), place],
                from_along[s].at[k],
                far,
                s * (shards - 1) + k,
                device,
            )
            for k, device in enumerate(along)
        ]
        for copy in sends:
            copy.start()
        third.append(sends)
    for s in range(count):
        for copy in third[s]:
            copy.wait_recv()
        full[s][place, side] = wide_sum([held[s][mine, place]] + [from_along[s][k] for k in range(shards - 1)])
        sends = [
            mesh_copy(full[s].at[place, side], full[s].at[place, side], back, s * (places - 1) + k, device)
            for k, device in enumerate(plane)
        ]
        for copy in sends:
            copy.start()
        fourth.append(sends)
    for s in range(count):
        for copy in fourth[s]:
            copy.wait_recv()
        copy = mesh_copy(full[s].at[:, side], full[s].at[:, side], over, s, pair)
        copy.start()
        fifth.append(copy)
    for s in range(count):
        first[s].wait_send()
        for copy in second[s] + third[s] + fourth[s]:
            copy.wait_send()
        fifth[s].wait()


def reduce_pieces(plan, parts, name, collective_id):
    shards, places = plan
    count = len(parts)
    tails = [part.shape[3:] for part in parts]

    def scratch(*lead):
        return [pltpu.VMEM(lead + tail, jnp.bfloat16) for tail in tails]

    return pl.pallas_call(
        functools.partial(reduce_kernel, plan, count),
        in_specs=[pl.BlockSpec(memory_space=pl.ANY)] * count,
        out_specs=[pl.BlockSpec(memory_space=pltpu.VMEM)] * count,
        out_shape=[jax.ShapeDtypeStruct((places, 2) + tail, jnp.bfloat16) for tail in tails],
        scratch_shapes=scratch(shards, places)
        + scratch(shards, places)
        + scratch(places - 1, shards)
        + scratch(shards - 1)
        + [
            pltpu.SemaphoreType.DMA((count,)),
            pltpu.SemaphoreType.DMA((2, count)),
            pltpu.SemaphoreType.DMA((2, count * (places - 1))),
            pltpu.SemaphoreType.DMA((2, count * (shards - 1))),
            pltpu.SemaphoreType.DMA((2, count * (places - 1))),
            pltpu.SemaphoreType.DMA((2, count)),
        ],
        compiler_params=pltpu.CompilerParams(
            collective_id=collective_id, has_side_effects=True, vmem_limit_bytes=48 << 20
        ),
        cost_estimate=pl.CostEstimate(flops=0, bytes_accessed=32 << 20, transcendentals=0),
        name=name,
    )(*parts)


def cut_of(rows, columns, dp):
    best = None
    across = 1
    while across <= dp and across * LANES <= columns:
        down = dp // across
        tall = -(-rows // (16 * down)) * 16
        if best is None or down * tall < best[0] * best[2]:
            best = (down, across, tall)
        across *= 2
    return best


def to_pieces(shards, array, dp):
    rows, columns = array.shape[1:]
    down, across, tall = cut_of(rows, columns, dp)
    array = jnp.pad(array, ((0, 0), (0, down * tall - rows), (0, 0)))
    array = array.reshape(shards, down, tall, across, columns // across).transpose(0, 1, 3, 2, 4)
    return array.reshape(shards, dp // 2, 2, tall, columns // across)


def from_pieces(pieces, rows, columns, dp):
    shards = pieces.shape[0]
    down, across, tall = cut_of(rows, columns, dp)
    array = pieces.reshape(shards, down, across, tall, columns // across).transpose(0, 1, 3, 2, 4)
    return array.reshape(shards, down * tall, columns)[:, :rows]


def own_piece(array, dp):
    rows, columns = array.shape
    down, across, tall = cut_of(rows, columns, dp)
    array = jnp.pad(array, ((0, down * tall - rows), (0, 0)))
    group = lax.axis_index("dp")
    at = (group // across * tall, lax.rem(group, across) * (columns // across))
    return lax.dynamic_slice(array, at, (tall, columns // across))


def contract(left, right, left_dim, right_dim):
    return lax.dot_general(
        left, right, (((left_dim,), (right_dim,)), ((), ())), preferred_element_type=jnp.float32
    )


def channel_decay(rows_total):
    places = jnp.arange(rows_total, dtype=jnp.int32)[:, None]
    return ((places >= N) & (places < N + CONV)).astype(jnp.float32)


def adam_direction(weight, grad, first, second, factor, decay):
    clipped = grad * factor
    first = beta_one * first + (1.0 - beta_one) * clipped
    second = beta_two * second + (1.0 - beta_two) * clipped * clipped
    first_hat = first / (1.0 - beta_one**adam_step)
    second_hat = second / (1.0 - beta_two**adam_step)
    return first_hat / (jnp.sqrt(second_hat) + adam_eps) + decay_rate * decay * weight


def local(
    shards,
    dp,
    tokens,
    lengths,
    cotangent,
    norm_gain,
    input_weight,
    select_weight,
    step_weight,
    channel_params,
    output_weight,
    moment_gain,
    moment_input,
    moment_select,
    moment_step,
    moment_channel,
    moment_output,
    square_gain,
    square_input,
    square_select,
    square_step,
    square_channel,
    square_output,
):
    row_count = tokens.shape[0]
    live_mask, offset = block_layout(lengths[0], row_count)
    restart = (offset == 0).astype(jnp.float32)
    plan = (shards, dp // 2)
    low_conv, low_gate, low_output = (
        own_piece(weight, dp).astype(jnp.bfloat16)
        for weight in (input_weight[:, :DI], input_weight[:, DI:], output_weight)
    )
    low_small = own_piece(jnp.concatenate([select_weight, step_weight], axis=0), dp).astype(jnp.bfloat16)
    width = channel_params.shape[1]
    vectors = jnp.concatenate(
        [channel_params, jnp.pad(norm_gain, (0, width - norm_gain.shape[0]))[None, :]], axis=0
    )
    full_conv, full_small, full_vectors, full_gate, full_output = gather_pieces(
        plan, [low_conv, low_small, own_piece(vectors, dp), low_gate, low_output], "gather_weights", 0
    )
    full_input = jnp.concatenate([full_conv.reshape(-1, DI), full_gate.reshape(-1, DI)], axis=1)
    full_output = full_output.reshape(DI, -1)
    small_rows = R + 2 * N + R
    full_small = from_pieces(full_small, small_rows, width, dp).transpose(1, 0, 2).reshape(small_rows, DI)
    full_select, full_step = full_small[: R + 2 * N], full_small[R + 2 * N :]
    full_vectors = from_pieces(full_vectors, vectors.shape[0], width, dp)
    gain = full_vectors[:, -1, : norm_gain.shape[0]].reshape(-1)
    channel = full_vectors[:, :-1].transpose(1, 0, 2).reshape(-1, DI)
    inputs = tokens.astype(jnp.float32)
    normed_value, norm_pull = jax.vjp(rms_scale, inputs, gain)
    normed = normed_value.astype(jnp.bfloat16)
    projected = jnp.dot(normed, full_input, preferred_element_type=jnp.float32)
    conv_input = projected[:, :DI]
    gate_half = projected[:, DI:]

    def conv_piece(values, kernel, shift):
        return jax.nn.silu(causal_conv(values, kernel, shift, offset))

    conv_value, conv_pull = jax.vjp(
        conv_piece, conv_input, channel[N : N + CONV], channel[N + CONV]
    )
    mixed = conv_value.astype(jnp.bfloat16)
    mixed_values = mixed.astype(jnp.float32)
    selection = contract(mixed, full_select, 1, 1)
    step_low = selection[:, :R].astype(jnp.bfloat16)
    step_pre = jnp.dot(step_low, full_step, preferred_element_type=jnp.float32)
    step_in = step_pre + channel[N + CONV + 1][None, :]
    step_size = jax.nn.softplus(step_in)
    rates = -jnp.exp(channel[:N])
    rates_low = (rates * math.log2(math.e)).reshape(2 * N, 8, LANES)
    chosen = jnp.concatenate(
        [selection[:, R:], restart[:, None], jnp.zeros((row_count, LANES - 2 * N - 1), jnp.float32)], axis=1
    )
    skip = channel[N + CONV + 2][None, :]
    state_out, states = scan_forward(step_size, mixed_values, chosen, rates_low)
    scanned = state_out + skip * mixed_values
    gate_value, gate_pull = jax.vjp(jax.nn.silu, gate_half)
    gated = (scanned * gate_value).astype(jnp.bfloat16)
    branch = jnp.dot(gated, full_output, preferred_element_type=jnp.float32)
    layer_output = (inputs + live_mask[:, None] * branch).astype(jnp.bfloat16)
    upstream = cotangent.astype(jnp.float32)
    grad_branch = (upstream * live_mask[:, None]).astype(jnp.bfloat16)
    grad_output = contract(gated, grad_branch, 0, 0).astype(jnp.bfloat16)
    grad_gated = contract(grad_branch, full_output, 1, 1)
    grad_scanned = grad_gated * gate_value
    (grad_gate,) = gate_pull(grad_gated * scanned)
    sum_in, sum_decay, parts, sums = scan_backward(
        step_size, mixed_values, grad_scanned, chosen, rates_low, states
    )
    grad_both = jnp.sum(parts, axis=2)
    grad_mixed = step_size * sum_in + skip * grad_scanned
    grad_pre = (mixed_values * sum_in + math.log(2.0) * sum_decay) * jax.nn.sigmoid(step_in)
    grad_pre_low = grad_pre.astype(jnp.bfloat16)
    grad_step = contract(step_low, grad_pre_low, 0, 0)
    grad_step_low = contract(grad_pre_low, full_step, 1, 1)
    grad_selection = jnp.concatenate([grad_step_low, grad_both], axis=1).astype(jnp.bfloat16)
    grad_select = contract(grad_selection, mixed, 0, 0)
    grad_mixed = grad_mixed + jnp.dot(
        grad_selection, full_select, preferred_element_type=jnp.float32
    )
    grad_conv_input, grad_kernel, grad_shift = conv_pull(grad_mixed)
    grad_projected = jnp.concatenate([grad_conv_input, grad_gate], axis=1).astype(jnp.bfloat16)
    grad_conv_weight, grad_gate_weight = (
        contract(normed, half, 0, 0).astype(jnp.bfloat16)
        for half in (grad_projected[:, :DI], grad_projected[:, DI:])
    )
    grad_normed = contract(grad_projected, full_input, 1, 1)
    grad_inputs, grad_gain = norm_pull(grad_normed)
    input_grad = (upstream + grad_inputs).astype(jnp.bfloat16)
    grad_channel = jnp.concatenate(
        [
            rates * sums.reshape(N, DI),
            grad_kernel,
            grad_shift[None, :],
            jnp.sum(grad_pre, axis=0, keepdims=True),
            jnp.sum(grad_scanned * mixed_values, axis=0, keepdims=True),
        ],
        axis=0,
    )
    small = jnp.concatenate([grad_select, grad_step, grad_channel], axis=0)
    small = small.reshape(-1, shards, width).transpose(1, 0, 2)
    small_gain = jnp.pad(grad_gain.reshape(shards, 1, -1), ((0, 0), (0, 0), (0, width - grad_gain.shape[0] // shards)))
    small = jnp.concatenate([small, small_gain], axis=1).astype(jnp.bfloat16)
    heights = [norm_gain.shape[0], output_weight.shape[0]]
    sum_output, sum_gate, sum_conv, sum_small = reduce_pieces(
        plan,
        [
            to_pieces(shards, grad_output.reshape(shards, heights[1], -1), dp),
            to_pieces(shards, grad_gate_weight.reshape(shards, heights[0], -1), dp),
            to_pieces(shards, grad_conv_weight.reshape(shards, heights[0], -1), dp),
            to_pieces(shards, small, dp),
        ],
        "sum_gradients",
        1,
    )
    sum_output, sum_gate, sum_conv, sum_small = (
        from_pieces(pieces[None], rows, columns, dp)[0].astype(jnp.float32)
        for pieces, rows, columns in (
            (sum_output, heights[1], output_weight.shape[1]),
            (sum_gate, heights[0], DI),
            (sum_conv, heights[0], DI),
            (sum_small, small.shape[1], width),
        )
    )
    sum_input = jnp.concatenate([sum_conv, sum_gate], axis=1)
    sum_select, sum_step = sum_small[: R + 2 * N], sum_small[R + 2 * N : small_rows]
    sum_channel, sum_gain = sum_small[small_rows:-1], sum_small[-1, : norm_gain.shape[0]]
    grads = (sum_gain, sum_input, sum_select, sum_step, sum_channel, sum_output)
    local_square = sum([jnp.sum(grad * grad) for grad in grads])
    total_square = lax.psum(local_square, "fsdp")
    grad_norm = jnp.sqrt(total_square)
    factor = jnp.minimum(1.0, clip_norm / (grad_norm + 1e-06))
    params = (norm_gain, input_weight, select_weight, step_weight, channel_params, output_weight)
    firsts = (moment_gain, moment_input, moment_select, moment_step, moment_channel, moment_output)
    seconds = (square_gain, square_input, square_select, square_step, square_channel, square_output)
    decays = (0.0, 1.0, 1.0, 1.0, channel_decay(channel_params.shape[0]), 1.0)
    updates = [
        adam_direction(
            params[which], grads[which], firsts[which], seconds[which], factor, decays[which]
        )
        for which in range(6)
    ]
    return (
        layer_output,
        input_grad,
        grad_norm,
        updates[0],
        updates[1],
        updates[2],
        updates[3],
        updates[4],
        updates[5],
        grads[0],
        grads[1],
        grads[2],
        grads[3],
        grads[4],
        grads[5],
    )


def solution(mesh):
    in_specs = (
        P(("dp", "fsdp"), None),
        P(("dp", "fsdp"), None),
        P(("dp", "fsdp"), None),
        P("fsdp"),
        P("fsdp", None),
        P(None, "fsdp"),
        P(None, "fsdp"),
        P(None, "fsdp"),
        P("fsdp", None),
        P("fsdp"),
        P("fsdp", None),
        P(None, "fsdp"),
        P(None, "fsdp"),
        P(None, "fsdp"),
        P("fsdp", None),
        P("fsdp"),
        P("fsdp", None),
        P(None, "fsdp"),
        P(None, "fsdp"),
        P(None, "fsdp"),
        P("fsdp", None),
    )
    out_specs = (
        P(("dp", "fsdp"), None),
        P(("dp", "fsdp"), None),
        P(),
        P("fsdp"),
        P("fsdp", None),
        P(None, "fsdp"),
        P(None, "fsdp"),
        P(None, "fsdp"),
        P("fsdp", None),
        P("fsdp"),
        P("fsdp", None),
        P(None, "fsdp"),
        P(None, "fsdp"),
        P(None, "fsdp"),
        P("fsdp", None),
    )
    shards, dp = mesh.shape["fsdp"], mesh.shape["dp"]
    return jax.shard_map(functools.partial(local, shards, dp), mesh=mesh, in_specs=in_specs, out_specs=out_specs, check_vma=False)
```

```python
import functools
import math

import jax
import jax.numpy as jnp
from jax import lax
from jax.experimental import pallas as pl
from jax.experimental.pallas import tpu as pltpu
from jax.sharding import PartitionSpec as P

DI = 2048
N = 16
R = 64
CONV = 4
LANES = 128
COLS = DI // LANES
HALVES = COLS // 8
BLOCK = 64
GROUP = 8
BACK = 4
WIDE = 512
TAIL = 4

norm_eps = 1e-05
beta_one = 0.9
beta_two = 0.95
adam_eps = 1e-08
decay_rate = 0.1
adam_step = 10.0
clip_norm = 1.0
RESET = 1e30


def block_layout(lengths_row, count):
    places = jnp.arange(count, dtype=jnp.int32)
    begun = jnp.zeros((count,), jnp.int32)
    end = jnp.zeros((), jnp.int32)
    for cluster in range(lengths_row.shape[0]):
        begun = jnp.where(end <= places, jnp.maximum(begun, end), begun)
        end = end + lengths_row[cluster]
    live_mask = (places < end).astype(jnp.float32)
    return live_mask, places - begun

def rms_scale(values, scales):
    return (
        values
        * lax.rsqrt(jnp.mean(values * values, axis=1, keepdims=True) + norm_eps)
        * scales[None, :]
    )


def causal_conv(values, kernel, shift, offset):
    total = shift[None, :] + kernel[CONV - 1][None, :] * values
    for distance in range(1, CONV):
        moved = jnp.pad(values, ((distance, 0), (0, 0)))[:-distance]
        keep = (offset >= distance).astype(jnp.float32)[:, None]
        total = total + kernel[CONV - 1 - distance][None, :] * moved * keep
    return total


def spread(ref, value, g):
    for col in range(COLS):
        ref[pl.ds(g * 8 * COLS + col, 8, stride=COLS), :] = value[:, LANES * col : LANES * (col + 1)]


def unspread(out, ref, g):
    rows = pl.multiple_of(g * 8, 8)
    for col in range(COLS):
        out[pl.ds(rows, 8), LANES * col : LANES * (col + 1)] = ref[pl.ds(g * 8 * COLS + col, 8, stride=COLS), :]


def token_rows(g, token):
    return pl.ds(pl.multiple_of(g * 8 * COLS, 8 * COLS) + token * COLS, COLS)


def prepare(g, sel, step, mixed, dts, us, bb):
    chosen = sel[pl.ds(pl.multiple_of(g * 8, 8), 8), :]
    fresh = chosen[:, 2 * N : 2 * N + 1] > 0.5
    spread(dts, jnp.where(fresh, RESET, step), g)
    spread(us, step * mixed, g)
    for k in range(2 * N):
        bb[g, k] = jnp.broadcast_to(chosen[:, k : k + 1], (8, LANES))


def splat(bb, g, first, count, token):
    return jnp.stack([bb[g, first + n, pl.ds(token, COLS, stride=0), :] for n in range(count)])


def softplus(v):
    small = jnp.exp(-jnp.abs(v))
    series = small * (1.0 - small * (1 / 2 - small * (1 / 3 - small * (1 / 4 - small * (1 / 5)))))
    return jnp.maximum(v, 0.0) + jnp.where(small < 1 / 32, series, jnp.log(1.0 + small))


def forward_kernel(v_ref, mixed_ref, sel, rates, y_ref, dt_ref, hs_ref, state, dts, us, bb, ys):
    @pl.when(pl.program_id(0) == 0)
    def _():
        state[...] = jnp.zeros_like(state)

    @pl.loop(0, BLOCK // 8)
    def _(g):
        rows = pl.ds(pl.multiple_of(g * 8, 8), 8)
        dt_ref[rows, :] = softplus(v_ref[rows, :])

    @pl.loop(0, BLOCK // 16)
    def _(pair):
        mixed = mixed_ref[pl.ds(pl.multiple_of(pair * 16, 16), 16), :].astype(jnp.float32)
        for side in range(2):
            g = pair * 2 + side
            step = dt_ref[pl.ds(pl.multiple_of(g * 8, 8), 8), :]
            prepare(g, sel, step, mixed[8 * side : 8 * side + 8], dts, us, bb)

    for low in range(0, N, GROUP):
        part = pl.ds(low, GROUP)

        def steps(g, kept):
            for token in range(8):
                at = token_rows(g, token)
                decay = jnp.exp2(dts[at, :][None] * rates[part])
                kept = decay * kept + splat(bb, g, low, GROUP, token) * us[at, :][None]
                hs_ref[g * 8 + token, part] = kept
                total = jnp.sum(splat(bb, g, N + low, GROUP, token) * kept, axis=0)
                ys[at, :] = total if low == 0 else ys[at, :] + total
            return kept

        state[part] = lax.fori_loop(0, BLOCK // 8, steps, state[part])

    @pl.loop(0, BLOCK // 8)
    def _(g):
        unspread(y_ref, ys, g)


def fold(value):
    return jnp.sum(value.reshape(value.shape[0] // 8, 8, value.shape[1]), axis=0)


def backward_kernel(
    v_ref, dt_ref, mixed_ref, gs_ref, sel, rates, vectors,
    step_weight, select_weight, hs_ref, last_ref, conv_ref, slope_ref, flags,
    grad_conv_in, pre_low, chosen, grad_rows, grad_rates,
    carry, dts, us, gss, bb, s1, s2, prods, parts, nat1, nat2, grad_mixed, taps,
):
    turn = lax.rem(pl.program_id(0), TAIL)
    tall = BLOCK * TAIL
    own = pl.ds(pl.multiple_of((TAIL - 1 - turn) * BLOCK, BLOCK), BLOCK)

    @pl.when(pl.program_id(0) == 0)
    def _():
        for ref in (carry, grad_rates, grad_rows, parts):
            ref[...] = jnp.zeros_like(ref)
        taps[:, tall:, :] = jnp.zeros_like(taps[:, tall:, :])

    @pl.loop(0, BLOCK // 16)
    def _(pair):
        mixed = mixed_ref[pl.ds(pl.multiple_of(pair * 16, 16), 16), :].astype(jnp.float32)
        for side in range(2):
            g = pair * 2 + side
            rows = pl.ds(pl.multiple_of(g * 8, 8), 8)
            prepare(g, sel, dt_ref[rows, :], mixed[8 * side : 8 * side + 8], dts, us, bb)
            spread(gss, gs_ref[rows, :], g)

    spot = lax.broadcasted_iota(jnp.int32, (8, LANES), 1)
    for low in range(0, N, BACK):
        part = pl.ds(low, BACK)

        def steps(step, carried):
            g = BLOCK // 8 - 1 - step
            kept, total, sums = carried
            for token in reversed(range(8)):
                at = token_rows(g, token)
                dt, u, gs = dts[at, :][None], us[at, :][None], gss[at, :][None]
                if token > 0:
                    before = hs_ref[g * 8 + token - 1, part]
                else:
                    before = jnp.where(g == 0, last_ref[0, part], hs_ref[jnp.maximum(g * 8 - 1, 0), part])
                rate = rates[part]
                adjoint = splat(bb, g, N + low, BACK, token) * gs + kept
                for_c = gs * hs_ref[g * 8 + token, part]
                for_b = adjoint * u
                in_sum = jnp.sum(splat(bb, g, low, BACK, token) * adjoint, axis=0)
                kept = jnp.exp2(dt * rate) * adjoint
                slope = kept * before
                decay_sum = jnp.sum(rate * slope, axis=0)
                total = total + dt * slope
                for kind, value in enumerate((for_b, for_c)):
                    prods[token % 2, pl.ds(8 * BACK * kind, 8 * BACK), :] = (value[:, :8] + value[:, 8:]).reshape(8 * BACK, LANES)
                here = spot == g * 8 + token
                new = []
                for first in range(0, 2 * BACK, 8):
                    rows_of = [prods[token % 2, pl.ds(8 * first + s, 8, stride=8), :] for s in range(8)]
                    while len(rows_of) > 1:
                        rows_of = [a + b for a, b in zip(rows_of[::2], rows_of[1::2])]
                    new.append(jnp.where(here, jnp.sum(rows_of[0], axis=1, keepdims=True), sums[first // 8]))
                sums = tuple(new)
                s1[at, :] = in_sum if low == 0 else s1[at, :] + in_sum
                s2[at, :] = decay_sum if low == 0 else s2[at, :] + decay_sum
            return kept, total, sums

        nothing = tuple(jnp.zeros((8, LANES), jnp.float32) for _ in range(2 * BACK // 8))
        carry[part], grad_rates[part], sums = lax.fori_loop(
            0, BLOCK // 8, steps, (carry[part], grad_rates[part], nothing)
        )
        sums = jnp.concatenate(sums, axis=0)
        parts[pl.ds(low, BACK), :] = sums[:BACK]
        parts[pl.ds(N + low, BACK), :] = sums[BACK:]

    @pl.loop(0, BLOCK // 8)
    def _(g):
        unspread(nat1, s1, g)
        unspread(nat2, s2, g)

    @pl.loop(0, DI // WIDE)
    def _(c):
        lanes = pl.ds(pl.multiple_of(c * WIDE, WIDE), WIDE)
        mixed = mixed_ref[:, lanes].astype(jnp.float32)
        step, gs, in_sum = dt_ref[:, lanes], gs_ref[:, lanes], nat1[:, lanes]
        pre = (mixed * in_sum + math.log(2.0) * nat2[:, lanes]) * jnp.exp(v_ref[:, lanes] - step)
        pre_low[own, lanes] = pre.astype(jnp.bfloat16)
        grad_mixed[own, lanes] = step * in_sum + vectors[CONV + 2 : CONV + 3, lanes] * gs
        grad_rows[CONV + 1, :, lanes] += fold(pre)
        grad_rows[CONV + 2, :, lanes] += fold(gs * mixed)

    chosen[own, R:] = parts[...].T[:BLOCK, : 2 * N].astype(jnp.bfloat16)

    @pl.when(turn == TAIL - 1)
    def _():
        chosen[:, :R] = dot(pre_low[...], step_weight[...], 1, 1).astype(jnp.bfloat16)

        @pl.loop(0, DI // WIDE)
        def _(c):
            lanes = pl.ds(pl.multiple_of(c * WIDE, WIDE), WIDE)
            total = grad_mixed[:, lanes] + dot(chosen[...], select_weight[:, lanes], 1, 0)
            grad_conv = total * slope_ref[:, lanes]
            value = conv_ref[:, lanes]
            grad_rows[CONV, :, lanes] += fold(grad_conv)
            result = vectors[CONV - 1 : CONV, lanes] * grad_conv
            grad_rows[CONV - 1, :, lanes] += fold(grad_conv * value)
            for j in range(1, CONV):
                taps[j - 1, :tall, lanes] = grad_conv * flags[:, 2 * N + j : 2 * N + j + 1]
                later = taps[j - 1, :, lanes][j : j + tall]
                grad_rows[CONV - 1 - j, :, lanes] += fold(later * value)
                result = result + vectors[CONV - 1 - j : CONV - j, lanes] * later
                taps[j - 1, tall:, lanes] = taps[j - 1, :8, lanes]
            grad_conv_in[:, lanes] = result.astype(jnp.bfloat16)


def dot(left, right, left_dim, right_dim):
    return lax.dot_general(
        left, right, (((left_dim,), (right_dim,)), ((), ())), preferred_element_type=jnp.float32
    )


def scan_forward(v, mixed, sel, rates):
    count = v.shape[0]
    rows = pl.BlockSpec((BLOCK, DI), lambda i: (i, 0))
    return pl.pallas_call(
        forward_kernel,
        grid=(count // BLOCK,),
        in_specs=[
            rows,
            rows,
            pl.BlockSpec((BLOCK, LANES), lambda i: (i, 0)),
            pl.BlockSpec((N, COLS, LANES), lambda i: (0, 0, 0)),
        ],
        out_specs=[rows, rows, pl.BlockSpec((BLOCK, N, COLS, LANES), lambda i: (i, 0, 0, 0))],
        out_shape=[
            jax.ShapeDtypeStruct((count, DI), jnp.float32),
            jax.ShapeDtypeStruct((count, DI), jnp.float32),
            jax.ShapeDtypeStruct((count, N, COLS, LANES), jnp.float32),
        ],
        scratch_shapes=[
            pltpu.VMEM((N, COLS, LANES), jnp.float32),
            pltpu.VMEM((BLOCK * COLS, LANES), jnp.float32),
            pltpu.VMEM((BLOCK * COLS, LANES), jnp.float32),
            pltpu.VMEM((BLOCK // 8, 2 * N, 8, LANES), jnp.float32),
            pltpu.VMEM((BLOCK * COLS, LANES), jnp.float32),
        ],
        compiler_params=pltpu.CompilerParams(vmem_limit_bytes=48 << 20),
        cost_estimate=pl.CostEstimate(
            flops=6 * count * N * DI, bytes_accessed=4 * count * N * DI, transcendentals=count * N * DI
        ),
        name="scan_forward",
    )(v, mixed, sel, rates)


def scan_backward(v, dt, mixed, gs, conv_input, slope, sel, rates, vectors, step_weight, select_weight, states):
    count = dt.shape[0]
    blocks = count // BLOCK
    rows = pl.BlockSpec((BLOCK, DI), lambda i: (blocks - 1 - i, 0))

    def tall(width):
        return pl.BlockSpec((BLOCK * TAIL, width), lambda i: (blocks // TAIL - 1 - i // TAIL, 0))

    def whole(*shape):
        return pl.BlockSpec(shape, lambda i: (0,) * len(shape))

    state = (N, COLS, LANES)
    return pl.pallas_call(
        backward_kernel,
        grid=(blocks,),
        in_specs=[
            rows,
            rows,
            rows,
            rows,
            pl.BlockSpec((BLOCK, LANES), lambda i: (blocks - 1 - i, 0)),
            whole(*state),
            whole(8, DI),
            whole(R, DI),
            whole(R + 2 * N, DI),
            pl.BlockSpec((BLOCK,) + state, lambda i: (blocks - 1 - i, 0, 0, 0)),
            pl.BlockSpec((1,) + state, lambda i: (jnp.maximum((blocks - 1 - i) * BLOCK - 1, 0), 0, 0, 0)),
            tall(DI),
            tall(DI),
            tall(LANES),
        ],
        out_specs=[tall(DI), tall(DI), tall(R + 2 * N), whole(8, 8, DI), whole(*state)],
        out_shape=[
            jax.ShapeDtypeStruct((count, DI), jnp.bfloat16),
            jax.ShapeDtypeStruct((count, DI), jnp.bfloat16),
            jax.ShapeDtypeStruct((count, R + 2 * N), jnp.bfloat16),
            jax.ShapeDtypeStruct((8, 8, DI), jnp.float32),
            jax.ShapeDtypeStruct(state, jnp.float32),
        ],
        scratch_shapes=[pltpu.VMEM(state, jnp.float32)]
        + [pltpu.VMEM((BLOCK * COLS, LANES), jnp.float32)] * 3
        + [pltpu.VMEM((BLOCK // 8, 2 * N, 8, LANES), jnp.float32)]
        + [pltpu.VMEM((BLOCK * COLS, LANES), jnp.float32)] * 2
        + [pltpu.VMEM((2, 16 * BACK, LANES), jnp.float32)]
        + [pltpu.VMEM((LANES, LANES), jnp.float32)]
        + [pltpu.VMEM((BLOCK, DI), jnp.float32)] * 2
        + [pltpu.VMEM((BLOCK * TAIL, DI), jnp.float32)]
        + [pltpu.VMEM((CONV - 1, BLOCK * TAIL + 8, DI), jnp.float32)],
        compiler_params=pltpu.CompilerParams(vmem_limit_bytes=60 << 20),
        cost_estimate=pl.CostEstimate(
            flops=20 * count * N * DI, bytes_accessed=4 * count * N * DI, transcendentals=count * N * DI
        ),
        name="scan_backward",
    )(
        v, dt, mixed, gs, sel, rates, vectors, step_weight, select_weight,
        states, states, conv_input, slope, sel,
    )


def mesh_copy(src, dst, sems, at, device):
    return pltpu.make_async_remote_copy(
        src_ref=src,
        dst_ref=dst,
        send_sem=sems.at[0, at],
        recv_sem=sems.at[1, at],
        device_id=device,
        device_id_type=pl.DeviceIdType.MESH,
    )


def placed(plan):
    group = lax.axis_index("dp")
    return lax.axis_index("fsdp"), group // 2, lax.rem(group, 2)


def peers_of(plan):
    shards, places = plan
    mine, place, side = placed(plan)
    along = [(place * 2 + side, lax.rem(mine + k, shards)) for k in range(1, shards)]
    plane = [((place ^ j) * 2 + side, mine) for j in range(1, places)]
    return along, plane, (place * 2 + 1 - side, mine)


def greet(plan):
    along, plane, pair = peers_of(plan)
    barrier = pltpu.get_barrier_semaphore()
    everyone = along + plane + [pair]
    for device in everyone:
        pl.semaphore_signal(barrier, inc=1, device_id=device, device_id_type=pl.DeviceIdType.MESH)
    pl.semaphore_wait(barrier, len(everyone))


def gather_kernel(plan, count, *refs):
    own, full = refs[:count], refs[count : 2 * count]
    near, far, wide, cross = refs[2 * count :]
    shards, places = plan
    mine, place, side = placed(plan)
    along, plane, pair = peers_of(plan)
    greet(plan)
    local, first, second, third = [], [], [], []
    for s in range(count):
        keep = pltpu.make_async_copy(own[s], full[s].at[mine, place, side], near.at[s])
        keep.start()
        local.append(keep)
        sends = [
            mesh_copy(own[s], full[s].at[mine, place, side], far, s * (shards - 1) + k, device)
            for k, device in enumerate(along)
        ]
        for copy in sends:
            copy.start()
        first.append(sends)
    for s in range(count):
        local[s].wait()
        for copy in first[s]:
            copy.wait_recv()
        sends = [
            mesh_copy(
                full[s].at[:, place, side], full[s].at[:, place, side], wide, s * (places - 1) + k, device
            )
            for k, device in enumerate(plane)
        ]
        for copy in sends:
            copy.start()
        second.append(sends)
    for s in range(count):
        for copy in second[s]:
            copy.wait_recv()
        copy = mesh_copy(full[s].at[:, :, side], full[s].at[:, :, side], cross, s, pair)
        copy.start()
        third.append(copy)
    for s in range(count):
        for copy in first[s] + second[s]:
            copy.wait_send()
        third[s].wait()


def gather_pieces(plan, pieces, name, collective_id):
    shards, places = plan
    count = len(pieces)
    return pl.pallas_call(
        functools.partial(gather_kernel, plan, count),
        in_specs=[pl.BlockSpec(memory_space=pl.ANY)] * count,
        out_specs=[pl.BlockSpec(memory_space=pl.ANY)] * count,
        out_shape=[jax.ShapeDtypeStruct((shards, places, 2) + piece.shape, piece.dtype) for piece in pieces],
        scratch_shapes=[
            pltpu.SemaphoreType.DMA((count,)),
            pltpu.SemaphoreType.DMA((2, count * (shards - 1))),
            pltpu.SemaphoreType.DMA((2, count * (places - 1))),
            pltpu.SemaphoreType.DMA((2, count)),
        ],
        compiler_params=pltpu.CompilerParams(collective_id=collective_id, has_side_effects=True),
        cost_estimate=pl.CostEstimate(flops=0, bytes_accessed=32 << 20, transcendentals=0),
        name=name,
    )(*pieces)


def wide_sum(values):
    total = values[0].astype(jnp.float32)
    for value in values[1:]:
        total = total + value.astype(jnp.float32)
    return total.astype(jnp.bfloat16)


def reduce_kernel(plan, count, *refs):
    parts, full = refs[:count], refs[count : 2 * count]
    held = refs[2 * count : 3 * count]
    from_pair = refs[3 * count : 4 * count]
    from_plane = refs[4 * count : 5 * count]
    from_along = refs[5 * count : 6 * count]
    near, cross, wide, far, back, over = refs[6 * count :]
    shards, places = plan
    mine, place, side = placed(plan)
    along, plane, pair = peers_of(plan)
    greet(plan)
    local, first, second, third, fourth, fifth = [], [], [], [], [], []
    for s in range(count):
        keep = pltpu.make_async_copy(parts[s].at[:, :, side], held[s], near.at[s])
        keep.start()
        local.append(keep)
        copy = mesh_copy(parts[s].at[:, :, 1 - side], from_pair[s], cross, s, pair)
        copy.start()
        first.append(copy)
    for s in range(count):
        local[s].wait()
        first[s].wait_recv()

        @pl.loop(0, shards * places)
        def _(i, s=s):
            a, b = i // places, lax.rem(i, places)
            held[s][a, b] = wide_sum([held[s][a, b], from_pair[s][a, b]])

        sends = [
            mesh_copy(held[s].at[:, place ^ (k + 1)], from_plane[s].at[k], wide, s * (places - 1) + k, device)
            for k, device in enumerate(plane)
        ]
        for copy in sends:
            copy.start()
        second.append(sends)
    for s in range(count):
        for copy in second[s]:
            copy.wait_recv()

        @pl.loop(0, shards)
        def _(i, s=s):
            held[s][i, place] = wide_sum([held[s][i, place]] + [from_plane[s][k, i] for k in range(places - 1)])

        sends = [
            mesh_copy(
                held[s].at[lax.rem(mine + k + 1, shards), place],
                from_along[s].at[k],
                far,
                s * (shards - 1) + k,
                device,
            )
            for k, device in enumerate(along)
        ]
        for copy in sends:
            copy.start()
        third.append(sends)
    for s in range(count):
        for copy in third[s]:
            copy.wait_recv()
        full[s][place, side] = wide_sum([held[s][mine, place]] + [from_along[s][k] for k in range(shards - 1)])
        sends = [
            mesh_copy(full[s].at[place, side], full[s].at[place, side], back, s * (places - 1) + k, device)
            for k, device in enumerate(plane)
        ]
        for copy in sends:
            copy.start()
        fourth.append(sends)
    for s in range(count):
        for copy in fourth[s]:
            copy.wait_recv()
        copy = mesh_copy(full[s].at[:, side], full[s].at[:, side], over, s, pair)
        copy.start()
        fifth.append(copy)
    for s in range(count):
        first[s].wait_send()
        for copy in second[s] + third[s] + fourth[s]:
            copy.wait_send()
        fifth[s].wait()


def reduce_pieces(plan, parts, name, collective_id):
    shards, places = plan
    count = len(parts)
    tails = [part.shape[3:] for part in parts]

    def scratch(*lead):
        return [pltpu.VMEM(lead + tail, jnp.bfloat16) for tail in tails]

    return pl.pallas_call(
        functools.partial(reduce_kernel, plan, count),
        in_specs=[pl.BlockSpec(memory_space=pl.ANY)] * count,
        out_specs=[pl.BlockSpec(memory_space=pltpu.VMEM)] * count,
        out_shape=[jax.ShapeDtypeStruct((places, 2) + tail, jnp.bfloat16) for tail in tails],
        scratch_shapes=scratch(shards, places)
        + scratch(shards, places)
        + scratch(places - 1, shards)
        + scratch(shards - 1)
        + [
            pltpu.SemaphoreType.DMA((count,)),
            pltpu.SemaphoreType.DMA((2, count)),
            pltpu.SemaphoreType.DMA((2, count * (places - 1))),
            pltpu.SemaphoreType.DMA((2, count * (shards - 1))),
            pltpu.SemaphoreType.DMA((2, count * (places - 1))),
            pltpu.SemaphoreType.DMA((2, count)),
        ],
        compiler_params=pltpu.CompilerParams(
            collective_id=collective_id, has_side_effects=True, vmem_limit_bytes=48 << 20
        ),
        cost_estimate=pl.CostEstimate(flops=0, bytes_accessed=32 << 20, transcendentals=0),
        name=name,
    )(*parts)


def cut_of(rows, columns, dp):
    best = None
    across = 1
    while across <= dp and across * LANES <= columns:
        down = dp // across
        tall = -(-rows // (16 * down)) * 16
        if best is None or down * tall < best[0] * best[2]:
            best = (down, across, tall)
        across *= 2
    return best


def to_pieces(shards, array, dp):
    rows, columns = array.shape[1:]
    down, across, tall = cut_of(rows, columns, dp)
    array = jnp.pad(array, ((0, 0), (0, down * tall - rows), (0, 0)))
    array = array.reshape(shards, down, tall, across, columns // across).transpose(0, 1, 3, 2, 4)
    return array.reshape(shards, dp // 2, 2, tall, columns // across)


def from_pieces(pieces, rows, columns, dp):
    shards = pieces.shape[0]
    down, across, tall = cut_of(rows, columns, dp)
    array = pieces.reshape(shards, down, across, tall, columns // across).transpose(0, 1, 3, 2, 4)
    return array.reshape(shards, down * tall, columns)[:, :rows]


def own_piece(array, dp):
    rows, columns = array.shape
    down, across, tall = cut_of(rows, columns, dp)
    array = jnp.pad(array, ((0, down * tall - rows), (0, 0)))
    group = lax.axis_index("dp")
    at = (group // across * tall, lax.rem(group, across) * (columns // across))
    return lax.dynamic_slice(array, at, (tall, columns // across))


def contract(left, right, left_dim, right_dim):
    return lax.dot_general(
        left, right, (((left_dim,), (right_dim,)), ((), ())), preferred_element_type=jnp.float32
    )


def channel_decay(rows_total):
    places = jnp.arange(rows_total, dtype=jnp.int32)[:, None]
    return ((places >= N) & (places < N + CONV)).astype(jnp.float32)


def adam_direction(weight, grad, first, second, factor, decay):
    clipped = grad * factor
    first = beta_one * first + (1.0 - beta_one) * clipped
    second = beta_two * second + (1.0 - beta_two) * clipped * clipped
    first_hat = first / (1.0 - beta_one**adam_step)
    second_hat = second / (1.0 - beta_two**adam_step)
    return first_hat / (jnp.sqrt(second_hat) + adam_eps) + decay_rate * decay * weight


def local(
    shards,
    dp,
    tokens,
    lengths,
    cotangent,
    norm_gain,
    input_weight,
    select_weight,
    step_weight,
    channel_params,
    output_weight,
    moment_gain,
    moment_input,
    moment_select,
    moment_step,
    moment_channel,
    moment_output,
    square_gain,
    square_input,
    square_select,
    square_step,
    square_channel,
    square_output,
):
    row_count = tokens.shape[0]
    live_mask, offset = block_layout(lengths[0], row_count)
    restart = (offset == 0).astype(jnp.float32)
    plan = (shards, dp // 2)
    low_conv, low_gate, low_output = (
        own_piece(weight, dp).astype(jnp.bfloat16)
        for weight in (input_weight[:, :DI], input_weight[:, DI:], output_weight)
    )
    low_small = own_piece(jnp.concatenate([select_weight, step_weight], axis=0), dp).astype(jnp.bfloat16)
    width = channel_params.shape[1]
    vectors = jnp.concatenate(
        [channel_params, jnp.pad(norm_gain, (0, width - norm_gain.shape[0]))[None, :]], axis=0
    )
    full_conv, full_small, full_vectors, full_gate, full_output = gather_pieces(
        plan, [low_conv, low_small, own_piece(vectors, dp), low_gate, low_output], "gather_weights", 0
    )
    full_conv, full_gate = full_conv.reshape(-1, DI), full_gate.reshape(-1, DI)
    full_output = full_output.reshape(DI, -1)
    small_rows = R + 2 * N + R
    full_small = from_pieces(full_small, small_rows, width, dp).transpose(1, 0, 2).reshape(small_rows, DI)
    full_select, full_step = full_small[: R + 2 * N], full_small[R + 2 * N :]
    full_vectors = from_pieces(full_vectors, vectors.shape[0], width, dp)
    gain = full_vectors[:, -1, : norm_gain.shape[0]].reshape(-1)
    channel = full_vectors[:, :-1].transpose(1, 0, 2).reshape(-1, DI)
    inputs = tokens.astype(jnp.float32)
    normed_value, norm_pull = jax.vjp(rms_scale, inputs, gain)
    normed = normed_value.astype(jnp.bfloat16)
    conv_input = jnp.dot(normed, full_conv, preferred_element_type=jnp.float32)
    gate_half = jnp.dot(normed, full_gate, preferred_element_type=jnp.float32)
    conv_out = causal_conv(conv_input, channel[N : N + CONV], channel[N + CONV], offset)
    sigmoid = jax.nn.sigmoid(conv_out)
    mixed, conv_slope = lax.optimization_barrier(
        ((conv_out * sigmoid).astype(jnp.bfloat16), sigmoid * (1.0 + conv_out * (1.0 - sigmoid)))
    )
    mixed_values = mixed.astype(jnp.float32)
    selection = contract(mixed, full_select, 1, 1)
    step_low = selection[:, :R].astype(jnp.bfloat16)
    step_in = jnp.dot(step_low, full_step, preferred_element_type=jnp.float32) + channel[N + CONV + 1][None, :]
    rates = -jnp.exp(channel[:N])
    rates_low = (rates * math.log2(math.e)).reshape(N, COLS, LANES)
    kept = [restart] + [(offset >= j).astype(jnp.float32) for j in range(1, CONV)]
    chosen = jnp.concatenate(
        [selection[:, R:], jnp.stack(kept, axis=1), jnp.zeros((row_count, LANES - 2 * N - CONV), jnp.float32)], axis=1
    )
    skip = channel[N + CONV + 2][None, :]
    state_out, step_size, states = scan_forward(step_in, mixed, chosen, rates_low)
    scanned = state_out + skip * mixed_values
    gate_value, gate_pull = jax.vjp(jax.nn.silu, gate_half)
    gated = (scanned * gate_value).astype(jnp.bfloat16)
    branch = jnp.dot(gated, full_output, preferred_element_type=jnp.float32)
    layer_output = (inputs + live_mask[:, None] * branch).astype(jnp.bfloat16)
    upstream = cotangent.astype(jnp.float32)
    grad_branch = (upstream * live_mask[:, None]).astype(jnp.bfloat16)
    grad_output = contract(gated, grad_branch, 0, 0).astype(jnp.bfloat16)
    grad_gated = contract(grad_branch, full_output, 1, 1)
    grad_scanned = grad_gated * gate_value
    (grad_gate,) = gate_pull(grad_gated * scanned)
    grad_conv_input, grad_pre_low, grad_selection, grad_rows, sums = scan_backward(
        step_in,
        step_size,
        mixed,
        grad_scanned,
        conv_input,
        conv_slope,
        chosen,
        rates_low,
        jnp.pad(channel[N:], ((0, 1), (0, 0))),
        full_step,
        full_select,
        states,
    )
    grad_gate = grad_gate.astype(jnp.bfloat16)
    grad_step = contract(step_low, grad_pre_low, 0, 0)
    grad_select = contract(grad_selection, mixed, 0, 0)
    grad_conv_weight, grad_gate_weight = (
        contract(normed, half, 0, 0).astype(jnp.bfloat16)
        for half in (grad_conv_input, grad_gate)
    )
    grad_normed = contract(grad_conv_input, full_conv, 1, 1) + contract(grad_gate, full_gate, 1, 1)
    grad_inputs, grad_gain = norm_pull(grad_normed)
    input_grad = (upstream + grad_inputs).astype(jnp.bfloat16)
    grad_channel = jnp.concatenate(
        [rates * sums.reshape(N, DI), jnp.sum(grad_rows[: CONV + 3], axis=1)], axis=0
    )
    small = jnp.concatenate([grad_select, grad_step, grad_channel], axis=0)
    small = small.reshape(-1, shards, width).transpose(1, 0, 2)
    small_gain = jnp.pad(grad_gain.reshape(shards, 1, -1), ((0, 0), (0, 0), (0, width - grad_gain.shape[0] // shards)))
    small = jnp.concatenate([small, small_gain], axis=1).astype(jnp.bfloat16)
    heights = [norm_gain.shape[0], output_weight.shape[0]]
    sum_output, sum_gate, sum_conv, sum_small = reduce_pieces(
        plan,
        [
            to_pieces(shards, grad_output.reshape(shards, heights[1], -1), dp),
            to_pieces(shards, grad_gate_weight.reshape(shards, heights[0], -1), dp),
            to_pieces(shards, grad_conv_weight.reshape(shards, heights[0], -1), dp),
            to_pieces(shards, small, dp),
        ],
        "sum_gradients",
        1,
    )
    sum_output, sum_gate, sum_conv, sum_small = (
        from_pieces(pieces[None], rows, columns, dp)[0].astype(jnp.float32)
        for pieces, rows, columns in (
            (sum_output, heights[1], output_weight.shape[1]),
            (sum_gate, heights[0], DI),
            (sum_conv, heights[0], DI),
            (sum_small, small.shape[1], width),
        )
    )
    sum_input = jnp.concatenate([sum_conv, sum_gate], axis=1)
    sum_select, sum_step = sum_small[: R + 2 * N], sum_small[R + 2 * N : small_rows]
    sum_channel, sum_gain = sum_small[small_rows:-1], sum_small[-1, : norm_gain.shape[0]]
    grads = (sum_gain, sum_input, sum_select, sum_step, sum_channel, sum_output)
    local_square = sum([jnp.sum(grad * grad) for grad in grads])
    total_square = lax.psum(local_square, "fsdp")
    grad_norm = jnp.sqrt(total_square)
    factor = jnp.minimum(1.0, clip_norm / (grad_norm + 1e-06))
    params = (norm_gain, input_weight, select_weight, step_weight, channel_params, output_weight)
    firsts = (moment_gain, moment_input, moment_select, moment_step, moment_channel, moment_output)
    seconds = (square_gain, square_input, square_select, square_step, square_channel, square_output)
    decays = (0.0, 1.0, 1.0, 1.0, channel_decay(channel_params.shape[0]), 1.0)
    updates = [
        adam_direction(
            params[which], grads[which], firsts[which], seconds[which], factor, decays[which]
        )
        for which in range(6)
    ]
    return (
        layer_output,
        input_grad,
        grad_norm,
        updates[0],
        updates[1],
        updates[2],
        updates[3],
        updates[4],
        updates[5],
        grads[0],
        grads[1],
        grads[2],
        grads[3],
        grads[4],
        grads[5],
    )


def solution(mesh):
    in_specs = (
        P(("dp", "fsdp"), None),
        P(("dp", "fsdp"), None),
        P(("dp", "fsdp"), None),
        P("fsdp"),
        P("fsdp", None),
        P(None, "fsdp"),
        P(None, "fsdp"),
        P(None, "fsdp"),
        P("fsdp", None),
        P("fsdp"),
        P("fsdp", None),
        P(None, "fsdp"),
        P(None, "fsdp"),
        P(None, "fsdp"),
        P("fsdp", None),
        P("fsdp"),
        P("fsdp", None),
        P(None, "fsdp"),
        P(None, "fsdp"),
        P(None, "fsdp"),
        P("fsdp", None),
    )
    out_specs = (
        P(("dp", "fsdp"), None),
        P(("dp", "fsdp"), None),
        P(),
        P("fsdp"),
        P("fsdp", None),
        P(None, "fsdp"),
        P(None, "fsdp"),
        P(None, "fsdp"),
        P("fsdp", None),
        P("fsdp"),
        P("fsdp", None),
        P(None, "fsdp"),
        P(None, "fsdp"),
        P(None, "fsdp"),
        P("fsdp", None),
    )
    shards, dp = mesh.shape["fsdp"], mesh.shape["dp"]
    return jax.shard_map(functools.partial(local, shards, dp), mesh=mesh, in_specs=in_specs, out_specs=out_specs, check_vma=False)
```

```python
import functools
import math

import jax
import jax.numpy as jnp
from jax import lax
from jax.experimental import pallas as pl
from jax.experimental.pallas import tpu as pltpu
from jax.sharding import PartitionSpec as P

DI = 2048
N = 16
R = 64
CONV = 4
LANES = 128
COLS = DI // LANES
HALVES = COLS // 8
BLOCK = 64
GROUP = 8
BACK = 4
WIDE = 512
TAIL = 2

norm_eps = 1e-05
beta_one = 0.9
beta_two = 0.95
adam_eps = 1e-08
decay_rate = 0.1
adam_step = 10.0
clip_norm = 1.0
RESET = 1e30


def block_layout(lengths_row, count):
    places = jnp.arange(count, dtype=jnp.int32)
    begun = jnp.zeros((count,), jnp.int32)
    end = jnp.zeros((), jnp.int32)
    for cluster in range(lengths_row.shape[0]):
        begun = jnp.where(end <= places, jnp.maximum(begun, end), begun)
        end = end + lengths_row[cluster]
    live_mask = (places < end).astype(jnp.float32)
    return live_mask, places - begun

def rms_scale(values, scales):
    return (
        values
        * lax.rsqrt(jnp.mean(values * values, axis=1, keepdims=True) + norm_eps)
        * scales[None, :]
    )


def causal_conv(values, kernel, shift, offset):
    total = shift[None, :] + kernel[CONV - 1][None, :] * values
    for distance in range(1, CONV):
        moved = jnp.pad(values, ((distance, 0), (0, 0)))[:-distance]
        keep = (offset >= distance).astype(jnp.float32)[:, None]
        total = total + kernel[CONV - 1 - distance][None, :] * moved * keep
    return total


def mesh_copy(src, dst, sems, at, device):
    return pltpu.make_async_remote_copy(
        src_ref=src,
        dst_ref=dst,
        send_sem=sems.at[0, at],
        recv_sem=sems.at[1, at],
        device_id=device,
        device_id_type=pl.DeviceIdType.MESH,
    )


def placed(plan):
    group = lax.axis_index("dp")
    return lax.axis_index("fsdp"), group // 2, lax.rem(group, 2)


def peers_of(plan):
    shards, places = plan
    mine, place, side = placed(plan)
    along = [(place * 2 + side, lax.rem(mine + k, shards)) for k in range(1, shards)]
    plane = [((place ^ j) * 2 + side, mine) for j in range(1, places)]
    return along, plane, (place * 2 + 1 - side, mine)


def greet(plan):
    along, plane, pair = peers_of(plan)
    barrier = pltpu.get_barrier_semaphore()
    everyone = along + plane + [pair]
    for device in everyone:
        pl.semaphore_signal(barrier, inc=1, device_id=device, device_id_type=pl.DeviceIdType.MESH)
    pl.semaphore_wait(barrier, len(everyone))


class Gather:
    def __init__(self, plan, own, full, near, far, wide, cross):
        self.plan, self.own, self.full = plan, own, full
        self.near, self.far, self.wide, self.cross = near, far, wide, cross
        self.count = len(own)

    @staticmethod
    def scratch(plan, count):
        shards, places = plan
        return [
            pltpu.SemaphoreType.DMA((count,)),
            pltpu.SemaphoreType.DMA((2, count * (shards - 1))),
            pltpu.SemaphoreType.DMA((2, count * (places - 1))),
            pltpu.SemaphoreType.DMA((2, count)),
        ]

    @staticmethod
    def shapes(plan, pieces):
        return [jax.ShapeDtypeStruct(plan + (2,) + piece.shape, piece.dtype) for piece in pieces]

    def keep(self, s):
        mine, place, side = placed(self.plan)
        return pltpu.make_async_copy(self.own[s], self.full[s].at[mine, place, side], self.near.at[s])

    def along(self, s):
        mine, place, side = placed(self.plan)
        return [
            mesh_copy(
                self.own[s], self.full[s].at[mine, place, side], self.far, s * (self.plan[0] - 1) + k, device
            )
            for k, device in enumerate(peers_of(self.plan)[0])
        ]

    def plane(self, s):
        _, place, side = placed(self.plan)
        part = self.full[s].at[:, place, side]
        return [
            mesh_copy(part, part, self.wide, s * (self.plan[1] - 1) + k, device)
            for k, device in enumerate(peers_of(self.plan)[1])
        ]

    def pair(self, s):
        part = self.full[s].at[:, :, placed(self.plan)[2]]
        return mesh_copy(part, part, self.cross, s, peers_of(self.plan)[2])

    def start(self, s):
        self.keep(s).start()
        for copy in self.along(s):
            copy.start()

    def spread(self, s):
        self.keep(s).wait()
        for copy in self.along(s):
            copy.wait_recv()
        for copy in self.plane(s):
            copy.start()

    def share(self, s):
        for copy in self.plane(s):
            copy.wait_recv()
        self.pair(s).start()

    def end(self, s):
        for copy in self.along(s) + self.plane(s):
            copy.wait_send()
        self.pair(s).wait()


def gather_kernel(plan, count, *refs):
    gather = Gather(plan, refs[:count], refs[count : 2 * count], *refs[2 * count :])
    greet(plan)
    for stage in (gather.start, gather.spread, gather.share, gather.end):
        for s in range(count):
            stage(s)


def gather_pieces(plan, pieces, name, collective_id):
    count = len(pieces)
    return pl.pallas_call(
        functools.partial(gather_kernel, plan, count),
        in_specs=[pl.BlockSpec(memory_space=pl.ANY)] * count,
        out_specs=[pl.BlockSpec(memory_space=pl.ANY)] * count,
        out_shape=Gather.shapes(plan, pieces),
        scratch_shapes=Gather.scratch(plan, count),
        compiler_params=pltpu.CompilerParams(collective_id=collective_id, has_side_effects=True),
        cost_estimate=pl.CostEstimate(flops=0, bytes_accessed=32 << 20, transcendentals=0),
        name=name,
    )(*pieces)


def wide_sum(values):
    total = values[0].astype(jnp.float32)
    for value in values[1:]:
        total = total + value.astype(jnp.float32)
    return total.astype(jnp.bfloat16)


class Reduce:
    def __init__(self, plan, parts, full, scratch):
        count = len(parts)
        self.plan, self.parts, self.full, self.count = plan, parts, full, count
        self.held, self.from_pair, self.from_plane, self.from_along, self.piece = (
            scratch[k * count : (k + 1) * count] for k in range(5)
        )
        self.near, self.cross, self.wide, self.far, self.back, self.over = scratch[5 * count :]

    @staticmethod
    def scratch(plan, parts):
        shards, places = plan
        count = len(parts)
        leads = [(shards, places), (shards, places), (places - 1, shards), (shards - 1,), ()]
        return [pltpu.VMEM(lead + part.shape[3:], jnp.bfloat16) for lead in leads for part in parts] + [
            pltpu.SemaphoreType.DMA((2, count)),
            pltpu.SemaphoreType.DMA((2, count)),
            pltpu.SemaphoreType.DMA((2, count * (places - 1))),
            pltpu.SemaphoreType.DMA((2, count * (shards - 1))),
            pltpu.SemaphoreType.DMA((2, count * (places - 1))),
            pltpu.SemaphoreType.DMA((2, count)),
        ]

    @staticmethod
    def shapes(plan, parts):
        return [jax.ShapeDtypeStruct((plan[1], 2) + part.shape[3:], jnp.bfloat16) for part in parts]

    def keep(self, s):
        side = placed(self.plan)[2]
        return pltpu.make_async_copy(self.parts[s].at[:, :, side], self.held[s], self.near.at[0, s])

    def pair(self, s):
        side = placed(self.plan)[2]
        return mesh_copy(
            self.parts[s].at[:, :, 1 - side], self.from_pair[s], self.cross, s, peers_of(self.plan)[2]
        )

    def plane(self, s):
        place = placed(self.plan)[1]
        return [
            mesh_copy(
                self.held[s].at[:, place ^ (k + 1)],
                self.from_plane[s].at[k],
                self.wide,
                s * (self.plan[1] - 1) + k,
                device,
            )
            for k, device in enumerate(peers_of(self.plan)[1])
        ]

    def along(self, s):
        mine, place, _ = placed(self.plan)
        shards = self.plan[0]
        return [
            mesh_copy(
                self.held[s].at[lax.rem(mine + k + 1, shards), place],
                self.from_along[s].at[k],
                self.far,
                s * (shards - 1) + k,
                device,
            )
            for k, device in enumerate(peers_of(self.plan)[0])
        ]

    def put(self, s):
        _, place, side = placed(self.plan)
        return pltpu.make_async_copy(self.piece[s], self.full[s].at[place, side], self.near.at[1, s])

    def home(self, s):
        _, place, side = placed(self.plan)
        return [
            mesh_copy(self.piece[s], self.full[s].at[place, side], self.back, s * (self.plan[1] - 1) + k, device)
            for k, device in enumerate(peers_of(self.plan)[1])
        ]

    def other(self, s):
        part = self.full[s].at[:, placed(self.plan)[2]]
        return mesh_copy(part, part, self.over, s, peers_of(self.plan)[2])

    def start(self, s):
        self.keep(s).start()
        self.pair(s).start()

    def sum_pair(self, s):
        self.keep(s).wait()
        self.pair(s).wait_recv()
        held, other = self.held[s], self.from_pair[s]

        @pl.loop(0, self.plan[0] * self.plan[1])
        def _(i):
            a, b = i // self.plan[1], lax.rem(i, self.plan[1])
            held[a, b] = wide_sum([held[a, b], other[a, b]])

        for copy in self.plane(s):
            copy.start()

    def sum_plane(self, s):
        place = placed(self.plan)[1]
        for copy in self.plane(s):
            copy.wait_recv()
        held, others = self.held[s], self.from_plane[s]

        @pl.loop(0, self.plan[0])
        def _(i):
            held[i, place] = wide_sum([held[i, place]] + [others[k, i] for k in range(self.plan[1] - 1)])

        for copy in self.along(s):
            copy.start()

    def sum_along(self, s):
        mine, place, _ = placed(self.plan)
        for copy in self.along(s):
            copy.wait_recv()
        others = self.from_along[s]
        self.piece[s][...] = wide_sum([self.held[s][mine, place]] + [others[k] for k in range(self.plan[0] - 1)])
        self.put(s).start()
        for copy in self.home(s):
            copy.start()

    def share(self, s):
        self.put(s).wait()
        for copy in self.home(s):
            copy.wait_recv()
        self.other(s).start()

    def end(self, s):
        self.pair(s).wait_send()
        for copy in self.plane(s) + self.along(s) + self.home(s):
            copy.wait_send()
        self.other(s).wait()


def reduce_kernel(plan, count, *refs):
    reduce = Reduce(plan, refs[:count], refs[count : 2 * count], refs[2 * count :])
    greet(plan)
    stages = (reduce.start, reduce.sum_pair, reduce.sum_plane, reduce.sum_along, reduce.share, reduce.end)
    for stage in stages:
        for s in range(count):
            stage(s)


def reduce_pieces(plan, parts, name, collective_id):
    count = len(parts)
    return pl.pallas_call(
        functools.partial(reduce_kernel, plan, count),
        in_specs=[pl.BlockSpec(memory_space=pl.ANY)] * count,
        out_specs=[pl.BlockSpec(memory_space=pl.ANY)] * count,
        out_shape=Reduce.shapes(plan, parts),
        scratch_shapes=Reduce.scratch(plan, parts),
        compiler_params=pltpu.CompilerParams(
            collective_id=collective_id, has_side_effects=True, vmem_limit_bytes=48 << 20
        ),
        cost_estimate=pl.CostEstimate(flops=0, bytes_accessed=32 << 20, transcendentals=0),
        name=name,
    )(*parts)


def at_steps(stages, count, steps):
    for stage, when in zip(stages, steps):
        for s in range(count):
            pl.when(pl.program_id(0) == when[s])(functools.partial(stage, s))


def cut_of(rows, columns, dp):
    best = None
    across = 1
    while across <= dp and across * LANES <= columns:
        down = dp // across
        tall = -(-rows // (16 * down)) * 16
        if best is None or down * tall < best[0] * best[2]:
            best = (down, across, tall)
        across *= 2
    return best


def to_pieces(shards, array, dp):
    rows, columns = array.shape[1:]
    down, across, tall = cut_of(rows, columns, dp)
    array = jnp.pad(array, ((0, 0), (0, down * tall - rows), (0, 0)))
    array = array.reshape(shards, down, tall, across, columns // across).transpose(0, 1, 3, 2, 4)
    return array.reshape(shards, dp // 2, 2, tall, columns // across)


def from_pieces(pieces, rows, columns, dp):
    shards = pieces.shape[0]
    down, across, tall = cut_of(rows, columns, dp)
    array = pieces.reshape(shards, down, across, tall, columns // across).transpose(0, 1, 3, 2, 4)
    return array.reshape(shards, down * tall, columns)[:, :rows]


def own_piece(array, dp):
    rows, columns = array.shape
    down, across, tall = cut_of(rows, columns, dp)
    array = jnp.pad(array, ((0, down * tall - rows), (0, 0)))
    group = lax.axis_index("dp")
    at = (group // across * tall, lax.rem(group, across) * (columns // across))
    return lax.dynamic_slice(array, at, (tall, columns // across))


def spread(ref, value, g):
    for col in range(COLS):
        ref[pl.ds(g * 8 * COLS + col, 8, stride=COLS), :] = value[:, LANES * col : LANES * (col + 1)]


def unspread(out, ref, g):
    rows = pl.multiple_of(g * 8, 8)
    for col in range(COLS):
        out[pl.ds(rows, 8), LANES * col : LANES * (col + 1)] = ref[pl.ds(g * 8 * COLS + col, 8, stride=COLS), :]


def token_rows(g, token):
    return pl.ds(pl.multiple_of(g * 8 * COLS, 8 * COLS) + token * COLS, COLS)


def prepare(g, sel, step, mixed, dts, us, bb):
    chosen = sel[pl.ds(pl.multiple_of(g * 8, 8), 8), :]
    fresh = chosen[:, 2 * N : 2 * N + 1] > 0.5
    spread(dts, jnp.where(fresh, RESET, step), g)
    spread(us, step * mixed, g)
    for k in range(2 * N):
        bb[g, k] = jnp.broadcast_to(chosen[:, k : k + 1], (8, LANES))


def splat(bb, g, first, count, token):
    return jnp.stack([bb[g, first + n, pl.ds(token, COLS, stride=0), :] for n in range(count)])


def softplus(v):
    small = jnp.exp(-jnp.abs(v))
    series = small * (1.0 - small * (1 / 2 - small * (1 / 3 - small * (1 / 4 - small * (1 / 5)))))
    return jnp.maximum(v, 0.0) + jnp.where(small < 1 / 32, series, jnp.log(1.0 + small))


def forward_kernel(plan, count, v_ref, mixed_ref, sel, rates, *refs):
    own, refs = refs[:count], refs[count:]
    (y_ref, dt_ref, hs_ref), full, refs = refs[:3], refs[3 : 3 + count], refs[3 + count :]
    state, dts, us, bb, ys = refs[:5]
    gather = Gather(plan, own, full, *refs[5:])

    @pl.when(pl.program_id(0) == 0)
    def _():
        state[...] = jnp.zeros_like(state)
        greet(plan)

    at_steps((gather.start, gather.spread, gather.share), count, ((0, 0), (3, 6), (8, 11)))

    @pl.loop(0, BLOCK // 8)
    def _(g):
        rows = pl.ds(pl.multiple_of(g * 8, 8), 8)
        dt_ref[rows, :] = softplus(v_ref[rows, :])

    @pl.loop(0, BLOCK // 16)
    def _(pair):
        mixed = mixed_ref[pl.ds(pl.multiple_of(pair * 16, 16), 16), :].astype(jnp.float32)
        for side in range(2):
            g = pair * 2 + side
            step = dt_ref[pl.ds(pl.multiple_of(g * 8, 8), 8), :]
            prepare(g, sel, step, mixed[8 * side : 8 * side + 8], dts, us, bb)

    for low in range(0, N, GROUP):
        part = pl.ds(low, GROUP)

        def steps(g, kept):
            for token in range(8):
                at = token_rows(g, token)
                decay = jnp.exp2(dts[at, :][None] * rates[part])
                kept = decay * kept + splat(bb, g, low, GROUP, token) * us[at, :][None]
                hs_ref[g * 8 + token, part] = kept
                total = jnp.sum(splat(bb, g, N + low, GROUP, token) * kept, axis=0)
                ys[at, :] = total if low == 0 else ys[at, :] + total
            return kept

        state[part] = lax.fori_loop(0, BLOCK // 8, steps, state[part])

    @pl.loop(0, BLOCK // 8)
    def _(g):
        unspread(y_ref, ys, g)

    at_steps((gather.end,), count, ((11, 11),))


def fold(value):
    return jnp.sum(value.reshape(value.shape[0] // 8, 8, value.shape[1]), axis=0)


def backward_kernel(
    plan, count, v_ref, dt_ref, mixed_ref, gs_ref, sel, rates, vectors,
    step_weight, select_weight, hs_ref, last_ref, conv_ref, slope_ref, flags,
    *refs,
):
    given, refs = refs[:count], refs[count:]
    (grad_conv_in, pre_low, chosen, grad_rows, grad_rates), refs = refs[:5], refs[5:]
    full, refs = refs[:count], refs[count:]
    (carry, dts, us, gss, bb, s1, s2, prods, parts, nat1, nat2, grad_mixed, taps), refs = refs[:13], refs[13:]
    reduce = Reduce(plan, given, full, refs)
    turn = lax.rem(pl.program_id(0), TAIL)
    tall = BLOCK * TAIL
    own = pl.ds(pl.multiple_of((TAIL - 1 - turn) * BLOCK, BLOCK), BLOCK)

    @pl.when(pl.program_id(0) == 0)
    def _():
        for ref in (carry, grad_rates, grad_rows, parts):
            ref[...] = jnp.zeros_like(ref)
        taps[:, tall:, :] = jnp.zeros_like(taps[:, tall:, :])
        greet(plan)

    at_steps(
        (reduce.start, reduce.sum_pair, reduce.sum_plane, reduce.sum_along, reduce.share),
        count,
        ((0, 0), (1, 2), (4, 6), (7, 9), (9, 11)),
    )

    @pl.loop(0, BLOCK // 16)
    def _(pair):
        mixed = mixed_ref[pl.ds(pl.multiple_of(pair * 16, 16), 16), :].astype(jnp.float32)
        for side in range(2):
            g = pair * 2 + side
            rows = pl.ds(pl.multiple_of(g * 8, 8), 8)
            prepare(g, sel, dt_ref[rows, :], mixed[8 * side : 8 * side + 8], dts, us, bb)
            spread(gss, gs_ref[rows, :], g)

    spot = lax.broadcasted_iota(jnp.int32, (8, LANES), 1)
    for low in range(0, N, BACK):
        part = pl.ds(low, BACK)

        def steps(step, carried):
            g = BLOCK // 8 - 1 - step
            kept, total, sums = carried
            for token in reversed(range(8)):
                at = token_rows(g, token)
                dt, u, gs = dts[at, :][None], us[at, :][None], gss[at, :][None]
                if token > 0:
                    before = hs_ref[g * 8 + token - 1, part]
                else:
                    before = jnp.where(g == 0, last_ref[0, part], hs_ref[jnp.maximum(g * 8 - 1, 0), part])
                rate = rates[part]
                adjoint = splat(bb, g, N + low, BACK, token) * gs + kept
                for_c = gs * hs_ref[g * 8 + token, part]
                for_b = adjoint * u
                in_sum = jnp.sum(splat(bb, g, low, BACK, token) * adjoint, axis=0)
                kept = jnp.exp2(dt * rate) * adjoint
                slope = kept * before
                decay_sum = jnp.sum(rate * slope, axis=0)
                total = total + dt * slope
                for kind, value in enumerate((for_b, for_c)):
                    prods[token % 2, pl.ds(8 * BACK * kind, 8 * BACK), :] = (value[:, :8] + value[:, 8:]).reshape(8 * BACK, LANES)
                here = spot == g * 8 + token
                new = []
                for first in range(0, 2 * BACK, 8):
                    rows_of = [prods[token % 2, pl.ds(8 * first + s, 8, stride=8), :] for s in range(8)]
                    while len(rows_of) > 1:
                        rows_of = [a + b for a, b in zip(rows_of[::2], rows_of[1::2])]
                    new.append(jnp.where(here, jnp.sum(rows_of[0], axis=1, keepdims=True), sums[first // 8]))
                sums = tuple(new)
                s1[at, :] = in_sum if low == 0 else s1[at, :] + in_sum
                s2[at, :] = decay_sum if low == 0 else s2[at, :] + decay_sum
            return kept, total, sums

        nothing = tuple(jnp.zeros((8, LANES), jnp.float32) for _ in range(2 * BACK // 8))
        carry[part], grad_rates[part], sums = lax.fori_loop(
            0, BLOCK // 8, steps, (carry[part], grad_rates[part], nothing)
        )
        sums = jnp.concatenate(sums, axis=0)
        parts[pl.ds(low, BACK), :] = sums[:BACK]
        parts[pl.ds(N + low, BACK), :] = sums[BACK:]

    @pl.loop(0, BLOCK // 8)
    def _(g):
        unspread(nat1, s1, g)
        unspread(nat2, s2, g)

    @pl.loop(0, DI // WIDE)
    def _(c):
        lanes = pl.ds(pl.multiple_of(c * WIDE, WIDE), WIDE)
        mixed = mixed_ref[:, lanes].astype(jnp.float32)
        step, gs, in_sum = dt_ref[:, lanes], gs_ref[:, lanes], nat1[:, lanes]
        pre = (mixed * in_sum + math.log(2.0) * nat2[:, lanes]) * jnp.exp(v_ref[:, lanes] - step)
        pre_low[own, lanes] = pre.astype(jnp.bfloat16)
        grad_mixed[own, lanes] = step * in_sum + vectors[CONV + 2 : CONV + 3, lanes] * gs
        grad_rows[CONV + 1, :, lanes] += fold(pre)
        grad_rows[CONV + 2, :, lanes] += fold(gs * mixed)

    chosen[own, R:] = parts[...].T[:BLOCK, : 2 * N].astype(jnp.bfloat16)

    @pl.when(turn == TAIL - 1)
    def _():
        chosen[:, :R] = dot(pre_low[...], step_weight[...], 1, 1).astype(jnp.bfloat16)

        @pl.loop(0, DI // WIDE)
        def _(c):
            lanes = pl.ds(pl.multiple_of(c * WIDE, WIDE), WIDE)
            total = grad_mixed[:, lanes] + dot(chosen[...], select_weight[:, lanes], 1, 0)
            grad_conv = total * slope_ref[:, lanes]
            value = conv_ref[:, lanes]
            grad_rows[CONV, :, lanes] += fold(grad_conv)
            result = vectors[CONV - 1 : CONV, lanes] * grad_conv
            grad_rows[CONV - 1, :, lanes] += fold(grad_conv * value)
            for j in range(1, CONV):
                taps[j - 1, :tall, lanes] = grad_conv * flags[:, 2 * N + j : 2 * N + j + 1]
                later = taps[j - 1, :, lanes][j : j + tall]
                grad_rows[CONV - 1 - j, :, lanes] += fold(later * value)
                result = result + vectors[CONV - 1 - j : CONV - j, lanes] * later
                taps[j - 1, tall:, lanes] = taps[j - 1, :8, lanes]
            grad_conv_in[:, lanes] = result.astype(jnp.bfloat16)

    at_steps((reduce.end,), count, ((11, 11),))


def dot(left, right, left_dim, right_dim):
    return lax.dot_general(
        left, right, (((left_dim,), (right_dim,)), ((), ())), preferred_element_type=jnp.float32
    )


def scan_forward(v, mixed, sel, rates, plan, pieces):
    count = v.shape[0]
    anywhere = [pl.BlockSpec(memory_space=pl.ANY)] * len(pieces)
    rows = pl.BlockSpec((BLOCK, DI), lambda i: (i, 0))
    return pl.pallas_call(
        functools.partial(forward_kernel, plan, len(pieces)),
        grid=(count // BLOCK,),
        in_specs=[
            rows,
            rows,
            pl.BlockSpec((BLOCK, LANES), lambda i: (i, 0)),
            pl.BlockSpec((N, COLS, LANES), lambda i: (0, 0, 0)),
        ]
        + anywhere,
        out_specs=[rows, rows, pl.BlockSpec((BLOCK, N, COLS, LANES), lambda i: (i, 0, 0, 0))] + anywhere,
        out_shape=[
            jax.ShapeDtypeStruct((count, DI), jnp.float32),
            jax.ShapeDtypeStruct((count, DI), jnp.float32),
            jax.ShapeDtypeStruct((count, N, COLS, LANES), jnp.float32),
        ]
        + Gather.shapes(plan, pieces),
        scratch_shapes=[
            pltpu.VMEM((N, COLS, LANES), jnp.float32),
            pltpu.VMEM((BLOCK * COLS, LANES), jnp.float32),
            pltpu.VMEM((BLOCK * COLS, LANES), jnp.float32),
            pltpu.VMEM((BLOCK // 8, 2 * N, 8, LANES), jnp.float32),
            pltpu.VMEM((BLOCK * COLS, LANES), jnp.float32),
        ]
        + Gather.scratch(plan, len(pieces)),
        compiler_params=pltpu.CompilerParams(
            vmem_limit_bytes=48 << 20, collective_id=2, has_side_effects=True
        ),
        cost_estimate=pl.CostEstimate(
            flops=6 * count * N * DI, bytes_accessed=4 * count * N * DI, transcendentals=count * N * DI
        ),
        name="scan_forward",
    )(v, mixed, sel, rates, *pieces)


def scan_backward(v, dt, mixed, gs, conv_input, slope, sel, rates, vectors, step_weight, select_weight, states, plan, summed):
    count = dt.shape[0]
    blocks = count // BLOCK
    anywhere = [pl.BlockSpec(memory_space=pl.ANY)] * len(summed)
    rows = pl.BlockSpec((BLOCK, DI), lambda i: (blocks - 1 - i, 0))

    def tall(width):
        return pl.BlockSpec((BLOCK * TAIL, width), lambda i: (blocks // TAIL - 1 - i // TAIL, 0))

    def whole(*shape):
        return pl.BlockSpec(shape, lambda i: (0,) * len(shape))

    state = (N, COLS, LANES)
    return pl.pallas_call(
        functools.partial(backward_kernel, plan, len(summed)),
        grid=(blocks,),
        in_specs=[
            rows,
            rows,
            rows,
            rows,
            pl.BlockSpec((BLOCK, LANES), lambda i: (blocks - 1 - i, 0)),
            whole(*state),
            whole(8, DI),
            whole(R, DI),
            whole(R + 2 * N, DI),
            pl.BlockSpec((BLOCK,) + state, lambda i: (blocks - 1 - i, 0, 0, 0)),
            pl.BlockSpec((1,) + state, lambda i: (jnp.maximum((blocks - 1 - i) * BLOCK - 1, 0), 0, 0, 0)),
            tall(DI),
            tall(DI),
            tall(LANES),
        ]
        + anywhere,
        out_specs=[tall(DI), tall(DI), tall(R + 2 * N), whole(8, 8, DI), whole(*state)] + anywhere,
        out_shape=[
            jax.ShapeDtypeStruct((count, DI), jnp.bfloat16),
            jax.ShapeDtypeStruct((count, DI), jnp.bfloat16),
            jax.ShapeDtypeStruct((count, R + 2 * N), jnp.bfloat16),
            jax.ShapeDtypeStruct((8, 8, DI), jnp.float32),
            jax.ShapeDtypeStruct(state, jnp.float32),
        ]
        + Reduce.shapes(plan, summed),
        scratch_shapes=[pltpu.VMEM(state, jnp.float32)]
        + [pltpu.VMEM((BLOCK * COLS, LANES), jnp.float32)] * 3
        + [pltpu.VMEM((BLOCK // 8, 2 * N, 8, LANES), jnp.float32)]
        + [pltpu.VMEM((BLOCK * COLS, LANES), jnp.float32)] * 2
        + [pltpu.VMEM((2, 16 * BACK, LANES), jnp.float32)]
        + [pltpu.VMEM((LANES, LANES), jnp.float32)]
        + [pltpu.VMEM((BLOCK, DI), jnp.float32)] * 2
        + [pltpu.VMEM((BLOCK * TAIL, DI), jnp.float32)]
        + [pltpu.VMEM((CONV - 1, BLOCK * TAIL + 8, DI), jnp.float32)]
        + Reduce.scratch(plan, summed),
        compiler_params=pltpu.CompilerParams(
            vmem_limit_bytes=60 << 20, collective_id=3, has_side_effects=True
        ),
        cost_estimate=pl.CostEstimate(
            flops=20 * count * N * DI, bytes_accessed=4 * count * N * DI, transcendentals=count * N * DI
        ),
        name="scan_backward",
    )(
        v, dt, mixed, gs, sel, rates, vectors, step_weight, select_weight,
        states, states, conv_input, slope, sel, *summed,
    )


def contract(left, right, left_dim, right_dim):
    return lax.dot_general(
        left, right, (((left_dim,), (right_dim,)), ((), ())), preferred_element_type=jnp.float32
    )


def channel_decay(rows_total):
    places = jnp.arange(rows_total, dtype=jnp.int32)[:, None]
    return ((places >= N) & (places < N + CONV)).astype(jnp.float32)


def adam_direction(weight, grad, first, second, factor, decay):
    clipped = grad * factor
    first = beta_one * first + (1.0 - beta_one) * clipped
    second = beta_two * second + (1.0 - beta_two) * clipped * clipped
    first_hat = first / (1.0 - beta_one**adam_step)
    second_hat = second / (1.0 - beta_two**adam_step)
    return first_hat / (jnp.sqrt(second_hat) + adam_eps) + decay_rate * decay * weight


def local(
    shards,
    dp,
    tokens,
    lengths,
    cotangent,
    norm_gain,
    input_weight,
    select_weight,
    step_weight,
    channel_params,
    output_weight,
    moment_gain,
    moment_input,
    moment_select,
    moment_step,
    moment_channel,
    moment_output,
    square_gain,
    square_input,
    square_select,
    square_step,
    square_channel,
    square_output,
):
    row_count = tokens.shape[0]
    live_mask, offset = block_layout(lengths[0], row_count)
    restart = (offset == 0).astype(jnp.float32)
    plan = (shards, dp // 2)
    low_conv, low_gate, low_output = (
        own_piece(weight, dp).astype(jnp.bfloat16)
        for weight in (input_weight[:, :DI], input_weight[:, DI:], output_weight)
    )
    low_small = own_piece(jnp.concatenate([select_weight, step_weight], axis=0), dp).astype(jnp.bfloat16)
    width = channel_params.shape[1]
    vectors = jnp.concatenate(
        [channel_params, jnp.pad(norm_gain, (0, width - norm_gain.shape[0]))[None, :]], axis=0
    )
    full_conv, full_small, full_vectors = gather_pieces(
        plan, [low_conv, low_small, own_piece(vectors, dp)], "gather_weights", 0
    )
    full_conv = from_pieces(full_conv, norm_gain.shape[0], DI, dp).reshape(-1, DI)
    small_rows = R + 2 * N + R
    full_small = from_pieces(full_small, small_rows, width, dp).transpose(1, 0, 2).reshape(small_rows, DI)
    full_select, full_step = full_small[: R + 2 * N], full_small[R + 2 * N :]
    full_vectors = from_pieces(full_vectors, vectors.shape[0], width, dp)
    gain = full_vectors[:, -1, : norm_gain.shape[0]].reshape(-1)
    channel = full_vectors[:, :-1].transpose(1, 0, 2).reshape(-1, DI)
    inputs = tokens.astype(jnp.float32)
    normed_value, norm_pull = jax.vjp(rms_scale, inputs, gain)
    normed = normed_value.astype(jnp.bfloat16)
    conv_input = jnp.dot(normed, full_conv, preferred_element_type=jnp.float32)
    conv_out = causal_conv(conv_input, channel[N : N + CONV], channel[N + CONV], offset)
    sigmoid = jax.nn.sigmoid(conv_out)
    mixed, conv_slope = lax.optimization_barrier(
        ((conv_out * sigmoid).astype(jnp.bfloat16), sigmoid * (1.0 + conv_out * (1.0 - sigmoid)))
    )
    mixed_values = mixed.astype(jnp.float32)
    selection = contract(mixed, full_select, 1, 1)
    step_low = selection[:, :R].astype(jnp.bfloat16)
    step_in = jnp.dot(step_low, full_step, preferred_element_type=jnp.float32) + channel[N + CONV + 1][None, :]
    rates = -jnp.exp(channel[:N])
    rates_low = (rates * math.log2(math.e)).reshape(N, COLS, LANES)
    kept = [restart] + [(offset >= j).astype(jnp.float32) for j in range(1, CONV)]
    chosen = jnp.concatenate(
        [selection[:, R:], jnp.stack(kept, axis=1), jnp.zeros((row_count, LANES - 2 * N - CONV), jnp.float32)], axis=1
    )
    skip = channel[N + CONV + 2][None, :]
    state_out, step_size, states, full_gate, full_output = scan_forward(
        step_in, mixed, chosen, rates_low, plan, [low_gate, low_output]
    )
    full_gate = from_pieces(full_gate, norm_gain.shape[0], DI, dp).reshape(-1, DI)
    full_output = from_pieces(full_output, output_weight.shape[0], output_weight.shape[1], dp).reshape(DI, -1)
    gate_half = jnp.dot(normed, full_gate, preferred_element_type=jnp.float32)
    scanned = state_out + skip * mixed_values
    gate_value, gate_pull = jax.vjp(jax.nn.silu, gate_half)
    gated = (scanned * gate_value).astype(jnp.bfloat16)
    branch = jnp.dot(gated, full_output, preferred_element_type=jnp.float32)
    layer_output = (inputs + live_mask[:, None] * branch).astype(jnp.bfloat16)
    upstream = cotangent.astype(jnp.float32)
    grad_branch = (upstream * live_mask[:, None]).astype(jnp.bfloat16)
    grad_output = contract(gated, grad_branch, 0, 0).astype(jnp.bfloat16)
    grad_gated = contract(grad_branch, full_output, 1, 1)
    grad_scanned = grad_gated * gate_value
    (grad_gate,) = gate_pull(grad_gated * scanned)
    grad_gate = grad_gate.astype(jnp.bfloat16)
    grad_gate_weight = contract(normed, grad_gate, 0, 0).astype(jnp.bfloat16)
    heights = [norm_gain.shape[0], output_weight.shape[0]]
    grad_conv_input, grad_pre_low, grad_selection, grad_rows, sums, sum_output, sum_gate = scan_backward(
        step_in,
        step_size,
        mixed,
        grad_scanned,
        conv_input,
        conv_slope,
        chosen,
        rates_low,
        jnp.pad(channel[N:], ((0, 1), (0, 0))),
        full_step,
        full_select,
        states,
        plan,
        [
            to_pieces(shards, grad_output.reshape(shards, heights[1], -1), dp),
            to_pieces(shards, grad_gate_weight.reshape(shards, heights[0], -1), dp),
        ],
    )
    grad_step = contract(step_low, grad_pre_low, 0, 0)
    grad_select = contract(grad_selection, mixed, 0, 0)
    grad_conv_weight = contract(normed, grad_conv_input, 0, 0).astype(jnp.bfloat16)
    grad_normed = contract(grad_conv_input, full_conv, 1, 1) + contract(grad_gate, full_gate, 1, 1)
    grad_inputs, grad_gain = norm_pull(grad_normed)
    input_grad = (upstream + grad_inputs).astype(jnp.bfloat16)
    grad_channel = jnp.concatenate(
        [rates * sums.reshape(N, DI), jnp.sum(grad_rows[: CONV + 3], axis=1)], axis=0
    )
    small = jnp.concatenate([grad_select, grad_step, grad_channel], axis=0)
    small = small.reshape(-1, shards, width).transpose(1, 0, 2)
    small_gain = jnp.pad(grad_gain.reshape(shards, 1, -1), ((0, 0), (0, 0), (0, width - grad_gain.shape[0] // shards)))
    small = jnp.concatenate([small, small_gain], axis=1).astype(jnp.bfloat16)
    sum_conv, sum_small = reduce_pieces(
        plan,
        [
            to_pieces(shards, grad_conv_weight.reshape(shards, heights[0], -1), dp),
            to_pieces(shards, small, dp),
        ],
        "sum_gradients",
        1,
    )
    sum_output, sum_gate, sum_conv, sum_small = (
        from_pieces(pieces[None], rows, columns, dp)[0].astype(jnp.float32)
        for pieces, rows, columns in (
            (sum_output, heights[1], output_weight.shape[1]),
            (sum_gate, heights[0], DI),
            (sum_conv, heights[0], DI),
            (sum_small, small.shape[1], width),
        )
    )
    sum_input = jnp.concatenate([sum_conv, sum_gate], axis=1)
    sum_select, sum_step = sum_small[: R + 2 * N], sum_small[R + 2 * N : small_rows]
    sum_channel, sum_gain = sum_small[small_rows:-1], sum_small[-1, : norm_gain.shape[0]]
    grads = (sum_gain, sum_input, sum_select, sum_step, sum_channel, sum_output)
    local_square = sum([jnp.sum(grad * grad) for grad in grads])
    total_square = lax.psum(local_square, "fsdp")
    grad_norm = jnp.sqrt(total_square)
    factor = jnp.minimum(1.0, clip_norm / (grad_norm + 1e-06))
    params = (norm_gain, input_weight, select_weight, step_weight, channel_params, output_weight)
    firsts = (moment_gain, moment_input, moment_select, moment_step, moment_channel, moment_output)
    seconds = (square_gain, square_input, square_select, square_step, square_channel, square_output)
    decays = (0.0, 1.0, 1.0, 1.0, channel_decay(channel_params.shape[0]), 1.0)
    updates = [
        adam_direction(
            params[which], grads[which], firsts[which], seconds[which], factor, decays[which]
        )
        for which in range(6)
    ]
    return (
        layer_output,
        input_grad,
        grad_norm,
        updates[0],
        updates[1],
        updates[2],
        updates[3],
        updates[4],
        updates[5],
        grads[0],
        grads[1],
        grads[2],
        grads[3],
        grads[4],
        grads[5],
    )


def solution(mesh):
    in_specs = (
        P(("dp", "fsdp"), None),
        P(("dp", "fsdp"), None),
        P(("dp", "fsdp"), None),
        P("fsdp"),
        P("fsdp", None),
        P(None, "fsdp"),
        P(None, "fsdp"),
        P(None, "fsdp"),
        P("fsdp", None),
        P("fsdp"),
        P("fsdp", None),
        P(None, "fsdp"),
        P(None, "fsdp"),
        P(None, "fsdp"),
        P("fsdp", None),
        P("fsdp"),
        P("fsdp", None),
        P(None, "fsdp"),
        P(None, "fsdp"),
        P(None, "fsdp"),
        P("fsdp", None),
    )
    out_specs = (
        P(("dp", "fsdp"), None),
        P(("dp", "fsdp"), None),
        P(),
        P("fsdp"),
        P("fsdp", None),
        P(None, "fsdp"),
        P(None, "fsdp"),
        P(None, "fsdp"),
        P("fsdp", None),
        P("fsdp"),
        P("fsdp", None),
        P(None, "fsdp"),
        P(None, "fsdp"),
        P(None, "fsdp"),
        P("fsdp", None),
    )
    shards, dp = mesh.shape["fsdp"], mesh.shape["dp"]
    return jax.shard_map(functools.partial(local, shards, dp), mesh=mesh, in_specs=in_specs, out_specs=out_specs, check_vma=False)
```

```python
import functools
import math

import jax
import jax.numpy as jnp
from jax import lax
from jax.experimental import pallas as pl
from jax.experimental.pallas import tpu as pltpu
from jax.sharding import PartitionSpec as P

DI = 2048
N = 16
R = 64
CONV = 4
LANES = 128
COLS = DI // LANES
HALVES = COLS // 8
BLOCK = 64
GROUP = 8
BACK = 4
GATHER_CUTS = (2, 2)
REDUCE_CUTS = (2, 2)
WIDE = 512
TAIL = 2

norm_eps = 1e-05
beta_one = 0.9
beta_two = 0.95
adam_eps = 1e-08
decay_rate = 0.1
adam_step = 10.0
clip_norm = 1.0
RESET = 1e30


def block_layout(lengths_row, count):
    places = lax.broadcasted_iota(jnp.int32, (count, LANES), 0)
    begun = jnp.zeros((count, LANES), jnp.int32)
    end = jnp.zeros((), jnp.int32)
    for cluster in range(lengths_row.shape[0]):
        begun = jnp.where(end <= places, jnp.maximum(begun, end), begun)
        end = end + lengths_row[cluster]
    return (places[:, :1] < end).astype(jnp.float32), places - begun


def rms_scale(values, scales):
    return (
        values
        * lax.rsqrt(jnp.mean(values * values, axis=1, keepdims=True) + norm_eps)
        * scales[None, :]
    )


def causal_conv(values, kernel, shift, offset):
    total = shift[None, :] + kernel[CONV - 1][None, :] * values
    for distance in range(1, CONV):
        moved = jnp.pad(values, ((distance, 0), (0, 0)))[:-distance]
        keep = (offset[:, :1] >= distance).astype(jnp.float32)
        total = total + kernel[CONV - 1 - distance][None, :] * moved * keep
    return total


def mesh_copy(src, dst, sems, at, device):
    return pltpu.make_async_remote_copy(
        src_ref=src,
        dst_ref=dst,
        send_sem=sems.at[0, at],
        recv_sem=sems.at[1, at],
        device_id=device,
        device_id_type=pl.DeviceIdType.MESH,
    )


def placed(plan):
    group = lax.axis_index("dp")
    return lax.axis_index("fsdp"), group // 2, lax.rem(group, 2)


def peers_of(plan):
    shards, places = plan
    mine, place, side = placed(plan)
    along = [(place * 2 + side, lax.rem(mine + k, shards)) for k in range(1, shards)]
    plane = [((place ^ j) * 2 + side, mine) for j in range(1, places)]
    return along, plane, (place * 2 + 1 - side, mine)


def greet(plan):
    along, plane, pair = peers_of(plan)
    barrier = pltpu.get_barrier_semaphore()
    everyone = along + plane + [pair]
    for device in everyone:
        pl.semaphore_signal(barrier, inc=1, device_id=device, device_id_type=pl.DeviceIdType.MESH)
    pl.semaphore_wait(barrier, len(everyone))


def chunks(arrays, cuts):
    made = []
    for i, (array, cut) in enumerate(zip(arrays, cuts)):
        width = array.shape[-1] // cut
        made += [(i, pl.ds(k * width, width)) for k in range(cut)]
    return made


class Gather:
    def __init__(self, plan, cuts, own, full, near, far, wide, cross):
        self.plan, self.all_own, self.all_full = plan, own, full
        self.near, self.far, self.wide, self.cross = near, far, wide, cross
        self.chunks = chunks(own, cuts)
        self.count = len(self.chunks)

    def own(self, s):
        i, columns = self.chunks[s]
        return self.all_own[i].at[:, columns]

    def full(self, s, *at):
        i, columns = self.chunks[s]
        return self.all_full[i].at[(*at, slice(None), columns)]

    @staticmethod
    def scratch(plan, count):
        shards, places = plan
        return [
            pltpu.SemaphoreType.DMA((count,)),
            pltpu.SemaphoreType.DMA((2, count * (shards - 1))),
            pltpu.SemaphoreType.DMA((2, count * places)),
            pltpu.SemaphoreType.DMA((2, count)),
        ]

    @staticmethod
    def shapes(plan, pieces):
        return [jax.ShapeDtypeStruct(plan + (2,) + piece.shape, piece.dtype) for piece in pieces]

    def keep(self, s):
        mine, place, side = placed(self.plan)
        return pltpu.make_async_copy(self.own(s), self.full(s, mine, place, side), self.near.at[s])

    def along(self, s):
        mine, place, side = placed(self.plan)
        return [
            mesh_copy(self.own(s), self.full(s, mine, place, side), self.far, s * (self.plan[0] - 1) + k, device)
            for k, device in enumerate(peers_of(self.plan)[0])
        ]

    def plane(self, s):
        _, place, side = placed(self.plan)
        part = self.full(s, slice(None), place, side)
        devices = peers_of(self.plan)[1]
        return [
            mesh_copy(part, part, self.wide, s * self.plan[1] + k, device)
            for k, device in enumerate(devices[:2] if self.plan[1] == 4 else devices)
        ]

    def relay(self, s):
        if self.plan[1] != 4:
            return []
        _, place, side = placed(self.plan)
        devices = peers_of(self.plan)[1]
        half = self.plan[0] // 2
        made = []
        for k, rows in enumerate((pl.ds(0, half), pl.ds(half, self.plan[0] - half))):
            part = self.full(s, rows, place ^ (k + 1), side)
            made.append(mesh_copy(part, part, self.wide, s * 4 + 2 + k, devices[1 - k]))
        return made

    def pair(self, s):
        part = self.full(s, slice(None), slice(None), placed(self.plan)[2])
        return mesh_copy(part, part, self.cross, s, peers_of(self.plan)[2])

    def start(self, s):
        self.keep(s).start()
        for copy in self.along(s):
            copy.start()

    def spread(self, s):
        self.keep(s).wait()
        for copy in self.along(s):
            copy.wait_recv()
        for copy in self.plane(s):
            copy.start()

    def pass_on(self, s):
        for copy in self.plane(s):
            copy.wait_recv()
        for copy in self.relay(s):
            copy.start()

    def share(self, s):
        for copy in self.relay(s):
            copy.wait_recv()
        self.pair(s).start()

    def end(self, s):
        for copy in self.along(s) + self.plane(s) + self.relay(s):
            copy.wait_send()
        self.pair(s).wait()


def gather_kernel(plan, cuts, count, *refs):
    gather = Gather(plan, cuts, refs[:count], refs[count : 2 * count], *refs[2 * count :])
    greet(plan)
    ahead = 2
    for s in range(gather.count + 4):
        for stage, wait in ((gather.start, 0), (gather.spread, ahead), (gather.pass_on, 3), (gather.share, 4)):
            if 0 <= s - wait < gather.count:
                stage(s - wait)
    for s in range(gather.count):
        gather.end(s)


def gather_pieces(plan, pieces, cuts, name, collective_id):
    count = len(pieces)
    return pl.pallas_call(
        functools.partial(gather_kernel, plan, cuts, count),
        in_specs=[pl.BlockSpec(memory_space=pl.ANY)] * count,
        out_specs=[pl.BlockSpec(memory_space=pl.ANY)] * count,
        out_shape=Gather.shapes(plan, pieces),
        scratch_shapes=Gather.scratch(plan, sum(cuts)),
        compiler_params=pltpu.CompilerParams(collective_id=collective_id, has_side_effects=True),
        cost_estimate=pl.CostEstimate(flops=0, bytes_accessed=32 << 20, transcendentals=0),
        name=name,
    )(*pieces)


def wide_sum(values):
    total = values[0].astype(jnp.float32)
    for value in values[1:]:
        total = total + value.astype(jnp.float32)
    return total.astype(jnp.bfloat16)


class Reduce:
    def __init__(self, plan, cuts, parts, full, squares, scratch):
        count = sum(cuts)
        self.squares = squares
        self.plan, self.all_parts, self.all_full, self.count = plan, parts, full, count
        self.chunks = chunks(parts, cuts)
        self.held, self.from_pair, self.from_plane, self.from_along, self.piece = (
            scratch[k * count : (k + 1) * count] for k in range(5)
        )
        self.near, self.cross, self.wide, self.far, self.back, self.over = scratch[5 * count :]

    def parts(self, s, *at):
        i, columns = self.chunks[s]
        return self.all_parts[i].at[(*at, slice(None), columns)]

    def full(self, s, *at):
        i, columns = self.chunks[s]
        return self.all_full[i].at[(*at, slice(None), columns)]

    @staticmethod
    def scratch(plan, cuts, parts):
        shards, places = plan
        count = sum(cuts)
        tails = [(part.shape[3], part.shape[4] // cut) for part, cut in zip(parts, cuts) for _ in range(cut)]
        leads = [(shards, places), (shards, places), (places - 1, shards), (shards - 1,), ()]
        return [pltpu.VMEM(lead + tail, jnp.bfloat16) for lead in leads for tail in tails] + [
            pltpu.SemaphoreType.DMA((2, count)),
            pltpu.SemaphoreType.DMA((2, count)),
            pltpu.SemaphoreType.DMA((2, count * (places - 1))),
            pltpu.SemaphoreType.DMA((2, count * (shards - 1))),
            pltpu.SemaphoreType.DMA((2, count * (places - 1))),
            pltpu.SemaphoreType.DMA((2, count)),
        ]

    @staticmethod
    def shapes(plan, parts):
        return [jax.ShapeDtypeStruct((plan[1], 2) + part.shape[3:], jnp.bfloat16) for part in parts]

    def keep(self, s):
        side = placed(self.plan)[2]
        return pltpu.make_async_copy(self.parts(s, slice(None), slice(None), side), self.held[s], self.near.at[0, s])

    def pair(self, s):
        side = placed(self.plan)[2]
        return mesh_copy(
            self.parts(s, slice(None), slice(None), 1 - side), self.from_pair[s], self.cross, s, peers_of(self.plan)[2]
        )

    def plane(self, s):
        place = placed(self.plan)[1]
        return [
            mesh_copy(
                self.held[s].at[:, place ^ (k + 1)],
                self.from_plane[s].at[k],
                self.wide,
                s * (self.plan[1] - 1) + k,
                device,
            )
            for k, device in enumerate(peers_of(self.plan)[1])
        ]

    def along(self, s):
        mine, place, _ = placed(self.plan)
        shards = self.plan[0]
        return [
            mesh_copy(
                self.held[s].at[lax.rem(mine + k + 1, shards), place],
                self.from_along[s].at[k],
                self.far,
                s * (shards - 1) + k,
                device,
            )
            for k, device in enumerate(peers_of(self.plan)[0])
        ]

    def put(self, s):
        _, place, side = placed(self.plan)
        return pltpu.make_async_copy(self.piece[s], self.full(s, place, side), self.near.at[1, s])

    def home(self, s):
        _, place, side = placed(self.plan)
        return [
            mesh_copy(self.piece[s], self.full(s, place, side), self.back, s * (self.plan[1] - 1) + k, device)
            for k, device in enumerate(peers_of(self.plan)[1])
        ]

    def other(self, s):
        part = self.full(s, slice(None), placed(self.plan)[2])
        return mesh_copy(part, part, self.over, s, peers_of(self.plan)[2])

    def start(self, s):
        self.keep(s).start()
        self.pair(s).start()

    def sum_pair(self, s):
        self.keep(s).wait()
        self.pair(s).wait_recv()
        held, other = self.held[s], self.from_pair[s]

        @pl.loop(0, self.plan[0] * self.plan[1])
        def _(i):
            a, b = i // self.plan[1], lax.rem(i, self.plan[1])
            held[a, b] = wide_sum([held[a, b], other[a, b]])

        for copy in self.plane(s):
            copy.start()

    def sum_plane(self, s):
        place = placed(self.plan)[1]
        for copy in self.plane(s):
            copy.wait_recv()
        held, others = self.held[s], self.from_plane[s]

        @pl.loop(0, self.plan[0])
        def _(i):
            held[i, place] = wide_sum([held[i, place]] + [others[k, i] for k in range(self.plan[1] - 1)])

        for copy in self.along(s):
            copy.start()

    def sum_along(self, s):
        mine, place, _ = placed(self.plan)
        for copy in self.along(s):
            copy.wait_recv()
        others = self.from_along[s]
        piece = wide_sum([self.held[s][mine, place]] + [others[k] for k in range(self.plan[0] - 1)])
        self.piece[s][...] = piece
        square = piece.astype(jnp.float32) * piece.astype(jnp.float32)
        square = jnp.sum(square.reshape(-1, 8, square.shape[1]), axis=0)
        for first in range(0, square.shape[1], LANES):
            self.squares[...] += square[:, first : first + LANES]
        self.put(s).start()
        for copy in self.home(s):
            copy.start()

    def share(self, s):
        self.put(s).wait()
        for copy in self.home(s):
            copy.wait_recv()
        self.other(s).start()

    def end(self, s):
        self.pair(s).wait_send()
        for copy in self.plane(s) + self.along(s) + self.home(s):
            copy.wait_send()
        self.other(s).wait()


class Total:
    def __init__(self, plan, value, scratch):
        self.plan, self.value = plan, value
        self.slots, self.sent, self.sems = scratch[:3], scratch[3], scratch[4:]

    @staticmethod
    def scratch(plan):
        sizes = (plan[0], plan[1], 2)
        return (
            [pltpu.VMEM((size, 8, LANES), jnp.float32) for size in sizes]
            + [pltpu.VMEM((3, 8, LANES), jnp.float32)]
            + [pltpu.SemaphoreType.DMA((2, size - 1)) for size in sizes]
        )

    def copies(self, level):
        along, plane, pair = peers_of(self.plan)
        at = placed(self.plan)[level]
        return [
            mesh_copy(self.sent.at[level], self.slots[level].at[at], self.sems[level], k, device)
            for k, device in enumerate((along, plane, [pair])[level])
        ]

    def start(self, level):
        self.sent[level] = self.value[...]
        self.slots[level][placed(self.plan)[level]] = self.value[...]
        for copy in self.copies(level):
            copy.start()

    def end(self, level):
        for copy in self.copies(level):
            copy.wait()
        total = self.slots[level][0]
        for k in range(1, self.slots[level].shape[0]):
            total = total + self.slots[level][k]
        self.value[...] = total


def reduce_kernel(plan, cuts, count, *refs):
    given, refs = refs[:count], refs[count:]
    before, refs = refs[0], refs[1:]
    full, squares, refs = refs[:count], refs[count], refs[count + 1 :]
    reduce = Reduce(plan, cuts, given, full, squares, refs[:-7])
    total = Total(plan, squares, refs[-7:])
    squares[...] = before[...]
    greet(plan)
    for stage in (reduce.start, reduce.sum_pair, reduce.sum_plane, reduce.sum_along):
        for s in range(reduce.count):
            stage(s)
    total.start(0)
    total.end(0)
    total.start(1)
    for s in range(reduce.count):
        reduce.share(s)
    total.end(1)
    total.start(2)
    for s in range(reduce.count):
        reduce.end(s)
    total.end(2)


def reduce_pieces(plan, parts, squares, cuts, name, collective_id):
    count = len(parts)
    return pl.pallas_call(
        functools.partial(reduce_kernel, plan, cuts, count),
        in_specs=[pl.BlockSpec(memory_space=pl.ANY)] * count + [pl.BlockSpec(memory_space=pltpu.VMEM)],
        out_specs=[pl.BlockSpec(memory_space=pl.ANY)] * count + [pl.BlockSpec(memory_space=pltpu.VMEM)],
        out_shape=Reduce.shapes(plan, parts) + [jax.ShapeDtypeStruct((8, LANES), jnp.float32)],
        scratch_shapes=Reduce.scratch(plan, cuts, parts) + Total.scratch(plan),
        compiler_params=pltpu.CompilerParams(
            collective_id=collective_id, has_side_effects=True, vmem_limit_bytes=48 << 20
        ),
        cost_estimate=pl.CostEstimate(flops=0, bytes_accessed=32 << 20, transcendentals=0),
        name=name,
    )(*parts, squares)


def at_steps(stages, count, steps):
    for stage, when in zip(stages, steps):
        for s in range(count):
            pl.when(pl.program_id(0) == when[s])(functools.partial(stage, s))


def cut_of(rows, columns, dp):
    best = None
    across = 1
    while across <= dp and across * LANES <= columns:
        down = dp // across
        tall = -(-rows // (16 * down)) * 16
        if best is None or down * tall < best[0] * best[2]:
            best = (down, across, tall)
        across *= 2
    return best


def to_pieces(shards, array, dp):
    rows, columns = array.shape[1:]
    down, across, tall = cut_of(rows, columns, dp)
    array = jnp.pad(array, ((0, 0), (0, down * tall - rows), (0, 0)))
    array = array.reshape(shards, down, tall, across, columns // across).transpose(0, 1, 3, 2, 4)
    return array.reshape(shards, dp // 2, 2, tall, columns // across)


def from_pieces(pieces, rows, columns, dp):
    shards = pieces.shape[0]
    down, across, tall = cut_of(rows, columns, dp)
    array = pieces.reshape(shards, down, across, tall, columns // across).transpose(0, 1, 3, 2, 4)
    return array.reshape(shards, down * tall, columns)[:, :rows]


def own_piece(array, dp, first=0, columns=None):
    columns = columns or array.shape[1]
    down, across, tall = cut_of(array.shape[0], columns, dp)
    array = jnp.pad(array, ((0, down * tall - array.shape[0]), (0, 0)))
    group = lax.axis_index("dp")
    at = (group // across * tall, first + lax.rem(group, across) * (columns // across))
    return lax.dynamic_slice(array, at, (tall, columns // across))


def spread(ref, value, g):
    for col in range(COLS):
        ref[pl.ds(g * 8 * COLS + col, 8, stride=COLS), :] = value[:, LANES * col : LANES * (col + 1)]


def unspread(out, ref, g):
    rows = pl.multiple_of(g * 8, 8)
    for col in range(COLS):
        out[pl.ds(rows, 8), LANES * col : LANES * (col + 1)] = ref[pl.ds(g * 8 * COLS + col, 8, stride=COLS), :]


def lay_rates(ref, rates):
    for col in range(COLS):
        ref[pl.ds(col, N, stride=COLS), :] = rates[:, LANES * col : LANES * (col + 1)]


def token_rows(g, token):
    return pl.ds(pl.multiple_of(g * 8 * COLS, 8 * COLS) + token * COLS, COLS)


def prepare(g, sel, step, mixed, dts, us, bb):
    chosen = sel[pl.ds(pl.multiple_of(g * 8, 8), 8), :]
    fresh = chosen[:, 2 * N : 2 * N + 1] > 0.5
    spread(dts, jnp.where(fresh, RESET, step), g)
    spread(us, step * mixed, g)
    for k in range(2 * N):
        bb[g, k] = jnp.broadcast_to(chosen[:, k : k + 1], (8, LANES))


def splat(bb, g, first, count, token):
    return jnp.stack([bb[g, first + n, pl.ds(token, COLS, stride=0), :] for n in range(count)])


def softplus(v):
    small = jnp.exp(-jnp.abs(v))
    series = small * (1.0 - small * (1 / 2 - small * (1 / 3 - small * (1 / 4 - small * (1 / 5)))))
    return jnp.maximum(v, 0.0) + jnp.where(small < 1 / 32, series, jnp.log(1.0 + small))


def forward_kernel(plan, count, v_ref, mixed_ref, sel, rates, *refs):
    own, refs = refs[:count], refs[count:]
    (y_ref, dt_ref, hs_ref), full, refs = refs[:3], refs[3 : 3 + count], refs[3 + count :]
    state, laid, dts, us, bb, ys = refs[:6]
    gather = Gather(plan, GATHER_CUTS, own, full, *refs[6:])

    @pl.when(pl.program_id(0) == 0)
    def _():
        state[...] = jnp.zeros_like(state)
        lay_rates(laid, rates)
        greet(plan)

    at_steps(
        (gather.start, gather.spread, gather.pass_on, gather.share),
        gather.count,
        ((0, 0, 1, 2), (2, 3, 5, 6), (4, 5, 7, 9), (5, 7, 9, 11)),
    )

    @pl.loop(0, BLOCK // 8)
    def _(g):
        rows = pl.ds(pl.multiple_of(g * 8, 8), 8)
        dt_ref[rows, :] = softplus(v_ref[rows, :])

    @pl.loop(0, BLOCK // 16)
    def _(pair):
        mixed = mixed_ref[pl.ds(pl.multiple_of(pair * 16, 16), 16), :].astype(jnp.float32)
        for side in range(2):
            g = pair * 2 + side
            step = dt_ref[pl.ds(pl.multiple_of(g * 8, 8), 8), :]
            prepare(g, sel, step, mixed[8 * side : 8 * side + 8], dts, us, bb)

    for low in range(0, N, GROUP):
        part = pl.ds(low, GROUP)
        laid_part = pl.ds(low * COLS, GROUP * COLS)

        def steps(g, kept):
            for token in range(8):
                at = token_rows(g, token)
                decay = jnp.exp2(dts[at, :][None] * laid[laid_part, :].reshape(GROUP, COLS, LANES))
                kept = decay * kept + splat(bb, g, low, GROUP, token) * us[at, :][None]
                hs_ref[g * 8 + token, part] = kept
                total = jnp.sum(splat(bb, g, N + low, GROUP, token) * kept, axis=0)
                ys[at, :] = total if low == 0 else ys[at, :] + total
            return kept

        state[part] = lax.fori_loop(0, BLOCK // 8, steps, state[part])

    @pl.loop(0, BLOCK // 8)
    def _(g):
        unspread(y_ref, ys, g)

    at_steps((gather.end,), gather.count, ((11,) * gather.count,))


def fold(value):
    return jnp.sum(value.reshape(value.shape[0] // 8, 8, value.shape[1]), axis=0)


def backward_kernel(
    plan, count, v_ref, dt_ref, mixed_ref, gs_ref, sel, rates, vectors,
    step_weight, select_weight, hs_ref, last_ref, conv_ref, slope_ref, flags,
    *refs,
):
    given, refs = refs[:count], refs[count:]
    (grad_conv_in, pre_low, chosen, grad_rows, grad_rates, squares), refs = refs[:6], refs[6:]
    full, refs = refs[:count], refs[count:]
    (carry, laid, dts, us, gss, bb, s1, s2, prods, parts, nat1, nat2, grad_mixed, taps), refs = refs[:14], refs[14:]
    reduce = Reduce(plan, REDUCE_CUTS, given, full, squares, refs)
    turn = lax.rem(pl.program_id(0), TAIL)
    tall = BLOCK * TAIL
    own = pl.ds(pl.multiple_of((TAIL - 1 - turn) * BLOCK, BLOCK), BLOCK)

    @pl.when(pl.program_id(0) == 0)
    def _():
        for ref in (carry, grad_rates, grad_rows, parts):
            ref[...] = jnp.zeros_like(ref)
        taps[:, tall:, :] = jnp.zeros_like(taps[:, tall:, :])
        lay_rates(laid, rates)
        squares[...] = jnp.zeros_like(squares)
        greet(plan)

    at_steps(
        (reduce.start, reduce.sum_pair, reduce.sum_plane, reduce.sum_along, reduce.share),
        reduce.count,
        ((0, 0, 0, 0), (1, 1, 2, 2), (3, 4, 5, 6), (5, 6, 7, 8), (7, 8, 9, 10)),
    )

    @pl.loop(0, BLOCK // 16)
    def _(pair):
        mixed = mixed_ref[pl.ds(pl.multiple_of(pair * 16, 16), 16), :].astype(jnp.float32)
        for side in range(2):
            g = pair * 2 + side
            rows = pl.ds(pl.multiple_of(g * 8, 8), 8)
            prepare(g, sel, dt_ref[rows, :], mixed[8 * side : 8 * side + 8], dts, us, bb)
            spread(gss, gs_ref[rows, :], g)

    spot = lax.broadcasted_iota(jnp.int32, (8, LANES), 1)
    for low in range(0, N, BACK):
        part = pl.ds(low, BACK)
        laid_part = pl.ds(low * COLS, BACK * COLS)

        def steps(step, carried):
            g = BLOCK // 8 - 1 - step
            kept, total, sums = carried
            for token in reversed(range(8)):
                at = token_rows(g, token)
                dt, u, gs = dts[at, :][None], us[at, :][None], gss[at, :][None]
                if token > 0:
                    before = hs_ref[g * 8 + token - 1, part]
                else:
                    before = jnp.where(g == 0, last_ref[0, part], hs_ref[jnp.maximum(g * 8 - 1, 0), part])
                rate = laid[laid_part, :].reshape(BACK, COLS, LANES)
                adjoint = splat(bb, g, N + low, BACK, token) * gs + kept
                for_c = gs * hs_ref[g * 8 + token, part]
                for_b = adjoint * u
                in_sum = jnp.sum(splat(bb, g, low, BACK, token) * adjoint, axis=0)
                kept = jnp.exp2(dt * rate) * adjoint
                slope = kept * before
                decay_sum = jnp.sum(rate * slope, axis=0)
                total = total + dt * slope
                for kind, value in enumerate((for_b, for_c)):
                    prods[token % 2, pl.ds(8 * BACK * kind, 8 * BACK), :] = (value[:, :8] + value[:, 8:]).reshape(8 * BACK, LANES)
                here = spot == g * 8 + token
                new = []
                for first in range(0, 2 * BACK, 8):
                    rows_of = [prods[token % 2, pl.ds(8 * first + s, 8, stride=8), :] for s in range(8)]
                    while len(rows_of) > 1:
                        rows_of = [a + b for a, b in zip(rows_of[::2], rows_of[1::2])]
                    new.append(jnp.where(here, jnp.sum(rows_of[0], axis=1, keepdims=True), sums[first // 8]))
                sums = tuple(new)
                s1[at, :] = in_sum if low == 0 else s1[at, :] + in_sum
                s2[at, :] = decay_sum if low == 0 else s2[at, :] + decay_sum
            return kept, total, sums

        nothing = tuple(jnp.zeros((8, LANES), jnp.float32) for _ in range(2 * BACK // 8))
        carry[part], grad_rates[part], sums = lax.fori_loop(
            0, BLOCK // 8, steps, (carry[part], grad_rates[part], nothing)
        )
        sums = jnp.concatenate(sums, axis=0)
        parts[pl.ds(low, BACK), :] = sums[:BACK]
        parts[pl.ds(N + low, BACK), :] = sums[BACK:]

    @pl.loop(0, BLOCK // 8)
    def _(g):
        unspread(nat1, s1, g)
        unspread(nat2, s2, g)

    @pl.loop(0, DI // WIDE)
    def _(c):
        lanes = pl.ds(pl.multiple_of(c * WIDE, WIDE), WIDE)
        mixed = mixed_ref[:, lanes].astype(jnp.float32)
        step, gs, in_sum = dt_ref[:, lanes], gs_ref[:, lanes], nat1[:, lanes]
        pre = (mixed * in_sum + math.log(2.0) * nat2[:, lanes]) * jnp.exp(v_ref[:, lanes] - step)
        pre_low[own, lanes] = pre.astype(jnp.bfloat16)
        grad_mixed[own, lanes] = step * in_sum + vectors[CONV + 2 : CONV + 3, lanes] * gs
        grad_rows[CONV + 1, :, lanes] += fold(pre)
        grad_rows[CONV + 2, :, lanes] += fold(gs * mixed)

    chosen[own, R:] = parts[...].T[:BLOCK, : 2 * N].astype(jnp.bfloat16)

    @pl.when(turn == TAIL - 1)
    def _():
        chosen[:, :R] = dot(pre_low[...], step_weight[...], 1, 1).astype(jnp.bfloat16)

        @pl.loop(0, DI // WIDE)
        def _(c):
            lanes = pl.ds(pl.multiple_of(c * WIDE, WIDE), WIDE)
            total = grad_mixed[:, lanes] + dot(chosen[...], select_weight[:, lanes], 1, 0)
            grad_conv = total * slope_ref[:, lanes]
            value = conv_ref[:, lanes]
            grad_rows[CONV, :, lanes] += fold(grad_conv)
            result = vectors[CONV - 1 : CONV, lanes] * grad_conv
            grad_rows[CONV - 1, :, lanes] += fold(grad_conv * value)
            for j in range(1, CONV):
                taps[j - 1, :tall, lanes] = grad_conv * flags[:, 2 * N + j : 2 * N + j + 1]
                later = taps[j - 1, :, lanes][j : j + tall]
                grad_rows[CONV - 1 - j, :, lanes] += fold(later * value)
                result = result + vectors[CONV - 1 - j : CONV - j, lanes] * later
                taps[j - 1, tall:, lanes] = taps[j - 1, :8, lanes]
            grad_conv_in[:, lanes] = result.astype(jnp.bfloat16)

    at_steps((reduce.end,), reduce.count, ((11,) * reduce.count,))


def dot(left, right, left_dim, right_dim):
    return lax.dot_general(
        left, right, (((left_dim,), (right_dim,)), ((), ())), preferred_element_type=jnp.float32
    )


def scan_forward(v, mixed, sel, rates, plan, pieces):
    count = v.shape[0]
    anywhere = [pl.BlockSpec(memory_space=pl.ANY)] * len(pieces)
    rows = pl.BlockSpec((BLOCK, DI), lambda i: (i, 0))
    return pl.pallas_call(
        functools.partial(forward_kernel, plan, len(pieces)),
        grid=(count // BLOCK,),
        in_specs=[
            rows,
            rows,
            pl.BlockSpec((BLOCK, LANES), lambda i: (i, 0)),
            pl.BlockSpec((N, DI), lambda i: (0, 0)),
        ]
        + anywhere,
        out_specs=[rows, rows, pl.BlockSpec((BLOCK, N, COLS, LANES), lambda i: (i, 0, 0, 0))] + anywhere,
        out_shape=[
            jax.ShapeDtypeStruct((count, DI), jnp.float32),
            jax.ShapeDtypeStruct((count, DI), jnp.float32),
            jax.ShapeDtypeStruct((count, N, COLS, LANES), jnp.float32),
        ]
        + Gather.shapes(plan, pieces),
        scratch_shapes=[
            pltpu.VMEM((N, COLS, LANES), jnp.float32),
            pltpu.VMEM((N * COLS, LANES), jnp.float32),
            pltpu.VMEM((BLOCK * COLS, LANES), jnp.float32),
            pltpu.VMEM((BLOCK * COLS, LANES), jnp.float32),
            pltpu.VMEM((BLOCK // 8, 2 * N, 8, LANES), jnp.float32),
            pltpu.VMEM((BLOCK * COLS, LANES), jnp.float32),
        ]
        + Gather.scratch(plan, sum(GATHER_CUTS)),
        compiler_params=pltpu.CompilerParams(
            vmem_limit_bytes=48 << 20, collective_id=2, has_side_effects=True
        ),
        cost_estimate=pl.CostEstimate(
            flops=6 * count * N * DI, bytes_accessed=4 * count * N * DI, transcendentals=count * N * DI
        ),
        name="scan_forward",
    )(v, mixed, sel, rates, *pieces)


def scan_backward(v, dt, mixed, gs, conv_input, slope, sel, rates, vectors, step_weight, select_weight, states, plan, summed):
    count = dt.shape[0]
    blocks = count // BLOCK
    anywhere = [pl.BlockSpec(memory_space=pl.ANY)] * len(summed)
    rows = pl.BlockSpec((BLOCK, DI), lambda i: (blocks - 1 - i, 0))

    def tall(width):
        return pl.BlockSpec((BLOCK * TAIL, width), lambda i: (blocks // TAIL - 1 - i // TAIL, 0))

    def whole(*shape):
        return pl.BlockSpec(shape, lambda i: (0,) * len(shape))

    state = (N, COLS, LANES)
    return pl.pallas_call(
        functools.partial(backward_kernel, plan, len(summed)),
        grid=(blocks,),
        in_specs=[
            rows,
            rows,
            rows,
            rows,
            pl.BlockSpec((BLOCK, LANES), lambda i: (blocks - 1 - i, 0)),
            whole(N, DI),
            whole(8, DI),
            whole(R, DI),
            whole(R + 2 * N, DI),
            pl.BlockSpec((BLOCK,) + state, lambda i: (blocks - 1 - i, 0, 0, 0)),
            pl.BlockSpec((1,) + state, lambda i: (jnp.maximum((blocks - 1 - i) * BLOCK - 1, 0), 0, 0, 0)),
            tall(DI),
            tall(DI),
            tall(LANES),
        ]
        + anywhere,
        out_specs=[tall(DI), tall(DI), tall(R + 2 * N), whole(8, 8, DI), whole(*state), whole(8, LANES)]
        + anywhere,
        out_shape=[
            jax.ShapeDtypeStruct((count, DI), jnp.bfloat16),
            jax.ShapeDtypeStruct((count, DI), jnp.bfloat16),
            jax.ShapeDtypeStruct((count, R + 2 * N), jnp.bfloat16),
            jax.ShapeDtypeStruct((8, 8, DI), jnp.float32),
            jax.ShapeDtypeStruct(state, jnp.float32),
            jax.ShapeDtypeStruct((8, LANES), jnp.float32),
        ]
        + Reduce.shapes(plan, summed),
        scratch_shapes=[pltpu.VMEM(state, jnp.float32), pltpu.VMEM((N * COLS, LANES), jnp.float32)]
        + [pltpu.VMEM((BLOCK * COLS, LANES), jnp.float32)] * 3
        + [pltpu.VMEM((BLOCK // 8, 2 * N, 8, LANES), jnp.float32)]
        + [pltpu.VMEM((BLOCK * COLS, LANES), jnp.float32)] * 2
        + [pltpu.VMEM((2, 16 * BACK, LANES), jnp.float32)]
        + [pltpu.VMEM((LANES, LANES), jnp.float32)]
        + [pltpu.VMEM((BLOCK, DI), jnp.float32)] * 2
        + [pltpu.VMEM((BLOCK * TAIL, DI), jnp.float32)]
        + [pltpu.VMEM((CONV - 1, BLOCK * TAIL + 8, DI), jnp.float32)]
        + Reduce.scratch(plan, REDUCE_CUTS, summed),
        compiler_params=pltpu.CompilerParams(
            vmem_limit_bytes=60 << 20, collective_id=3, has_side_effects=True
        ),
        cost_estimate=pl.CostEstimate(
            flops=20 * count * N * DI, bytes_accessed=4 * count * N * DI, transcendentals=count * N * DI
        ),
        name="scan_backward",
    )(
        v, dt, mixed, gs, sel, rates, vectors, step_weight, select_weight,
        states, states, conv_input, slope, sel, *summed,
    )


def contract(left, right, left_dim, right_dim):
    return lax.dot_general(
        left, right, (((left_dim,), (right_dim,)), ((), ())), preferred_element_type=jnp.float32
    )


def channel_decay(rows_total):
    places = jnp.arange(rows_total, dtype=jnp.int32)[:, None]
    return ((places >= N) & (places < N + CONV)).astype(jnp.float32)


def adam_direction(weight, grad, first, second, factor, decay):
    clipped = grad * factor
    first = beta_one * first + (1.0 - beta_one) * clipped
    second = beta_two * second + (1.0 - beta_two) * clipped * clipped
    first_hat = first / (1.0 - beta_one**adam_step)
    second_hat = second / (1.0 - beta_two**adam_step)
    return first_hat / (jnp.sqrt(second_hat) + adam_eps) + decay_rate * decay * weight


def local(
    shards,
    dp,
    tokens,
    lengths,
    cotangent,
    norm_gain,
    input_weight,
    select_weight,
    step_weight,
    channel_params,
    output_weight,
    moment_gain,
    moment_input,
    moment_select,
    moment_step,
    moment_channel,
    moment_output,
    square_gain,
    square_input,
    square_select,
    square_step,
    square_channel,
    square_output,
):
    row_count = tokens.shape[0]
    live_mask, offset = block_layout(lengths[0], row_count)
    plan = (shards, dp // 2)
    low_conv = own_piece(input_weight, dp, 0, DI).astype(jnp.bfloat16)
    low_gate = own_piece(input_weight, dp, DI, DI).astype(jnp.bfloat16)
    low_output = own_piece(output_weight, dp).astype(jnp.bfloat16)
    low_small = own_piece(jnp.concatenate([select_weight, step_weight], axis=0), dp).astype(jnp.bfloat16)
    width = channel_params.shape[1]
    vectors = jnp.concatenate(
        [channel_params, jnp.pad(norm_gain, (0, width - norm_gain.shape[0]))[None, :]], axis=0
    )
    full_conv, full_small, full_vectors = gather_pieces(
        plan, [low_conv, low_small, own_piece(vectors, dp)], (4, 1, 1), "gather_weights", 0
    )
    full_conv = from_pieces(full_conv, norm_gain.shape[0], DI, dp).reshape(-1, DI)
    small_rows = R + 2 * N + R
    full_small = from_pieces(full_small, small_rows, width, dp).transpose(1, 0, 2).reshape(small_rows, DI)
    full_select, full_step = full_small[: R + 2 * N], full_small[R + 2 * N :]
    full_vectors = from_pieces(full_vectors, vectors.shape[0], width, dp)
    gain = full_vectors[:, -1, : norm_gain.shape[0]].reshape(-1)
    channel = full_vectors[:, :-1].transpose(1, 0, 2).reshape(-1, DI)
    inputs = tokens.astype(jnp.float32)
    normed_value, norm_pull = jax.vjp(rms_scale, inputs, gain)
    normed = normed_value.astype(jnp.bfloat16)
    conv_input = jnp.dot(normed, full_conv, preferred_element_type=jnp.float32)
    conv_out = causal_conv(conv_input, channel[N : N + CONV], channel[N + CONV], offset)
    sigmoid = jax.nn.sigmoid(conv_out)
    mixed, conv_slope = lax.optimization_barrier(
        ((conv_out * sigmoid).astype(jnp.bfloat16), sigmoid * (1.0 + conv_out * (1.0 - sigmoid)))
    )
    mixed_values = mixed.astype(jnp.float32)
    wide_select = jnp.concatenate([full_select[R:], jnp.zeros((R - 2 * N, DI), jnp.bfloat16), full_select[:R]], axis=0)
    selection = contract(mixed, wide_select, 1, 1)
    step_low = selection[:, LANES - R :].astype(jnp.bfloat16)
    step_in = jnp.dot(step_low, full_step, preferred_element_type=jnp.float32) + channel[N + CONV + 1][None, :]
    rates = -jnp.exp(channel[:N])
    rates_low = rates * math.log2(math.e)
    lane = lax.broadcasted_iota(jnp.int32, (row_count, LANES), 1)
    flag = jnp.where(lane == 2 * N, offset == 0, offset >= lane - 2 * N).astype(jnp.float32)
    chosen = jnp.where(lane < 2 * N, selection, jnp.where(lane < 2 * N + CONV, flag, 0.0))
    skip = channel[N + CONV + 2][None, :]
    state_out, step_size, states, full_gate, full_output = scan_forward(
        step_in, mixed, chosen, rates_low, plan, [low_gate, low_output]
    )
    full_gate = from_pieces(full_gate, norm_gain.shape[0], DI, dp).reshape(-1, DI)
    full_output = from_pieces(full_output, output_weight.shape[0], output_weight.shape[1], dp).reshape(DI, -1)
    gate_half = jnp.dot(normed, full_gate, preferred_element_type=jnp.float32)
    scanned = state_out + skip * mixed_values
    gate_value, gate_pull = jax.vjp(jax.nn.silu, gate_half)
    gated = (scanned * gate_value).astype(jnp.bfloat16)
    branch = jnp.dot(gated, full_output, preferred_element_type=jnp.float32)
    layer_output = (inputs + live_mask * branch).astype(jnp.bfloat16)
    upstream = cotangent.astype(jnp.float32)
    grad_branch = (upstream * live_mask).astype(jnp.bfloat16)
    grad_output = contract(gated, grad_branch, 0, 0).astype(jnp.bfloat16)
    grad_gated = contract(grad_branch, full_output, 1, 1)
    grad_scanned = grad_gated * gate_value
    (grad_gate,) = gate_pull(grad_gated * scanned)
    grad_gate = grad_gate.astype(jnp.bfloat16)
    grad_gate_weight = contract(normed, grad_gate, 0, 0).astype(jnp.bfloat16)
    heights = [norm_gain.shape[0], output_weight.shape[0]]
    grad_conv_input, grad_pre_low, grad_selection, grad_rows, sums, squares, sum_output, sum_gate = scan_backward(
        step_in,
        step_size,
        mixed,
        grad_scanned,
        conv_input,
        conv_slope,
        chosen,
        rates_low,
        jnp.pad(channel[N:], ((0, 1), (0, 0))),
        full_step,
        full_select,
        states,
        plan,
        [
            to_pieces(shards, grad_output.reshape(shards, heights[1], -1), dp),
            to_pieces(shards, grad_gate_weight.reshape(shards, heights[0], -1), dp),
        ],
    )
    grad_step = contract(step_low, grad_pre_low, 0, 0)
    grad_select = contract(grad_selection, mixed, 0, 0)
    grad_conv_weight = contract(normed, grad_conv_input, 0, 0).astype(jnp.bfloat16)
    grad_normed = contract(grad_conv_input, full_conv, 1, 1) + contract(grad_gate, full_gate, 1, 1)
    grad_inputs, grad_gain = norm_pull(grad_normed)
    input_grad = (upstream + grad_inputs).astype(jnp.bfloat16)
    grad_channel = jnp.concatenate(
        [rates * sums.reshape(N, DI), jnp.sum(grad_rows[: CONV + 3], axis=1)], axis=0
    )
    small = jnp.concatenate([grad_select, grad_step, grad_channel], axis=0)
    small = small.reshape(-1, shards, width).transpose(1, 0, 2)
    small_gain = jnp.pad(grad_gain.reshape(shards, 1, -1), ((0, 0), (0, 0), (0, width - grad_gain.shape[0] // shards)))
    small = jnp.concatenate([small, small_gain], axis=1).astype(jnp.bfloat16)
    sum_conv, sum_small, squares = reduce_pieces(
        plan,
        [
            to_pieces(shards, grad_conv_weight.reshape(shards, heights[0], -1), dp),
            to_pieces(shards, small, dp),
        ],
        squares,
        (4, 1),
        "sum_gradients",
        1,
    )
    sum_output, sum_gate, sum_conv, sum_small = (
        from_pieces(pieces[None], rows, columns, dp)[0].astype(jnp.float32)
        for pieces, rows, columns in (
            (sum_output, heights[1], output_weight.shape[1]),
            (sum_gate, heights[0], DI),
            (sum_conv, heights[0], DI),
            (sum_small, small.shape[1], width),
        )
    )
    sum_input = jnp.concatenate([sum_conv, sum_gate], axis=1)
    sum_select, sum_step = sum_small[: R + 2 * N], sum_small[R + 2 * N : small_rows]
    sum_channel, sum_gain = sum_small[small_rows:-1], sum_small[-1, : norm_gain.shape[0]]
    grads = (sum_gain, sum_input, sum_select, sum_step, sum_channel, sum_output)
    grad_norm = jnp.sqrt(jnp.sum(squares))
    factor = jnp.minimum(1.0, clip_norm / (grad_norm + 1e-06))
    params = (norm_gain, input_weight, select_weight, step_weight, channel_params, output_weight)
    firsts = (moment_gain, moment_input, moment_select, moment_step, moment_channel, moment_output)
    seconds = (square_gain, square_input, square_select, square_step, square_channel, square_output)
    decays = (0.0, 1.0, 1.0, 1.0, channel_decay(channel_params.shape[0]), 1.0)
    updates = [
        adam_direction(
            params[which], grads[which], firsts[which], seconds[which], factor, decays[which]
        )
        for which in range(6)
    ]
    return (
        layer_output,
        input_grad,
        grad_norm,
        updates[0],
        updates[1],
        updates[2],
        updates[3],
        updates[4],
        updates[5],
        grads[0],
        grads[1],
        grads[2],
        grads[3],
        grads[4],
        grads[5],
    )


def solution(mesh):
    in_specs = (
        P(("dp", "fsdp"), None),
        P(("dp", "fsdp"), None),
        P(("dp", "fsdp"), None),
        P("fsdp"),
        P("fsdp", None),
        P(None, "fsdp"),
        P(None, "fsdp"),
        P(None, "fsdp"),
        P("fsdp", None),
        P("fsdp"),
        P("fsdp", None),
        P(None, "fsdp"),
        P(None, "fsdp"),
        P(None, "fsdp"),
        P("fsdp", None),
        P("fsdp"),
        P("fsdp", None),
        P(None, "fsdp"),
        P(None, "fsdp"),
        P(None, "fsdp"),
        P("fsdp", None),
    )
    out_specs = (
        P(("dp", "fsdp"), None),
        P(("dp", "fsdp"), None),
        P(),
        P("fsdp"),
        P("fsdp", None),
        P(None, "fsdp"),
        P(None, "fsdp"),
        P(None, "fsdp"),
        P("fsdp", None),
        P("fsdp"),
        P("fsdp", None),
        P(None, "fsdp"),
        P(None, "fsdp"),
        P(None, "fsdp"),
        P("fsdp", None),
    )
    shards, dp = mesh.shape["fsdp"], mesh.shape["dp"]
    return jax.shard_map(functools.partial(local, shards, dp), mesh=mesh, in_specs=in_specs, out_specs=out_specs, check_vma=False)
```

```python
import functools
import math

import jax
import jax.numpy as jnp
from jax import lax
from jax.experimental import pallas as pl
from jax.experimental.pallas import tpu as pltpu
from jax.sharding import PartitionSpec as P

DI = 2048
N = 16
R = 64
CONV = 4
LANES = 128
COLS = DI // LANES
HALVES = COLS // 8
BLOCK = 64
GROUP = 8
BACK = 4
AHEAD = 16
BEHIND = 16
GATHER_CUTS = (2, 2)
REDUCE_CUTS = (2, 2)
WIDE = 512
TAIL = 2

norm_eps = 1e-05
beta_one = 0.9
beta_two = 0.95
adam_eps = 1e-08
decay_rate = 0.1
adam_step = 10.0
clip_norm = 1.0
RESET = 1e30


def block_layout(lengths_row, count):
    places = lax.broadcasted_iota(jnp.int32, (count, LANES), 0)
    begun = jnp.zeros((count, LANES), jnp.int32)
    end = jnp.zeros((), jnp.int32)
    for cluster in range(lengths_row.shape[0]):
        begun = jnp.where(end <= places, jnp.maximum(begun, end), begun)
        end = end + lengths_row[cluster]
    return (places[:, :1] < end).astype(jnp.float32), places - begun


def rms_scale(values, scales):
    return (
        values
        * lax.rsqrt(jnp.mean(values * values, axis=1, keepdims=True) + norm_eps)
        * scales[None, :]
    )


def causal_conv(values, kernel, shift, offset):
    total = shift[None, :] + kernel[CONV - 1][None, :] * values
    for distance in range(1, CONV):
        moved = jnp.pad(values, ((distance, 0), (0, 0)))[:-distance]
        keep = (offset[:, :1] >= distance).astype(jnp.float32)
        total = total + kernel[CONV - 1 - distance][None, :] * moved * keep
    return total


def mesh_copy(src, dst, sems, at, device):
    return pltpu.make_async_remote_copy(
        src_ref=src,
        dst_ref=dst,
        send_sem=sems.at[0, at],
        recv_sem=sems.at[1, at],
        device_id=device,
        device_id_type=pl.DeviceIdType.MESH,
    )


def placed(plan):
    group = lax.axis_index("dp")
    return lax.axis_index("fsdp"), group // 2, lax.rem(group, 2)


def peers_of(plan):
    shards, places = plan
    mine, place, side = placed(plan)
    along = [(place * 2 + side, lax.rem(mine + k, shards)) for k in range(1, shards)]
    plane = [((place ^ j) * 2 + side, mine) for j in range(1, places)]
    return along, plane, (place * 2 + 1 - side, mine)


def greet(plan):
    along, plane, pair = peers_of(plan)
    barrier = pltpu.get_barrier_semaphore()
    everyone = along + plane + [pair]
    for device in everyone:
        pl.semaphore_signal(barrier, inc=1, device_id=device, device_id_type=pl.DeviceIdType.MESH)
    pl.semaphore_wait(barrier, len(everyone))


def chunks(arrays, cuts):
    made = []
    for i, (array, cut) in enumerate(zip(arrays, cuts)):
        width = array.shape[-1] // cut
        made += [(i, pl.ds(k * width, width)) for k in range(cut)]
    return made


class Gather:
    def __init__(self, plan, cuts, own, full, near, far, wide, cross):
        self.plan, self.all_own, self.all_full = plan, own, full
        self.near, self.far, self.wide, self.cross = near, far, wide, cross
        self.chunks = chunks(own, cuts)
        self.count = len(self.chunks)

    def own(self, s):
        i, columns = self.chunks[s]
        return self.all_own[i].at[:, columns]

    def full(self, s, *at):
        i, columns = self.chunks[s]
        return self.all_full[i].at[(*at, slice(None), columns)]

    @staticmethod
    def scratch(plan, count):
        shards, places = plan
        return [
            pltpu.SemaphoreType.DMA((count,)),
            pltpu.SemaphoreType.DMA((2, count * (shards - 1))),
            pltpu.SemaphoreType.DMA((2, count * places)),
            pltpu.SemaphoreType.DMA((2, count)),
        ]

    @staticmethod
    def shapes(plan, pieces):
        return [jax.ShapeDtypeStruct(plan + (2,) + piece.shape, piece.dtype) for piece in pieces]

    def keep(self, s):
        mine, place, side = placed(self.plan)
        return pltpu.make_async_copy(self.own(s), self.full(s, mine, place, side), self.near.at[s])

    def along(self, s):
        mine, place, side = placed(self.plan)
        return [
            mesh_copy(self.own(s), self.full(s, mine, place, side), self.far, s * (self.plan[0] - 1) + k, device)
            for k, device in enumerate(peers_of(self.plan)[0])
        ]

    def plane(self, s):
        _, place, side = placed(self.plan)
        part = self.full(s, slice(None), place, side)
        devices = peers_of(self.plan)[1]
        return [
            mesh_copy(part, part, self.wide, s * self.plan[1] + k, device)
            for k, device in enumerate(devices[:2] if self.plan[1] == 4 else devices)
        ]

    def relay(self, s):
        if self.plan[1] != 4:
            return []
        _, place, side = placed(self.plan)
        devices = peers_of(self.plan)[1]
        half = self.plan[0] // 2
        made = []
        for k, rows in enumerate((pl.ds(0, half), pl.ds(half, self.plan[0] - half))):
            part = self.full(s, rows, place ^ (k + 1), side)
            made.append(mesh_copy(part, part, self.wide, s * 4 + 2 + k, devices[1 - k]))
        return made

    def pair(self, s):
        part = self.full(s, slice(None), slice(None), placed(self.plan)[2])
        return mesh_copy(part, part, self.cross, s, peers_of(self.plan)[2])

    def start(self, s):
        self.keep(s).start()
        for copy in self.along(s):
            copy.start()

    def spread(self, s):
        self.keep(s).wait()
        for copy in self.along(s):
            copy.wait_recv()
        for copy in self.plane(s):
            copy.start()

    def pass_on(self, s):
        for copy in self.plane(s):
            copy.wait_recv()
        for copy in self.relay(s):
            copy.start()

    def share(self, s):
        for copy in self.relay(s):
            copy.wait_recv()
        self.pair(s).start()

    def end(self, s):
        for copy in self.along(s) + self.plane(s) + self.relay(s):
            copy.wait_send()
        self.pair(s).wait()


def gather_kernel(plan, cuts, count, *refs):
    gather = Gather(plan, cuts, refs[:count], refs[count : 2 * count], *refs[2 * count :])
    greet(plan)
    ahead = 2
    for s in range(gather.count + 4):
        for stage, wait in ((gather.start, 0), (gather.spread, ahead), (gather.pass_on, 3), (gather.share, 4)):
            if 0 <= s - wait < gather.count:
                stage(s - wait)
    for s in range(gather.count):
        gather.end(s)


def gather_pieces(plan, pieces, cuts, name, collective_id):
    count = len(pieces)
    return pl.pallas_call(
        functools.partial(gather_kernel, plan, cuts, count),
        in_specs=[pl.BlockSpec(memory_space=pl.ANY)] * count,
        out_specs=[pl.BlockSpec(memory_space=pltpu.VMEM)] * count,
        out_shape=Gather.shapes(plan, pieces),
        scratch_shapes=Gather.scratch(plan, sum(cuts)),
        compiler_params=pltpu.CompilerParams(collective_id=collective_id, has_side_effects=True, vmem_limit_bytes=32 << 20),
        cost_estimate=pl.CostEstimate(flops=0, bytes_accessed=32 << 20, transcendentals=0),
        name=name,
    )(*pieces)


def wide_sum(values):
    total = values[0].astype(jnp.float32)
    for value in values[1:]:
        total = total + value.astype(jnp.float32)
    return total.astype(jnp.bfloat16)


class Reduce:
    def __init__(self, plan, cuts, parts, full, squares, scratch):
        count = sum(cuts)
        self.squares = squares
        self.plan, self.all_parts, self.all_full, self.count = plan, parts, full, count
        self.chunks = chunks(parts, cuts)
        self.held, self.from_pair, self.from_plane, self.from_along, self.piece = (
            scratch[k * count : (k + 1) * count] for k in range(5)
        )
        self.near, self.cross, self.wide, self.far, self.back, self.over = scratch[5 * count :]

    def parts(self, s, *at):
        i, columns = self.chunks[s]
        return self.all_parts[i].at[(*at, slice(None), columns)]

    def full(self, s, *at):
        i, columns = self.chunks[s]
        return self.all_full[i].at[(*at, slice(None), columns)]

    @staticmethod
    def scratch(plan, cuts, parts):
        shards, places = plan
        count = sum(cuts)
        tails = [(part.shape[3], part.shape[4] // cut) for part, cut in zip(parts, cuts) for _ in range(cut)]
        leads = [(shards, places), (shards, places), (places - 1, shards), (shards - 1,), ()]
        return [pltpu.VMEM(lead + tail, jnp.bfloat16) for lead in leads for tail in tails] + [
            pltpu.SemaphoreType.DMA((2, count)),
            pltpu.SemaphoreType.DMA((2, count)),
            pltpu.SemaphoreType.DMA((2, count * (places - 1))),
            pltpu.SemaphoreType.DMA((2, count * (shards - 1))),
            pltpu.SemaphoreType.DMA((2, count * (places - 1))),
            pltpu.SemaphoreType.DMA((2, count)),
        ]

    @staticmethod
    def shapes(plan, parts):
        return [jax.ShapeDtypeStruct((plan[1], 2) + part.shape[3:], jnp.bfloat16) for part in parts]

    def keep(self, s):
        side = placed(self.plan)[2]
        return pltpu.make_async_copy(self.parts(s, slice(None), slice(None), side), self.held[s], self.near.at[0, s])

    def pair(self, s):
        side = placed(self.plan)[2]
        return mesh_copy(
            self.parts(s, slice(None), slice(None), 1 - side), self.from_pair[s], self.cross, s, peers_of(self.plan)[2]
        )

    def plane(self, s):
        place = placed(self.plan)[1]
        return [
            mesh_copy(
                self.held[s].at[:, place ^ (k + 1)],
                self.from_plane[s].at[k],
                self.wide,
                s * (self.plan[1] - 1) + k,
                device,
            )
            for k, device in enumerate(peers_of(self.plan)[1])
        ]

    def along(self, s):
        mine, place, _ = placed(self.plan)
        shards = self.plan[0]
        return [
            mesh_copy(
                self.held[s].at[lax.rem(mine + k + 1, shards), place],
                self.from_along[s].at[k],
                self.far,
                s * (shards - 1) + k,
                device,
            )
            for k, device in enumerate(peers_of(self.plan)[0])
        ]

    def put(self, s):
        _, place, side = placed(self.plan)
        return pltpu.make_async_copy(self.piece[s], self.full(s, place, side), self.near.at[1, s])

    def home(self, s):
        _, place, side = placed(self.plan)
        return [
            mesh_copy(self.piece[s], self.full(s, place, side), self.back, s * (self.plan[1] - 1) + k, device)
            for k, device in enumerate(peers_of(self.plan)[1])
        ]

    def other(self, s):
        part = self.full(s, slice(None), placed(self.plan)[2])
        return mesh_copy(part, part, self.over, s, peers_of(self.plan)[2])

    def start(self, s):
        self.keep(s).start()
        self.pair(s).start()

    def sum_pair(self, s):
        self.keep(s).wait()
        self.pair(s).wait_recv()
        held, other = self.held[s], self.from_pair[s]

        @pl.loop(0, self.plan[0] * self.plan[1])
        def _(i):
            a, b = i // self.plan[1], lax.rem(i, self.plan[1])
            held[a, b] = wide_sum([held[a, b], other[a, b]])

        for copy in self.plane(s):
            copy.start()

    def sum_plane(self, s):
        place = placed(self.plan)[1]
        for copy in self.plane(s):
            copy.wait_recv()
        held, others = self.held[s], self.from_plane[s]

        @pl.loop(0, self.plan[0])
        def _(i):
            held[i, place] = wide_sum([held[i, place]] + [others[k, i] for k in range(self.plan[1] - 1)])

        for copy in self.along(s):
            copy.start()

    def sum_along(self, s):
        mine, place, _ = placed(self.plan)
        for copy in self.along(s):
            copy.wait_recv()
        others = self.from_along[s]
        piece = wide_sum([self.held[s][mine, place]] + [others[k] for k in range(self.plan[0] - 1)])
        self.piece[s][...] = piece
        square = piece.astype(jnp.float32) * piece.astype(jnp.float32)
        square = jnp.sum(square.reshape(-1, 8, square.shape[1]), axis=0)
        for first in range(0, square.shape[1], LANES):
            self.squares[...] += square[:, first : first + LANES]
        self.put(s).start()
        for copy in self.home(s):
            copy.start()

    def share(self, s):
        self.put(s).wait()
        for copy in self.home(s):
            copy.wait_recv()
        self.other(s).start()

    def end(self, s):
        self.pair(s).wait_send()
        for copy in self.plane(s) + self.along(s) + self.home(s):
            copy.wait_send()
        self.other(s).wait()


class Total:
    def __init__(self, plan, value, scratch):
        self.plan, self.value = plan, value
        self.slots, self.sent, self.sems = scratch[:3], scratch[3], scratch[4:]

    @staticmethod
    def scratch(plan):
        sizes = (plan[0], plan[1], 2)
        return (
            [pltpu.VMEM((size, 8, LANES), jnp.float32) for size in sizes]
            + [pltpu.VMEM((3, 8, LANES), jnp.float32)]
            + [pltpu.SemaphoreType.DMA((2, size - 1)) for size in sizes]
        )

    def copies(self, level):
        along, plane, pair = peers_of(self.plan)
        at = placed(self.plan)[level]
        return [
            mesh_copy(self.sent.at[level], self.slots[level].at[at], self.sems[level], k, device)
            for k, device in enumerate((along, plane, [pair])[level])
        ]

    def start(self, level):
        self.sent[level] = self.value[...]
        self.slots[level][placed(self.plan)[level]] = self.value[...]
        for copy in self.copies(level):
            copy.start()

    def end(self, level):
        for copy in self.copies(level):
            copy.wait()
        total = self.slots[level][0]
        for k in range(1, self.slots[level].shape[0]):
            total = total + self.slots[level][k]
        self.value[...] = total


def reduce_kernel(plan, cuts, count, *refs):
    given, refs = refs[:count], refs[count:]
    before, refs = refs[0], refs[1:]
    full, squares, refs = refs[:count], refs[count], refs[count + 1 :]
    reduce = Reduce(plan, cuts, given, full, squares, refs[:-7])
    total = Total(plan, squares, refs[-7:])
    squares[...] = before[...]
    greet(plan)
    for stage in (reduce.start, reduce.sum_pair, reduce.sum_plane, reduce.sum_along):
        for s in range(reduce.count):
            stage(s)
    total.start(0)
    total.end(0)
    total.start(1)
    for s in range(reduce.count):
        reduce.share(s)
    total.end(1)
    total.start(2)
    for s in range(reduce.count):
        reduce.end(s)
    total.end(2)


def reduce_pieces(plan, parts, squares, cuts, name, collective_id):
    count = len(parts)
    return pl.pallas_call(
        functools.partial(reduce_kernel, plan, cuts, count),
        in_specs=[pl.BlockSpec(memory_space=pl.ANY)] * count + [pl.BlockSpec(memory_space=pltpu.VMEM)],
        out_specs=[pl.BlockSpec(memory_space=pl.ANY)] * count + [pl.BlockSpec(memory_space=pltpu.VMEM)],
        out_shape=Reduce.shapes(plan, parts) + [jax.ShapeDtypeStruct((8, LANES), jnp.float32)],
        scratch_shapes=Reduce.scratch(plan, cuts, parts) + Total.scratch(plan),
        compiler_params=pltpu.CompilerParams(
            collective_id=collective_id, has_side_effects=True, vmem_limit_bytes=48 << 20
        ),
        cost_estimate=pl.CostEstimate(flops=0, bytes_accessed=32 << 20, transcendentals=0),
        name=name,
    )(*parts, squares)


def at_steps(stages, count, steps):
    for stage, when in zip(stages, steps):
        for s in range(count):
            pl.when(pl.program_id(0) == when[s])(functools.partial(stage, s))


def cut_of(rows, columns, dp):
    best = None
    across = 1
    while across <= dp and across * LANES <= columns:
        down = dp // across
        tall = -(-rows // (16 * down)) * 16
        if best is None or down * tall < best[0] * best[2]:
            best = (down, across, tall)
        across *= 2
    return best


def to_pieces(shards, array, dp):
    rows, columns = array.shape[1:]
    down, across, tall = cut_of(rows, columns, dp)
    array = jnp.pad(array, ((0, 0), (0, down * tall - rows), (0, 0)))
    array = array.reshape(shards, down, tall, across, columns // across).transpose(0, 1, 3, 2, 4)
    return array.reshape(shards, dp // 2, 2, tall, columns // across)


def from_pieces(pieces, rows, columns, dp):
    shards = pieces.shape[0]
    down, across, tall = cut_of(rows, columns, dp)
    array = pieces.reshape(shards, down, across, tall, columns // across).transpose(0, 1, 3, 2, 4)
    return array.reshape(shards, down * tall, columns)[:, :rows]


def own_piece(array, dp, first=0, columns=None):
    columns = columns or array.shape[1]
    down, across, tall = cut_of(array.shape[0], columns, dp)
    array = jnp.pad(array, ((0, down * tall - array.shape[0]), (0, 0)))
    group = lax.axis_index("dp")
    at = (group // across * tall, first + lax.rem(group, across) * (columns // across))
    return lax.dynamic_slice(array, at, (tall, columns // across))


def spread(ref, value, g):
    for col in range(COLS):
        ref[pl.ds(g * 8 * COLS + col, 8, stride=COLS), :] = value[:, LANES * col : LANES * (col + 1)]


def unspread(out, ref, g):
    rows = pl.multiple_of(g * 8, 8)
    for col in range(COLS):
        out[pl.ds(rows, 8), LANES * col : LANES * (col + 1)] = ref[pl.ds(g * 8 * COLS + col, 8, stride=COLS), :]


def lay_rates(ref, rates):
    for col in range(COLS):
        ref[pl.ds(col, N, stride=COLS), :] = rates[:, LANES * col : LANES * (col + 1)]


def token_rows(row):
    return pl.ds(pl.multiple_of(row * COLS, COLS), COLS)


def prepare(g, sel, step, mixed, dts, us, bb):
    chosen = sel[pl.ds(pl.multiple_of(g * 8, 8), 8), :]
    fresh = chosen[:, 2 * N : 2 * N + 1] > 0.5
    spread(dts, jnp.where(fresh, RESET, step), g)
    spread(us, step * mixed, g)
    for k in range(2 * N):
        bb[g, k] = jnp.broadcast_to(chosen[:, k : k + 1], (8, LANES))


def splat(bb, g, first, count, token):
    rows = [bb[g, first + n, pl.ds(token, 8, stride=0), :] for n in range(count)]
    return jnp.stack([jnp.concatenate([row] * HALVES, axis=0) for row in rows])


def softplus(v):
    small = jnp.exp(-jnp.abs(v))
    series = small * (1.0 - small * (1 / 2 - small * (1 / 3 - small * (1 / 4 - small * (1 / 5)))))
    return jnp.maximum(v, 0.0) + jnp.where(small < 1 / 32, series, jnp.log(1.0 + small))


def forward_kernel(plan, count, v_ref, mixed_ref, sel, rates, *refs):
    own, refs = refs[:count], refs[count:]
    (y_ref, dt_ref, hs_ref), full, refs = refs[:3], refs[3 : 3 + count], refs[3 + count :]
    state, laid, dts, us, bb, ys = refs[:6]
    gather = Gather(plan, GATHER_CUTS, own, full, *refs[6:])

    @pl.when(pl.program_id(0) == 0)
    def _():
        state[...] = jnp.zeros_like(state)
        lay_rates(laid, rates)
        greet(plan)

    at_steps(
        (gather.start, gather.spread, gather.pass_on, gather.share),
        gather.count,
        ((0, 0, 1, 2), (2, 3, 5, 6), (4, 5, 7, 9), (5, 7, 9, 11)),
    )

    @pl.loop(0, BLOCK // 8)
    def _(g):
        rows = pl.ds(pl.multiple_of(g * 8, 8), 8)
        dt_ref[rows, :] = softplus(v_ref[rows, :])

    @pl.loop(0, BLOCK // 16)
    def _(pair):
        mixed = mixed_ref[pl.ds(pl.multiple_of(pair * 16, 16), 16), :].astype(jnp.float32)
        for side in range(2):
            g = pair * 2 + side
            step = dt_ref[pl.ds(pl.multiple_of(g * 8, 8), 8), :]
            prepare(g, sel, step, mixed[8 * side : 8 * side + 8], dts, us, bb)

    for low in range(0, N, GROUP):
        part = pl.ds(low, GROUP)
        laid_part = pl.ds(low * COLS, GROUP * COLS)

        def steps(step, kept):
            first = step * AHEAD
            for k in range(AHEAD):
                row = first + k
                g, token = step * (AHEAD // 8) + k // 8, k % 8
                at = token_rows(row)
                decay = jnp.exp2(dts[at, :][None] * laid[laid_part, :].reshape(GROUP, COLS, LANES))
                kept = decay * kept + splat(bb, g, low, GROUP, token) * us[at, :][None]
                hs_ref[row, part] = kept
                total = jnp.sum(splat(bb, g, N + low, GROUP, token) * kept, axis=0)
                ys[at, :] = total if low == 0 else ys[at, :] + total
            return kept

        state[part] = lax.fori_loop(0, BLOCK // AHEAD, steps, state[part])

    @pl.loop(0, BLOCK // 8)
    def _(g):
        unspread(y_ref, ys, g)

    at_steps((gather.end,), gather.count, ((11,) * gather.count,))


def fold(value):
    return jnp.sum(value.reshape(value.shape[0] // 8, 8, value.shape[1]), axis=0)


def backward_kernel(
    plan, count, v_ref, dt_ref, mixed_ref, gs_ref, sel, rates, vectors,
    step_weight, select_weight, hs_ref, last_ref, conv_ref, slope_ref, flags,
    *refs,
):
    given, refs = refs[:count], refs[count:]
    (grad_conv_in, pre_low, chosen, grad_rows, grad_rates, squares), refs = refs[:6], refs[6:]
    full, refs = refs[:count], refs[count:]
    (carry, laid, dts, us, gss, bb, s1, s2, prods, parts, nat1, nat2, grad_mixed, taps), refs = refs[:14], refs[14:]
    reduce = Reduce(plan, REDUCE_CUTS, given, full, squares, refs)
    turn = lax.rem(pl.program_id(0), TAIL)
    tall = BLOCK * TAIL
    own = pl.ds(pl.multiple_of((TAIL - 1 - turn) * BLOCK, BLOCK), BLOCK)

    @pl.when(pl.program_id(0) == 0)
    def _():
        for ref in (carry, grad_rates, grad_rows, parts):
            ref[...] = jnp.zeros_like(ref)
        taps[:, tall:, :] = jnp.zeros_like(taps[:, tall:, :])
        lay_rates(laid, rates)
        squares[...] = jnp.zeros_like(squares)
        greet(plan)

    at_steps(
        (reduce.start, reduce.sum_pair, reduce.sum_plane, reduce.sum_along, reduce.share),
        reduce.count,
        ((0, 0, 0, 0), (1, 1, 2, 2), (3, 4, 5, 6), (5, 6, 7, 8), (7, 8, 9, 10)),
    )

    @pl.loop(0, BLOCK // 16)
    def _(pair):
        mixed = mixed_ref[pl.ds(pl.multiple_of(pair * 16, 16), 16), :].astype(jnp.float32)
        for side in range(2):
            g = pair * 2 + side
            rows = pl.ds(pl.multiple_of(g * 8, 8), 8)
            prepare(g, sel, dt_ref[rows, :], mixed[8 * side : 8 * side + 8], dts, us, bb)
            spread(gss, gs_ref[rows, :], g)

    spot = lax.broadcasted_iota(jnp.int32, (8, LANES), 1)
    for low in range(0, N, BACK):
        part = pl.ds(low, BACK)
        laid_part = pl.ds(low * COLS, BACK * COLS)

        def steps(step, carried):
            first = BLOCK - BEHIND * (step + 1)
            kept, total, sums = carried
            before = hs_ref[first + BEHIND - 1, part]
            for k in reversed(range(BEHIND)):
                row = first + k
                g, token = BLOCK // 8 - (step + 1) * (BEHIND // 8) + k // 8, k % 8
                now = before
                at = token_rows(row)
                dt, u, gs = dts[at, :][None], us[at, :][None], gss[at, :][None]
                if k > 0:
                    before = hs_ref[row - 1, part]
                else:
                    before = jnp.where(first == 0, last_ref[0, part], hs_ref[jnp.maximum(first - 1, 0), part])
                rate = laid[laid_part, :].reshape(BACK, COLS, LANES)
                adjoint = splat(bb, g, N + low, BACK, token) * gs + kept
                for_c = gs * now
                for_b = adjoint * u
                in_sum = jnp.sum(splat(bb, g, low, BACK, token) * adjoint, axis=0)
                kept = jnp.exp2(dt * rate) * adjoint
                slope = kept * before
                decay_sum = jnp.sum(rate * slope, axis=0)
                total = total + dt * slope
                for kind, value in enumerate((for_b, for_c)):
                    prods[k % 2, pl.ds(8 * BACK * kind, 8 * BACK), :] = (value[:, :8] + value[:, 8:]).reshape(8 * BACK, LANES)
                here = spot == row
                new = []
                for low_row in range(0, 2 * BACK, 8):
                    rows_of = [prods[k % 2, pl.ds(8 * low_row + s, 8, stride=8), :] for s in range(8)]
                    while len(rows_of) > 1:
                        rows_of = [a + b for a, b in zip(rows_of[::2], rows_of[1::2])]
                    new.append(jnp.where(here, jnp.sum(rows_of[0], axis=1, keepdims=True), sums[low_row // 8]))
                sums = tuple(new)
                s1[at, :] = in_sum if low == 0 else s1[at, :] + in_sum
                s2[at, :] = decay_sum if low == 0 else s2[at, :] + decay_sum
            return kept, total, sums

        nothing = tuple(jnp.zeros((8, LANES), jnp.float32) for _ in range(2 * BACK // 8))
        carry[part], grad_rates[part], sums = lax.fori_loop(
            0, BLOCK // BEHIND, steps, (carry[part], grad_rates[part], nothing)
        )
        sums = jnp.concatenate(sums, axis=0)
        parts[pl.ds(low, BACK), :] = sums[:BACK]
        parts[pl.ds(N + low, BACK), :] = sums[BACK:]

    @pl.loop(0, BLOCK // 8)
    def _(g):
        unspread(nat1, s1, g)
        unspread(nat2, s2, g)

    @pl.loop(0, DI // WIDE)
    def _(c):
        lanes = pl.ds(pl.multiple_of(c * WIDE, WIDE), WIDE)
        mixed = mixed_ref[:, lanes].astype(jnp.float32)
        step, gs, in_sum = dt_ref[:, lanes], gs_ref[:, lanes], nat1[:, lanes]
        pre = (mixed * in_sum + math.log(2.0) * nat2[:, lanes]) * jnp.exp(v_ref[:, lanes] - step)
        pre_low[own, lanes] = pre.astype(jnp.bfloat16)
        grad_mixed[own, lanes] = step * in_sum + vectors[CONV + 2 : CONV + 3, lanes] * gs
        grad_rows[CONV + 1, :, lanes] += fold(pre)
        grad_rows[CONV + 2, :, lanes] += fold(gs * mixed)

    chosen[own, R:] = parts[...].T[:BLOCK, : 2 * N].astype(jnp.bfloat16)

    @pl.when(turn == TAIL - 1)
    def _():
        chosen[:, :R] = dot(pre_low[...], step_weight[...], 1, 1).astype(jnp.bfloat16)

        @pl.loop(0, DI // WIDE)
        def _(c):
            lanes = pl.ds(pl.multiple_of(c * WIDE, WIDE), WIDE)
            total = grad_mixed[:, lanes] + dot(chosen[...], select_weight[:, lanes], 1, 0)
            grad_conv = total * slope_ref[:, lanes]
            value = conv_ref[:, lanes]
            grad_rows[CONV, :, lanes] += fold(grad_conv)
            result = vectors[CONV - 1 : CONV, lanes] * grad_conv
            grad_rows[CONV - 1, :, lanes] += fold(grad_conv * value)
            for j in range(1, CONV):
                taps[j - 1, :tall, lanes] = grad_conv * flags[:, 2 * N + j : 2 * N + j + 1]
                later = taps[j - 1, :, lanes][j : j + tall]
                grad_rows[CONV - 1 - j, :, lanes] += fold(later * value)
                result = result + vectors[CONV - 1 - j : CONV - j, lanes] * later
                taps[j - 1, tall:, lanes] = taps[j - 1, :8, lanes]
            grad_conv_in[:, lanes] = result.astype(jnp.bfloat16)

    at_steps((reduce.end,), reduce.count, ((11,) * reduce.count,))


def dot(left, right, left_dim, right_dim):
    return lax.dot_general(
        left, right, (((left_dim,), (right_dim,)), ((), ())), preferred_element_type=jnp.float32
    )


def scan_forward(v, mixed, sel, rates, plan, pieces):
    count = v.shape[0]
    anywhere = [pl.BlockSpec(memory_space=pl.ANY)] * len(pieces)
    rows = pl.BlockSpec((BLOCK, DI), lambda i: (i, 0))
    return pl.pallas_call(
        functools.partial(forward_kernel, plan, len(pieces)),
        grid=(count // BLOCK,),
        in_specs=[
            rows,
            rows,
            pl.BlockSpec((BLOCK, LANES), lambda i: (i, 0)),
            pl.BlockSpec((N, DI), lambda i: (0, 0)),
        ]
        + anywhere,
        out_specs=[rows, rows, pl.BlockSpec((BLOCK, N, COLS, LANES), lambda i: (i, 0, 0, 0))] + anywhere,
        out_shape=[
            jax.ShapeDtypeStruct((count, DI), jnp.float32),
            jax.ShapeDtypeStruct((count, DI), jnp.float32),
            jax.ShapeDtypeStruct((count, N, COLS, LANES), jnp.float32),
        ]
        + Gather.shapes(plan, pieces),
        scratch_shapes=[
            pltpu.VMEM((N, COLS, LANES), jnp.float32),
            pltpu.VMEM((N * COLS, LANES), jnp.float32),
            pltpu.VMEM((BLOCK * COLS, LANES), jnp.float32),
            pltpu.VMEM((BLOCK * COLS, LANES), jnp.float32),
            pltpu.VMEM((BLOCK // 8, 2 * N, 8, LANES), jnp.float32),
            pltpu.VMEM((BLOCK * COLS, LANES), jnp.float32),
        ]
        + Gather.scratch(plan, sum(GATHER_CUTS)),
        compiler_params=pltpu.CompilerParams(
            vmem_limit_bytes=48 << 20, collective_id=2, has_side_effects=True
        ),
        cost_estimate=pl.CostEstimate(
            flops=6 * count * N * DI, bytes_accessed=4 * count * N * DI, transcendentals=count * N * DI
        ),
        name="scan_forward",
    )(v, mixed, sel, rates, *pieces)


def scan_backward(v, dt, mixed, gs, conv_input, slope, sel, rates, vectors, step_weight, select_weight, states, plan, summed):
    count = dt.shape[0]
    blocks = count // BLOCK
    anywhere = [pl.BlockSpec(memory_space=pl.ANY)] * len(summed)
    rows = pl.BlockSpec((BLOCK, DI), lambda i: (blocks - 1 - i, 0))

    def tall(width):
        return pl.BlockSpec((BLOCK * TAIL, width), lambda i: (blocks // TAIL - 1 - i // TAIL, 0))

    def whole(*shape):
        return pl.BlockSpec(shape, lambda i: (0,) * len(shape))

    state = (N, COLS, LANES)
    return pl.pallas_call(
        functools.partial(backward_kernel, plan, len(summed)),
        grid=(blocks,),
        in_specs=[
            rows,
            rows,
            rows,
            rows,
            pl.BlockSpec((BLOCK, LANES), lambda i: (blocks - 1 - i, 0)),
            whole(N, DI),
            whole(8, DI),
            whole(R, DI),
            whole(R + 2 * N, DI),
            pl.BlockSpec((BLOCK,) + state, lambda i: (blocks - 1 - i, 0, 0, 0)),
            pl.BlockSpec((1,) + state, lambda i: (jnp.maximum((blocks - 1 - i) * BLOCK - 1, 0), 0, 0, 0)),
            tall(DI),
            tall(DI),
            tall(LANES),
        ]
        + anywhere,
        out_specs=[tall(DI), tall(DI), tall(R + 2 * N), whole(8, 8, DI), whole(*state), whole(8, LANES)]
        + anywhere,
        out_shape=[
            jax.ShapeDtypeStruct((count, DI), jnp.bfloat16),
            jax.ShapeDtypeStruct((count, DI), jnp.bfloat16),
            jax.ShapeDtypeStruct((count, R + 2 * N), jnp.bfloat16),
            jax.ShapeDtypeStruct((8, 8, DI), jnp.float32),
            jax.ShapeDtypeStruct(state, jnp.float32),
            jax.ShapeDtypeStruct((8, LANES), jnp.float32),
        ]
        + Reduce.shapes(plan, summed),
        scratch_shapes=[pltpu.VMEM(state, jnp.float32), pltpu.VMEM((N * COLS, LANES), jnp.float32)]
        + [pltpu.VMEM((BLOCK * COLS, LANES), jnp.float32)] * 3
        + [pltpu.VMEM((BLOCK // 8, 2 * N, 8, LANES), jnp.float32)]
        + [pltpu.VMEM((BLOCK * COLS, LANES), jnp.float32)] * 2
        + [pltpu.VMEM((2, 16 * BACK, LANES), jnp.float32)]
        + [pltpu.VMEM((LANES, LANES), jnp.float32)]
        + [pltpu.VMEM((BLOCK, DI), jnp.float32)] * 2
        + [pltpu.VMEM((BLOCK * TAIL, DI), jnp.float32)]
        + [pltpu.VMEM((CONV - 1, BLOCK * TAIL + 8, DI), jnp.float32)]
        + Reduce.scratch(plan, REDUCE_CUTS, summed),
        compiler_params=pltpu.CompilerParams(
            vmem_limit_bytes=60 << 20, collective_id=3, has_side_effects=True
        ),
        cost_estimate=pl.CostEstimate(
            flops=20 * count * N * DI, bytes_accessed=4 * count * N * DI, transcendentals=count * N * DI
        ),
        name="scan_backward",
    )(
        v, dt, mixed, gs, sel, rates, vectors, step_weight, select_weight,
        states, states, conv_input, slope, sel, *summed,
    )


def contract(left, right, left_dim, right_dim):
    return lax.dot_general(
        left, right, (((left_dim,), (right_dim,)), ((), ())), preferred_element_type=jnp.float32
    )


def channel_decay(rows_total):
    places = jnp.arange(rows_total, dtype=jnp.int32)[:, None]
    return ((places >= N) & (places < N + CONV)).astype(jnp.float32)


def adam_direction(weight, grad, first, second, factor, decay):
    clipped = grad * factor
    first = beta_one * first + (1.0 - beta_one) * clipped
    second = beta_two * second + (1.0 - beta_two) * clipped * clipped
    first_hat = first / (1.0 - beta_one**adam_step)
    second_hat = second / (1.0 - beta_two**adam_step)
    return first_hat / (jnp.sqrt(second_hat) + adam_eps) + decay_rate * decay * weight


def local(
    shards,
    dp,
    tokens,
    lengths,
    cotangent,
    norm_gain,
    input_weight,
    select_weight,
    step_weight,
    channel_params,
    output_weight,
    moment_gain,
    moment_input,
    moment_select,
    moment_step,
    moment_channel,
    moment_output,
    square_gain,
    square_input,
    square_select,
    square_step,
    square_channel,
    square_output,
):
    row_count = tokens.shape[0]
    live_mask, offset = block_layout(lengths[0], row_count)
    plan = (shards, dp // 2)
    low_conv = own_piece(input_weight, dp, 0, DI).astype(jnp.bfloat16)
    low_gate = own_piece(input_weight, dp, DI, DI).astype(jnp.bfloat16)
    low_output = own_piece(output_weight, dp).astype(jnp.bfloat16)
    low_small = own_piece(jnp.concatenate([select_weight, step_weight], axis=0), dp).astype(jnp.bfloat16)
    width = channel_params.shape[1]
    vectors = jnp.concatenate(
        [channel_params, jnp.pad(norm_gain, (0, width - norm_gain.shape[0]))[None, :]], axis=0
    )
    full_conv, full_small, full_vectors = gather_pieces(
        plan, [low_conv, low_small, own_piece(vectors, dp)], (4, 1, 1), "gather_weights", 0
    )
    full_conv = from_pieces(full_conv, norm_gain.shape[0], DI, dp).reshape(-1, DI)
    small_rows = R + 2 * N + R
    full_small = from_pieces(full_small, small_rows, width, dp).transpose(1, 0, 2).reshape(small_rows, DI)
    full_select, full_step = full_small[: R + 2 * N], full_small[R + 2 * N :]
    full_vectors = from_pieces(full_vectors, vectors.shape[0], width, dp)
    gain = full_vectors[:, -1, : norm_gain.shape[0]].reshape(-1)
    channel = full_vectors[:, :-1].transpose(1, 0, 2).reshape(-1, DI)
    inputs = tokens.astype(jnp.float32)
    normed_value, norm_pull = jax.vjp(rms_scale, inputs, gain)
    normed = normed_value.astype(jnp.bfloat16)
    conv_input = jnp.dot(normed, full_conv, preferred_element_type=jnp.float32)
    conv_out = causal_conv(conv_input, channel[N : N + CONV], channel[N + CONV], offset)
    sigmoid = jax.nn.sigmoid(conv_out)
    mixed, conv_slope = lax.optimization_barrier(
        ((conv_out * sigmoid).astype(jnp.bfloat16), sigmoid * (1.0 + conv_out * (1.0 - sigmoid)))
    )
    mixed_values = mixed.astype(jnp.float32)
    wide_select = jnp.concatenate([full_select[R:], jnp.zeros((R - 2 * N, DI), jnp.bfloat16), full_select[:R]], axis=0)
    selection = contract(mixed, wide_select, 1, 1)
    step_low = selection[:, LANES - R :].astype(jnp.bfloat16)
    step_in = jnp.dot(step_low, full_step, preferred_element_type=jnp.float32) + channel[N + CONV + 1][None, :]
    rates = -jnp.exp(channel[:N])
    rates_low = rates * math.log2(math.e)
    lane = lax.broadcasted_iota(jnp.int32, (row_count, LANES), 1)
    flag = jnp.where(lane == 2 * N, offset == 0, offset >= lane - 2 * N).astype(jnp.float32)
    chosen = jnp.where(lane < 2 * N, selection, jnp.where(lane < 2 * N + CONV, flag, 0.0))
    skip = channel[N + CONV + 2][None, :]
    state_out, step_size, states, full_gate, full_output = scan_forward(
        step_in, mixed, chosen, rates_low, plan, [low_gate, low_output]
    )
    full_gate = from_pieces(full_gate, norm_gain.shape[0], DI, dp).reshape(-1, DI)
    full_output = from_pieces(full_output, output_weight.shape[0], output_weight.shape[1], dp).reshape(DI, -1)
    gate_half = jnp.dot(normed, full_gate, preferred_element_type=jnp.float32)
    scanned = state_out + skip * mixed_values
    gate_value, gate_pull = jax.vjp(jax.nn.silu, gate_half)
    gated = (scanned * gate_value).astype(jnp.bfloat16)
    branch = jnp.dot(gated, full_output, preferred_element_type=jnp.float32)
    layer_output = (inputs + live_mask * branch).astype(jnp.bfloat16)
    upstream = cotangent.astype(jnp.float32)
    grad_branch = (upstream * live_mask).astype(jnp.bfloat16)
    grad_output = contract(gated, grad_branch, 0, 0).astype(jnp.bfloat16)
    grad_gated = contract(grad_branch, full_output, 1, 1)
    grad_scanned = grad_gated * gate_value
    (grad_gate,) = gate_pull(grad_gated * scanned)
    grad_gate = grad_gate.astype(jnp.bfloat16)
    grad_gate_weight = contract(normed, grad_gate, 0, 0).astype(jnp.bfloat16)
    heights = [norm_gain.shape[0], output_weight.shape[0]]
    grad_conv_input, grad_pre_low, grad_selection, grad_rows, sums, squares, sum_output, sum_gate = scan_backward(
        step_in,
        step_size,
        mixed,
        grad_scanned,
        conv_input,
        conv_slope,
        chosen,
        rates_low,
        jnp.pad(channel[N:], ((0, 1), (0, 0))),
        full_step,
        full_select,
        states,
        plan,
        [
            to_pieces(shards, grad_output.reshape(shards, heights[1], -1), dp),
            to_pieces(shards, grad_gate_weight.reshape(shards, heights[0], -1), dp),
        ],
    )
    grad_step = contract(step_low, grad_pre_low, 0, 0)
    grad_select = contract(grad_selection, mixed, 0, 0)
    grad_conv_weight = contract(normed, grad_conv_input, 0, 0).astype(jnp.bfloat16)
    grad_normed = contract(grad_conv_input, full_conv, 1, 1) + contract(grad_gate, full_gate, 1, 1)
    grad_inputs, grad_gain = norm_pull(grad_normed)
    input_grad = (upstream + grad_inputs).astype(jnp.bfloat16)
    grad_channel = jnp.concatenate(
        [rates * sums.reshape(N, DI), jnp.sum(grad_rows[: CONV + 3], axis=1)], axis=0
    )
    small = jnp.concatenate([grad_select, grad_step, grad_channel], axis=0)
    small = small.reshape(-1, shards, width).transpose(1, 0, 2)
    small_gain = jnp.pad(grad_gain.reshape(shards, 1, -1), ((0, 0), (0, 0), (0, width - grad_gain.shape[0] // shards)))
    small = jnp.concatenate([small, small_gain], axis=1).astype(jnp.bfloat16)
    sum_conv, sum_small, squares = reduce_pieces(
        plan,
        [
            to_pieces(shards, grad_conv_weight.reshape(shards, heights[0], -1), dp),
            to_pieces(shards, small, dp),
        ],
        squares,
        (4, 1),
        "sum_gradients",
        1,
    )
    sum_output, sum_gate, sum_conv, sum_small = (
        from_pieces(pieces[None], rows, columns, dp)[0].astype(jnp.float32)
        for pieces, rows, columns in (
            (sum_output, heights[1], output_weight.shape[1]),
            (sum_gate, heights[0], DI),
            (sum_conv, heights[0], DI),
            (sum_small, small.shape[1], width),
        )
    )
    sum_input = jnp.concatenate([sum_conv, sum_gate], axis=1)
    sum_select, sum_step = sum_small[: R + 2 * N], sum_small[R + 2 * N : small_rows]
    sum_channel, sum_gain = sum_small[small_rows:-1], sum_small[-1, : norm_gain.shape[0]]
    grads = (sum_gain, sum_input, sum_select, sum_step, sum_channel, sum_output)
    grad_norm = jnp.sqrt(jnp.sum(squares))
    factor = jnp.minimum(1.0, clip_norm / (grad_norm + 1e-06))
    params = (norm_gain, input_weight, select_weight, step_weight, channel_params, output_weight)
    firsts = (moment_gain, moment_input, moment_select, moment_step, moment_channel, moment_output)
    seconds = (square_gain, square_input, square_select, square_step, square_channel, square_output)
    decays = (0.0, 1.0, 1.0, 1.0, channel_decay(channel_params.shape[0]), 1.0)
    updates = [
        adam_direction(
            params[which], grads[which], firsts[which], seconds[which], factor, decays[which]
        )
        for which in range(6)
    ]
    return (
        layer_output,
        input_grad,
        grad_norm,
        updates[0],
        updates[1],
        updates[2],
        updates[3],
        updates[4],
        updates[5],
        grads[0],
        grads[1],
        grads[2],
        grads[3],
        grads[4],
        grads[5],
    )


def solution(mesh):
    in_specs = (
        P(("dp", "fsdp"), None),
        P(("dp", "fsdp"), None),
        P(("dp", "fsdp"), None),
        P("fsdp"),
        P("fsdp", None),
        P(None, "fsdp"),
        P(None, "fsdp"),
        P(None, "fsdp"),
        P("fsdp", None),
        P("fsdp"),
        P("fsdp", None),
        P(None, "fsdp"),
        P(None, "fsdp"),
        P(None, "fsdp"),
        P("fsdp", None),
        P("fsdp"),
        P("fsdp", None),
        P(None, "fsdp"),
        P(None, "fsdp"),
        P(None, "fsdp"),
        P("fsdp", None),
    )
    out_specs = (
        P(("dp", "fsdp"), None),
        P(("dp", "fsdp"), None),
        P(),
        P("fsdp"),
        P("fsdp", None),
        P(None, "fsdp"),
        P(None, "fsdp"),
        P(None, "fsdp"),
        P("fsdp", None),
        P("fsdp"),
        P("fsdp", None),
        P(None, "fsdp"),
        P(None, "fsdp"),
        P(None, "fsdp"),
        P("fsdp", None),
    )
    shards, dp = mesh.shape["fsdp"], mesh.shape["dp"]
    return jax.shard_map(functools.partial(local, shards, dp), mesh=mesh, in_specs=in_specs, out_specs=out_specs, check_vma=False)
```
